32 devices in a mesh: row: 8 (over z, y), col: 4 (over x, core).
Axes of the slice: x: 2, y: 2, z: 4, core: 2. Of those that a mesh axis runs over, the one named last changes fastest.
Arguments:
- pair_slab: bfloat16 [16, 256, 128], P('col', 'row'), may hold values from -6 to 6
- pair_full: bfloat16 [256, 256, 128], P('col', 'row'), may hold values from -6 to 6
- grad_out: bfloat16 [16, 256, 128], P('row', 'col'), may hold values from -0.59765625 to 0.59765625
- w_a_lin: bfloat16 [128, 128], replicated, may hold values from -0.5 to 0.5
- w_a_gate: bfloat16 [128, 128], replicated, may hold values from -0.5 to 0.5
- w_b_lin: bfloat16 [128, 128], replicated, may hold values from -0.5 to 0.5
- w_b_gate: bfloat16 [128, 128], replicated, may hold values from -0.5 to 0.5
- mask_slab: int32 [16], replicated, may hold values 0 or 1
- mask_residue: int32 [256], replicated, may hold values 0 or 1
Outputs:
- grad_slab: bfloat16 [16, 256, 128], P('col', 'row')
- grad_pair: bfloat16 [256, 256, 128], P('col', 'row')
- grad_weights: float32 [4, 128, 128], replicated
The draws below stay inside these ranges and needn't reach their ends.
All inputs are finite; a program needn't handle non-finite values.
Results may differ from the reference program's by a relative error of at most 0.0057.
Values may be sent and summed in bfloat16 or wider, within the bound.
No kernel may reach another device: no remote copies, remote signals or barrier semaphores. Data moves between devices by JAX's collectives and lax.ppermute only.
A program may use at most 64 MiB of HBM per device.

```python
import jax
import jax.numpy as jnp
from jax import lax

CZ = 128
CH = 128
N = 256
I = 16
N_COL = 4


def set_ends(values, stream_key, smallest, high):
    longest = values.shape.index(max(values.shape))
    spots = []
    for shift in (0, 1):
        where = [jax.random.randint(jax.random.fold_in(stream_key, axis), (), 0, length) for axis, length in enumerate(values.shape)]
        where[longest] = (where[longest] + shift) % values.shape[longest]
        spots.append(tuple(where))
    return values.at[spots[0]].set(smallest).at[spots[1]].set(high)


def levels(key, shape, shards, smallest, top_value):
    factor_of, own = 1.0, jax.random.fold_in(key, 6)
    for dim, parts in shards:
        heights = jnp.exp(jax.random.uniform(jax.random.fold_in(own, dim), (parts,), jnp.float32, smallest / len(shards), top_value / len(shards)))
        factor_of = factor_of * jnp.repeat(heights, shape[dim] // parts).reshape([-1 if axis == dim else 1 for axis in range(len(shape))])
    return factor_of


def bell_draw(own_key, dims, deviation, most, cuts=(), dtype=jnp.bfloat16):
    entries = deviation * jax.random.normal(own_key, dims, jnp.float32)
    if cuts:
        entries = entries * levels(own_key, dims, cuts, -0.22, 0.18)
    return jnp.clip(entries, -most, most).astype(dtype)


def setup_inputs(seed: int = 0) -> dict:
    streams_of = jax.random.split(jax.random.key(seed), 10)
    return {
        "pair_slab": bell_draw(streams_of[0], (I, N, CZ), 1.0, 6.0, ((0, 4), (1, 8))),
        "pair_full": bell_draw(streams_of[1], (N, N, CZ), 1.0, 6.0, ((0, 4), (1, 8))),
        "grad_out": bell_draw(streams_of[2], (I, N, CH), 0.1, 0.59765625, ((0, 8), (1, 4))),
        "w_a_lin": bell_draw(streams_of[3], (CZ, CH), CZ ** -0.5, 0.5),
        "w_a_gate": bell_draw(streams_of[4], (CZ, CH), CZ ** -0.5, 0.5),
        "w_b_lin": bell_draw(streams_of[5], (CZ, CH), CZ ** -0.5, 0.5),
        "w_b_gate": bell_draw(streams_of[6], (CZ, CH), CZ ** -0.5, 0.5),
        "mask_slab": set_ends((jax.random.randint(streams_of[7], (I,), 0, 8) < 7).astype(jnp.int32), jax.random.fold_in(streams_of[7], 1), 0, 1),
        "mask_residue": set_ends((jax.random.randint(streams_of[8], (N,), 0, 8) < 7).astype(jnp.int32), jax.random.fold_in(streams_of[8], 1), 0, 1),
    }


def narrow(values):
    return lax.optimization_barrier(values.astype(jnp.bfloat16)).astype(jnp.float32)


def project(pair, weight):
    return jnp.einsum('rkd,dc->rkc', pair.astype(jnp.float32), weight.astype(jnp.float32))


def forward_gate(pair, w_linear, w_gate, mask):
    linear = project(pair, w_linear)
    sigmoid = jax.nn.sigmoid(project(pair, w_gate))
    value = narrow(mask * sigmoid * linear)
    return linear, sigmoid, value


def gate_back(grad, mask, linear, sigmoid):
    d_linear = narrow(grad * mask * sigmoid)
    d_gate = narrow(grad * mask * linear * sigmoid * (1.0 - sigmoid))
    return d_linear, d_gate


def input_grads(pair, d_linear, d_gate, w_linear, w_gate):
    pair_wide = pair.astype(jnp.float32)
    input_grad = jnp.einsum('rkc,dc->rkd', d_linear, w_linear.astype(jnp.float32))
    input_grad = input_grad + jnp.einsum('rkc,dc->rkd', d_gate, w_gate.astype(jnp.float32))
    weight_linear = jnp.einsum('rkd,rkc->dc', pair_wide, d_linear)
    weight_gate = jnp.einsum('rkd,rkc->dc', pair_wide, d_gate)
    return input_grad.astype(jnp.bfloat16), weight_linear, weight_gate


def reference(pair_slab, pair_full, grad_out, w_a_lin, w_a_gate, w_b_lin, w_b_gate, mask_slab, mask_residue):
    slab_flags = mask_slab.astype(jnp.float32)
    res_flags = mask_residue.astype(jnp.float32)
    slab_mask = (slab_flags[:, None] * res_flags[None, :])[:, :, None]
    slab_linear, slab_sigmoid, slab_value = forward_gate(pair_slab, w_a_lin, w_a_gate, slab_mask)
    block_width = N // N_COL
    pair_blocks = pair_full.reshape(N_COL, block_width, N, CZ)
    grad_blocks = jnp.transpose(grad_out.reshape(I, N_COL, block_width, CH), (1, 0, 2, 3))
    flag_blocks = res_flags.reshape(N_COL, block_width)

    def visit_block(running, block_items):
        slab_sum, lin_sum, gate_sum = running
        pair_block, grad_block, flag_block = block_items
        pair_mask = (flag_block[:, None] * res_flags[None, :])[:, :, None]
        pair_linear, pair_sigmoid, pair_value = forward_gate(pair_block, w_b_lin, w_b_gate, pair_mask)
        grad_wide = grad_block.astype(jnp.float32)
        slab_sum = slab_sum + jnp.einsum('ijc,jkc->ikc', grad_wide, pair_value)
        pair_grad = jnp.einsum('ijc,ikc->jkc', grad_wide, slab_value)
        d_linear, d_gate = gate_back(pair_grad, pair_mask, pair_linear, pair_sigmoid)
        block_out, weight_linear, weight_gate = input_grads(pair_block, d_linear, d_gate, w_b_lin, w_b_gate)
        return (slab_sum, lin_sum + weight_linear, gate_sum + weight_gate), block_out

    start = (jnp.zeros((I, N, CH), jnp.float32), jnp.zeros((CZ, CH), jnp.float32), jnp.zeros((CZ, CH), jnp.float32))
    (slab_grad, pair_lin_w, pair_gate_w), pair_out = lax.scan(visit_block, start, (pair_blocks, grad_blocks, flag_blocks))
    grad_pair = pair_out.reshape(N, N, CZ)
    d_linear, d_gate = gate_back(slab_grad, slab_mask, slab_linear, slab_sigmoid)
    grad_slab, slab_lin_w, slab_gate_w = input_grads(pair_slab, d_linear, d_gate, w_a_lin, w_a_gate)
    grad_weights = jnp.stack([slab_lin_w, slab_gate_w, pair_lin_w, pair_gate_w]) / N
    return grad_slab, grad_pair, grad_weights
```

```python
import functools

import jax
import jax.numpy as jnp
from jax import lax
from jax.experimental import pallas as pl
from jax.experimental.pallas import tpu as pltpu
from jax.sharding import PartitionSpec as P

F32 = jnp.float32
BF16 = jnp.bfloat16
VMEM = pl.BlockSpec(memory_space=pltpu.VMEM)
SMEM = pl.BlockSpec(memory_space=pltpu.SMEM)
J_STEP = 4
I_STEP = 16


def bits_of(size):
    return [1 << b for b in range(size.bit_length() - 1)]


def swap(value, axis, bit):
    size = lax.axis_size(axis)
    return lax.ppermute(value, axis, [(d, d ^ bit) for d in range(size)])


def params(mib=32):
    return pltpu.CompilerParams(vmem_limit_bytes=mib * 1024 * 1024)


def cost(flops, bytes_accessed, transcendentals=0):
    return pl.CostEstimate(
        flops=flops, bytes_accessed=bytes_accessed, transcendentals=transcendentals
    )


def key_mask(flags_row, start, keys):
    residues = flags_row.shape[1]
    lane = lax.broadcasted_iota(jnp.int32, (keys, residues), 1)
    want = lax.broadcasted_iota(jnp.int32, (keys, residues), 0) + start
    picked = jnp.where(lane == want, flags_row.astype(F32), 0.0)
    return jnp.sum(picked, axis=1, keepdims=True)


def project(rows, w_lin, w_gate):
    both = jnp.dot(
        rows, jnp.concatenate([w_lin, w_gate], axis=1), preferred_element_type=F32
    )
    ch = w_lin.shape[1]
    linear = both[:, :ch]
    sigmoid = 1.0 / (1.0 + jnp.exp(-both[:, ch:]))
    return linear, sigmoid


def pair_forward_kernel(
    pair_ref, w_lin_ref, w_gate_ref, flags_ref, flags_row_ref, value_ref, lin_ref, gate_ref
):
    cols, keys, cz = pair_ref.shape
    ch = w_lin_ref.shape[1]
    row, col = lax.axis_index("row"), lax.axis_index("col")
    km = jnp.broadcast_to(key_mask(flags_row_ref[...], row * keys, keys), (keys, ch))
    step = 8

    def body(s, carry):
        j0 = pl.multiple_of(s * step, step)
        rows = pair_ref[pl.ds(j0, step)].reshape(step * keys, cz)
        linear, sigmoid = project(rows, w_lin_ref[...], w_gate_ref[...])
        linear = linear.reshape(step, keys, ch)
        sigmoid = sigmoid.reshape(step, keys, ch)
        for j in range(step):
            m = km * flags_ref[col * cols + j0 + j].astype(F32)
            masked = m * sigmoid[j]
            lin = linear[j]
            value_ref[j0 + j] = (masked * lin).astype(BF16).astype(F32)
            lin_ref[j0 + j] = masked
            gate_ref[j0 + j] = masked * lin * (1.0 - sigmoid[j])
        return carry

    lax.fori_loop(0, cols // step, body, 0)


def pair_forward(pair, w_lin, w_gate, flags):
    cols, keys, cz = pair.shape
    ch = w_lin.shape[1]
    out = jax.ShapeDtypeStruct((cols, keys, ch), F32)
    return pl.pallas_call(
        pair_forward_kernel,
        out_shape=(out, out, out),
        in_specs=[VMEM, VMEM, VMEM, SMEM, VMEM],
        out_specs=(VMEM, VMEM, VMEM),
        compiler_params=params(),
        cost_estimate=cost(4 * cols * keys * cz * ch, 14 * cols * keys * ch, cols * keys * ch),
        name="pair_forward",
    )(pair, w_lin, w_gate, flags, flags[None, :])


def slab_forward_kernel(n_blocks, *refs):
    blocks = refs[:n_blocks]
    (w_lin_ref, w_gate_ref, slab_flags_ref, flags_row_ref) = refs[n_blocks : n_blocks + 4]
    slab_ref, value_ref, lin_ref, gate_ref = refs[n_blocks + 4 :]
    rows, keys, cz = blocks[0].shape
    ch = w_lin_ref.shape[1]
    row, col = lax.axis_index("row"), lax.axis_index("col")
    km = jnp.broadcast_to(key_mask(flags_row_ref[...], row * keys, keys), (keys, ch))
    for b in range(n_blocks):
        first = (col ^ b) * rows
        block = blocks[b][...]
        linear, sigmoid = project(
            block.reshape(rows * keys, cz), w_lin_ref[...], w_gate_ref[...]
        )
        linear = linear.reshape(rows, keys, ch)
        sigmoid = sigmoid.reshape(rows, keys, ch)
        for r in range(rows):
            i = first + r
            m = km * slab_flags_ref[i].astype(F32)
            masked = m * sigmoid[r]
            slab_ref[i] = block[r]
            value_ref[i] = (masked * linear[r]).astype(BF16).astype(F32)
            lin_ref[i] = masked
            gate_ref[i] = masked * linear[r] * (1.0 - sigmoid[r])


def slab_forward(blocks, w_lin, w_gate, slab_flags, flags):
    rows, keys, cz = blocks[0].shape
    n = len(blocks)
    ch = w_lin.shape[1]
    out = jax.ShapeDtypeStruct((n * rows, keys, ch), F32)
    raw = jax.ShapeDtypeStruct((n * rows, keys, cz), BF16)
    return pl.pallas_call(
        functools.partial(slab_forward_kernel, n),
        out_shape=(raw, out, out, out),
        in_specs=[VMEM] * n + [VMEM, VMEM, SMEM, VMEM],
        out_specs=(VMEM,) * 4,
        compiler_params=params(),
        cost_estimate=cost(4 * n * rows * keys * cz * ch, 16 * n * rows * keys * ch),
        name="slab_forward",
    )(*blocks, w_lin, w_gate, slab_flags, flags[None, :])


def main_kernel(
    order,
    grad_ref,
    pair_ref,
    value_ref,
    lin_ref,
    gate_ref,
    slab_ref,
    slab_value_ref,
    slab_lin_ref,
    slab_gate_ref,
    d_lin_ref,
    d_gate_ref,
    sum_keep_ref,
    sum_send_ref,
    w_keep_ref,
    w_send_ref,
    grad_wide,
    slab_sum,
):
    cols, keys, cz = pair_ref.shape
    ch = value_ref.shape[2]
    slab_rows = slab_ref.shape[0]
    per = slab_rows // len(order)
    row, col = lax.axis_index("row"), lax.axis_index("col")
    for p in range(slab_rows):
        i = (row ^ order[p // per]) * per + p % per
        grad_wide[i] = grad_ref[p].astype(F32)
    slab_sum[...] = jnp.zeros_like(slab_sum)

    def step(s, carry):
        j0 = pl.multiple_of(s * J_STEP, J_STEP)
        values = [value_ref[j0 + j] for j in range(J_STEP)]

        def rows_of(t, totals):
            totals = list(totals)
            for u in range(I_STEP):
                i = t * I_STEP + u
                mine = slab_value_ref[i]
                total = slab_sum[i]
                for j in range(J_STEP):
                    g = jnp.broadcast_to(grad_wide[i, pl.ds(j0 + j, 1), :], (keys, ch))
                    totals[j] = totals[j] + g * mine
                    total = total + g * values[j]
                slab_sum[i] = total
            return tuple(totals)

        totals = tuple(jnp.zeros((keys, ch), F32) for _ in range(J_STEP))
        if slab_rows == I_STEP:
            totals = rows_of(0, totals)
        else:
            totals = lax.fori_loop(0, slab_rows // I_STEP, rows_of, totals)
        for j in range(J_STEP):
            d_lin_ref[j0 + j] = (totals[j] * lin_ref[j0 + j]).astype(BF16)
            d_gate_ref[j0 + j] = (totals[j] * gate_ref[j0 + j]).astype(BF16)
        return carry

    lax.fori_loop(0, cols // J_STEP, step, 0)

    def weights(rows, d_lin, d_gate):
        both = jnp.concatenate([d_lin, d_gate], axis=1)
        return lax.dot_general(
            rows, both, (((0,), (0,)), ((), ())), preferred_element_type=F32
        )

    sums = slab_sum[...]
    s_lin = (sums * slab_lin_ref[...]).astype(BF16).reshape(slab_rows * keys, ch)
    s_gate = (sums * slab_gate_ref[...]).astype(BF16).reshape(slab_rows * keys, ch)
    slab_w = weights(slab_ref[...].reshape(slab_rows * keys, cz), s_lin, s_gate)
    pair_w = weights(
        pair_ref[...].reshape(cols * keys, cz),
        d_lin_ref[...].reshape(cols * keys, ch),
        d_gate_ref[...].reshape(cols * keys, ch),
    )
    first = col % 2 == 0
    keep = jnp.where(first, slab_w, pair_w)
    send = jnp.where(first, pair_w, slab_w)
    for h in range(2):
        w_keep_ref[h] = keep[:, h * ch : (h + 1) * ch]
        w_send_ref[h] = send[:, h * ch : (h + 1) * ch]
    halves, own = sum_keep_ref.shape[:2]
    for b in range(halves):
        sum_keep_ref[b] = slab_sum[pl.ds((col ^ (2 * b)) * own, own)]
        sum_send_ref[b] = slab_sum[pl.ds((col ^ (2 * b + 1)) * own, own)]


def main_part(order, n_col, grads, pair, value, lin, gate, slab, s_value, s_lin, s_gate):
    cols, keys, cz = pair.shape
    ch = value.shape[2]
    slab_rows = slab.shape[0]
    own = slab_rows // n_col
    d_type = jax.ShapeDtypeStruct((cols, keys, ch), BF16)
    s_type = jax.ShapeDtypeStruct((n_col // 2, own, keys, ch), F32)
    w_type = jax.ShapeDtypeStruct((2, cz, ch), F32)
    return pl.pallas_call(
        functools.partial(main_kernel, order),
        out_shape=(d_type, d_type, s_type, s_type, w_type, w_type),
        in_specs=[VMEM] * 9,
        out_specs=(VMEM,) * 6,
        scratch_shapes=[
            pltpu.VMEM((slab_rows, cols, ch), F32),
            pltpu.VMEM((slab_rows, keys, ch), F32),
        ],
        compiler_params=params(),
        cost_estimate=cost(8 * cols * keys * cz * ch, 16 * cols * keys * ch),
        name="pair_and_slab_sums",
    )(grads, pair, value, lin, gate, slab, s_value, s_lin, s_gate)


def pair_out_kernel(d_lin_ref, d_gate_ref, w_lin_ref, w_gate_ref, out_ref):
    rows, ch = d_lin_ref.shape
    weights = jnp.concatenate([w_lin_ref[...], w_gate_ref[...]], axis=1)
    step = 256

    def body(s, carry):
        at = pl.ds(pl.multiple_of(s * step, step), step)
        both = jnp.concatenate([d_lin_ref[at, :], d_gate_ref[at, :]], axis=1)
        out = lax.dot_general(
            both, weights, (((1,), (1,)), ((), ())), preferred_element_type=F32
        )
        out_ref[at, :] = out.astype(BF16)
        return carry

    lax.fori_loop(0, rows // step, body, 0)


def pair_out(d_lin, d_gate, w_lin, w_gate):
    cols, keys, ch = d_lin.shape
    cz = w_lin.shape[0]
    out = pl.pallas_call(
        pair_out_kernel,
        out_shape=jax.ShapeDtypeStruct((cols * keys, cz), BF16),
        in_specs=[VMEM] * 4,
        out_specs=VMEM,
        compiler_params=params(),
        cost_estimate=cost(4 * cols * keys * cz * ch, 6 * cols * keys * ch),
        name="pair_input_grad",
    )(d_lin.reshape(cols * keys, ch), d_gate.reshape(cols * keys, ch), w_lin, w_gate)
    return out.reshape(cols, keys, cz)


def slab_out_kernel(sum_ref, got_ref, lin_ref, gate_ref, w_lin_ref, w_gate_ref, out_ref):
    own, keys, ch = sum_ref.shape
    col = lax.axis_index("col")
    at = pl.ds(col * own, own)
    total = sum_ref[...] + got_ref[...].astype(F32)
    d_lin = (total * lin_ref[at]).astype(BF16).reshape(own * keys, ch)
    d_gate = (total * gate_ref[at]).astype(BF16).reshape(own * keys, ch)
    both = jnp.concatenate([d_lin, d_gate], axis=1)
    weights = jnp.concatenate([w_lin_ref[...], w_gate_ref[...]], axis=1)
    out = lax.dot_general(both, weights, (((1,), (1,)), ((), ())), preferred_element_type=F32)
    out_ref[...] = out.astype(BF16).reshape(own, keys, w_lin_ref.shape[0])


def slab_out(total, got, lin, gate, w_lin, w_gate):
    own, keys, ch = total.shape
    cz = w_lin.shape[0]
    return pl.pallas_call(
        slab_out_kernel,
        out_shape=jax.ShapeDtypeStruct((own, keys, cz), BF16),
        in_specs=[VMEM] * 6,
        out_specs=VMEM,
        compiler_params=params(),
        cost_estimate=cost(4 * own * keys * cz * ch, 16 * own * keys * ch),
        name="slab_input_grad",
    )(total, got, lin, gate, w_lin, w_gate)


def on_device(
    pair_slab, pair_full, grad_out, w_a_lin, w_a_gate, w_b_lin, w_b_gate, mask_slab, mask_residue
):
    n_row, n_col = lax.axis_size("row"), lax.axis_size("col")
    row_bits, col_bits = bits_of(n_row), bits_of(n_col)
    residues = mask_residue.shape[0]

    blocks = {0: pair_slab}
    for bit in reversed(col_bits):
        for b in list(blocks):
            blocks[b ^ bit] = swap(blocks[b], "col", bit)
    blocks = [blocks[b] for b in range(n_col)]
    grads, order = grad_out, [0]
    for bit in row_bits[1:] + row_bits[:1]:
        grads = jnp.concatenate([grads, swap(grads, "row", bit)], axis=0)
        order = order + [n ^ bit for n in order]

    value, lin, gate = pair_forward(pair_full, w_b_lin, w_b_gate, mask_residue)
    slab, s_value, s_lin, s_gate = slab_forward(
        blocks, w_a_lin, w_a_gate, mask_slab, mask_residue
    )
    d_lin, d_gate, sum_keep, sum_send, w_keep, w_send = main_part(
        order, n_col, grads, pair_full, value, lin, gate, slab, s_value, s_lin, s_gate
    )
    weights = w_keep + swap(w_send, "col", 1)
    sums = sum_keep + swap(sum_send, "col", 1)
    for bit in col_bits[1:]:
        narrow = weights.astype(BF16)
        weights = narrow.astype(F32) + swap(narrow, "col", bit).astype(F32)
    for bit in row_bits:
        narrow = weights.astype(BF16)
        weights = narrow.astype(F32) + swap(narrow, "row", bit).astype(F32)
    for bit in reversed(col_bits[2:]):
        half = sums.shape[0] // 2
        sums = sums[:half] + swap(sums[half:].astype(BF16), "col", bit).astype(F32)
    got = swap(sums[1].astype(BF16), "col", 2)
    grad_slab = slab_out(sums[0], got, s_lin, s_gate, w_a_lin, w_a_gate)
    grad_pair = pair_out(d_lin, d_gate, w_b_lin, w_b_gate)
    weights = weights / residues
    other = swap(weights, "col", 1)
    first = lax.axis_index("col") % 2 == 0
    grad_weights = jnp.where(
        first,
        jnp.concatenate([weights, other], axis=0),
        jnp.concatenate([other, weights], axis=0),
    )
    return (grad_slab, grad_pair, grad_weights)


def solution(mesh):
    return jax.shard_map(
        on_device,
        mesh=mesh,
        in_specs=(
            P("col", "row", None),
            P("col", "row", None),
            P("row", "col", None),
            P(),
            P(),
            P(),
            P(),
            P(),
            P(),
        ),
        out_specs=(P("col", "row", None), P("col", "row", None), P()),
        check_vma=False,
    )
```

```python
import functools

import jax
import jax.numpy as jnp
from jax import lax
from jax.experimental import pallas as pl
from jax.experimental.pallas import tpu as pltpu
from jax.sharding import PartitionSpec as P

F32 = jnp.float32
BF16 = jnp.bfloat16
VMEM = pl.BlockSpec(memory_space=pltpu.VMEM)
WHOLE = pl.BlockSpec()
SMEM = pl.BlockSpec(memory_space=pltpu.SMEM)
J_STEP = 4
STAGE_COST = 400000


def bits_of(size):
    return [1 << b for b in range(size.bit_length() - 1)]


def swap(value, axis, bit):
    size = lax.axis_size(axis)
    return lax.ppermute(value, axis, [(d, d ^ bit) for d in range(size)])


def params(mib=32):
    return pltpu.CompilerParams(vmem_limit_bytes=mib * 1024 * 1024)


def cost(flops, bytes_accessed, transcendentals=0):
    return pl.CostEstimate(
        flops=flops, bytes_accessed=bytes_accessed, transcendentals=transcendentals
    )


def project(rows, w_lin, w_gate):
    both = jnp.dot(
        rows, jnp.concatenate([w_lin, w_gate], axis=1), preferred_element_type=F32
    )
    ch = w_lin.shape[1]
    linear = both[:, :ch]
    sigmoid = 1.0 / (1.0 + jnp.exp(-both[:, ch:]))
    return linear, sigmoid


def stage_kernel(n, *refs):
    for source_ref, copy_ref in zip(refs[:n], refs[n:]):
        copy_ref[...] = source_ref[...]


def stage(*sources):
    n = len(sources)
    return pl.pallas_call(
        functools.partial(stage_kernel, n),
        out_shape=tuple(jax.ShapeDtypeStruct(s.shape, s.dtype) for s in sources),
        in_specs=[VMEM] * n,
        out_specs=(VMEM,) * n,
        compiler_params=params(),
        cost_estimate=cost(STAGE_COST * sources[0].size, 4 * sources[0].size),
        name="stage",
    )(*sources)


def pair_forward_kernel(pair_ref, w_lin_ref, w_gate_ref, flags_ref, value_ref, lin_ref, gate_ref):
    cols, keys, cz = pair_ref.shape
    row, col = lax.axis_index("row"), lax.axis_index("col")
    km = flags_ref[pl.ds(pl.multiple_of(row * keys, 16), keys)].astype(F32)
    step = 8

    def body(s, carry):
        j0 = pl.multiple_of(s * step, step)
        rows = pair_ref[pl.ds(j0, step)].reshape(step * keys, cz)
        linear, sigmoid = project(rows, w_lin_ref[...], w_gate_ref[...])
        linear = linear.reshape(step, keys, -1)
        sigmoid = sigmoid.reshape(step, keys, -1)
        flags = flags_ref[pl.ds(pl.multiple_of(col * cols + j0, step), step)].astype(F32)
        for j in range(step):
            m = km * flags[j : j + 1]
            masked = m * sigmoid[j]
            lin = linear[j]
            value_ref[j0 + j] = (masked * lin).astype(BF16).astype(F32)
            lin_ref[j0 + j] = masked
            gate_ref[j0 + j] = masked * lin * (1.0 - sigmoid[j])
        return carry

    lax.fori_loop(0, cols // step, body, 0)


def pair_forward(pair, w_lin, w_gate, flags):
    cols, keys, cz = pair.shape
    ch = w_lin.shape[1]
    out = jax.ShapeDtypeStruct((cols, keys, ch), F32)
    return pl.pallas_call(
        pair_forward_kernel,
        out_shape=(out, out, out),
        in_specs=[VMEM] * 4,
        out_specs=(VMEM, VMEM, VMEM),
        compiler_params=params(),
        cost_estimate=cost(4 * cols * keys * cz * ch, 14 * cols * keys * ch, cols * keys * ch),
        name="pair_forward",
    )(pair, w_lin, w_gate, flags)


def slab_forward_kernel(
    n_blocks,
    even_ref,
    odd_ref,
    w_lin_ref,
    w_gate_ref,
    slab_flags_ref,
    flags_ref,
    slab_ref,
    value_ref,
    lin_ref,
    gate_ref,
):
    _, keys, cz = even_ref.shape
    rows = 2 * even_ref.shape[0] // n_blocks
    row, col = lax.axis_index("row"), lax.axis_index("col")
    km = flags_ref[pl.ds(pl.multiple_of(row * keys, 16), keys)].astype(F32)
    flags = slab_flags_ref[...].astype(F32)
    for i in range(n_blocks * rows):
        value_ref[i] = km * flags[i : i + 1]
    for b in range(n_blocks):
        first = (col ^ b) * rows
        block = (odd_ref if b % 2 else even_ref)[(b // 2) * rows : (b // 2 + 1) * rows]
        linear, sigmoid = project(
            block.reshape(rows * keys, cz),
            w_lin_ref[...],
            w_gate_ref[...],
        )
        linear = linear.reshape(rows, keys, -1)
        sigmoid = sigmoid.reshape(rows, keys, -1)
        for r in range(rows):
            i = first + r
            masked = value_ref[i] * sigmoid[r]
            slab_ref[i] = block[r]
            value_ref[i] = (masked * linear[r]).astype(BF16).astype(F32)
            lin_ref[i] = masked
            gate_ref[i] = masked * linear[r] * (1.0 - sigmoid[r])


def slab_forward(blocks, n, w_lin, w_gate, slab_flags, flags):
    half, keys, cz = blocks[0].shape
    rows = 2 * half // n
    ch = w_lin.shape[1]
    out = jax.ShapeDtypeStruct((n * rows, keys, ch), F32)
    raw = jax.ShapeDtypeStruct((n * rows, keys, cz), BF16)
    return pl.pallas_call(
        functools.partial(slab_forward_kernel, n),
        out_shape=(raw, out, out, out),
        in_specs=[VMEM] * 6,
        out_specs=(VMEM,) * 4,
        compiler_params=params(),
        cost_estimate=cost(4 * n * rows * keys * cz * ch, 16 * n * rows * keys * ch),
        name="slab_forward",
    )(*blocks, w_lin, w_gate, slab_flags, flags)


def row_of(order, per, p):
    return (lax.axis_index("row") ^ order[p // per]) * per + p % per


def add_rows(cols, keys, grad_ref, rows, value_ref, slab_value_ref, sums_ref, start, finish):
    ch = value_ref.shape[2]

    def step(s, carry):
        j0 = pl.multiple_of(s * J_STEP, J_STEP)
        values = [value_ref[j0 + j] for j in range(J_STEP)]
        totals = [start(j0 + j) for j in range(J_STEP)]
        for p, i in enumerate(rows):
            mine = slab_value_ref[i]
            total = sums_ref[p]
            for j in range(J_STEP):
                g = jnp.broadcast_to(grad_ref[p, pl.ds(j0 + j, 1), :], (keys, ch))
                totals[j] = totals[j] + g * mine
                total = total + g * values[j]
            sums_ref[p] = total
        for j in range(J_STEP):
            finish(j0 + j, totals[j])
        return carry

    lax.fori_loop(0, cols // J_STEP, step, 0)


def first_kernel(order, n_grads, *refs):
    grads, (value_ref, slab_value_ref, total_ref, sums_ref, wide) = refs[:n_grads], refs[n_grads:]
    cols, keys, ch = value_ref.shape
    per = grads[0].shape[0] * n_grads // len(order)
    at = 0
    for grad_ref in grads:
        wide[at : at + grad_ref.shape[0]] = grad_ref[...].astype(F32)
        at += grad_ref.shape[0]
    sums_ref[...] = jnp.zeros_like(sums_ref)
    rows = [row_of(order, per, p) for p in range(at)]

    def start(j):
        return jnp.zeros((keys, ch), F32)

    def finish(j, total):
        total_ref[j] = total

    add_rows(cols, keys, wide, rows, value_ref, slab_value_ref, sums_ref, start, finish)


def first_part(order, grads, value, slab_value):
    cols, keys, ch = value.shape
    rows = sum(g.shape[0] for g in grads)
    return pl.pallas_call(
        functools.partial(first_kernel, order, len(grads)),
        out_shape=(
            jax.ShapeDtypeStruct((cols, keys, ch), F32),
            jax.ShapeDtypeStruct((rows, keys, ch), F32),
        ),
        in_specs=[VMEM] * (len(grads) + 2),
        out_specs=(VMEM, VMEM),
        scratch_shapes=[pltpu.VMEM((rows, cols, ch), F32)],
        compiler_params=params(),
        cost_estimate=cost(4 * rows * cols * keys * ch, 8 * cols * keys * ch),
        name="first_rows",
    )(*grads, value, slab_value)


def main_kernel(order, n_grads, *refs):
    grads = refs[:n_grads]
    (
        total_ref,
        first_sums_ref,
        pair_ref,
        value_ref,
        lin_ref,
        gate_ref,
        slab_ref,
        slab_value_ref,
        slab_lin_ref,
        slab_gate_ref,
        d_lin_ref,
        d_gate_ref,
        sum_keep_ref,
        sum_send_ref,
        w_keep_ref,
        w_send_ref,
        wide,
        sums_ref,
        slab_sum,
    ) = refs[n_grads:]
    cols, keys, cz = pair_ref.shape
    ch = value_ref.shape[2]
    slab_rows = slab_ref.shape[0]
    done = first_sums_ref.shape[0]
    per = slab_rows // len(order)
    col = lax.axis_index("col")
    at = 0
    for grad_ref in grads:
        wide[at : at + grad_ref.shape[0]] = grad_ref[...].astype(F32)
        at += grad_ref.shape[0]
    sums_ref[...] = jnp.zeros_like(sums_ref)
    rows = [row_of(order, per, done + p) for p in range(at)]

    def start(j):
        return total_ref[j]

    def finish(j, total):
        d_lin_ref[j] = (total * lin_ref[j]).astype(BF16)
        d_gate_ref[j] = (total * gate_ref[j]).astype(BF16)

    add_rows(cols, keys, wide, rows, value_ref, slab_value_ref, sums_ref, start, finish)
    for p in range(done):
        slab_sum[row_of(order, per, p)] = first_sums_ref[p]
    for p in range(at):
        slab_sum[rows[p]] = sums_ref[p]

    def weights(rows, d_lin, d_gate):
        both = jnp.concatenate([d_lin, d_gate], axis=1)
        return lax.dot_general(
            rows, both, (((0,), (0,)), ((), ())), preferred_element_type=F32
        )

    sums = slab_sum[...]
    s_lin = (sums * slab_lin_ref[...]).astype(BF16).reshape(slab_rows * keys, ch)
    s_gate = (sums * slab_gate_ref[...]).astype(BF16).reshape(slab_rows * keys, ch)
    slab_w = weights(slab_ref[...].reshape(slab_rows * keys, cz), s_lin, s_gate)
    pair_w = weights(
        pair_ref[...].reshape(cols * keys, cz),
        d_lin_ref[...].reshape(cols * keys, ch),
        d_gate_ref[...].reshape(cols * keys, ch),
    )
    first = col % 2 == 0
    keep = jnp.where(first, slab_w, pair_w)
    send = jnp.where(first, pair_w, slab_w)
    for h in range(2):
        w_keep_ref[h] = keep[:, h * ch : (h + 1) * ch]
        w_send_ref[h] = send[:, h * ch : (h + 1) * ch]
    halves, own = sum_keep_ref.shape[:2]
    for b in range(halves):
        sum_keep_ref[b] = slab_sum[pl.ds((col ^ (2 * b)) * own, own)]
        sum_send_ref[b] = slab_sum[pl.ds((col ^ (2 * b + 1)) * own, own)]


def main_part(order, n_col, grads, first, pair, value, lin, gate, slab, s_value, s_lin, s_gate):
    cols, keys, cz = pair.shape
    ch = value.shape[2]
    slab_rows = slab.shape[0]
    rows = sum(g.shape[0] for g in grads)
    own = slab_rows // n_col
    d_type = jax.ShapeDtypeStruct((cols, keys, ch), BF16)
    s_type = jax.ShapeDtypeStruct((n_col // 2, own, keys, ch), F32)
    w_type = jax.ShapeDtypeStruct((2, cz, ch), F32)
    return pl.pallas_call(
        functools.partial(main_kernel, order, len(grads)),
        out_shape=(d_type, d_type, s_type, s_type, w_type, w_type),
        in_specs=[VMEM] * (len(grads) + 10),
        out_specs=(VMEM,) * 6,
        scratch_shapes=[
            pltpu.VMEM((rows, cols, ch), F32),
            pltpu.VMEM((rows, keys, ch), F32),
            pltpu.VMEM((slab_rows, keys, ch), F32),
        ],
        compiler_params=params(),
        cost_estimate=cost(8 * cols * keys * cz * ch, 16 * cols * keys * ch),
        name="last_rows",
    )(*grads, *first, pair, value, lin, gate, slab, s_value, s_lin, s_gate)


def pair_out_kernel(d_lin_ref, d_gate_ref, w_lin_ref, w_gate_ref, out_ref):
    rows, ch = d_lin_ref.shape
    weights = jnp.concatenate([w_lin_ref[...], w_gate_ref[...]], axis=1)
    step = 256

    def body(s, carry):
        at = pl.ds(pl.multiple_of(s * step, step), step)
        both = jnp.concatenate([d_lin_ref[at, :], d_gate_ref[at, :]], axis=1)
        out = lax.dot_general(
            both, weights, (((1,), (1,)), ((), ())), preferred_element_type=F32
        )
        out_ref[at, :] = out.astype(BF16)
        return carry

    lax.fori_loop(0, rows // step, body, 0)


def pair_out(d_lin, d_gate, w_lin, w_gate):
    cols, keys, ch = d_lin.shape
    cz = w_lin.shape[0]
    out = pl.pallas_call(
        pair_out_kernel,
        out_shape=jax.ShapeDtypeStruct((cols * keys, cz), BF16),
        in_specs=[VMEM] * 4,
        out_specs=VMEM,
        compiler_params=params(),
        cost_estimate=cost(4 * cols * keys * cz * ch, 6 * cols * keys * ch),
        name="pair_input_grad",
    )(d_lin.reshape(cols * keys, ch), d_gate.reshape(cols * keys, ch), w_lin, w_gate)
    return out.reshape(cols, keys, cz)


def slab_out_kernel(sum_ref, got_ref, lin_ref, gate_ref, w_lin_ref, w_gate_ref, out_ref):
    own, keys, ch = sum_ref.shape
    col = lax.axis_index("col")
    at = pl.ds(col * own, own)
    total = sum_ref[...] + got_ref[...].astype(F32)
    d_lin = (total * lin_ref[at]).astype(BF16).reshape(own * keys, ch)
    d_gate = (total * gate_ref[at]).astype(BF16).reshape(own * keys, ch)
    both = jnp.concatenate([d_lin, d_gate], axis=1)
    weights = jnp.concatenate([w_lin_ref[...], w_gate_ref[...]], axis=1)
    out = lax.dot_general(both, weights, (((1,), (1,)), ((), ())), preferred_element_type=F32)
    out_ref[...] = out.astype(BF16).reshape(own, keys, w_lin_ref.shape[0])


def slab_out(total, got, lin, gate, w_lin, w_gate):
    own, keys, ch = total.shape
    cz = w_lin.shape[0]
    return pl.pallas_call(
        slab_out_kernel,
        out_shape=jax.ShapeDtypeStruct((own, keys, cz), BF16),
        in_specs=[VMEM] * 6,
        out_specs=VMEM,
        compiler_params=params(),
        cost_estimate=cost(4 * own * keys * cz * ch, 16 * own * keys * ch),
        name="slab_input_grad",
    )(total, got, lin, gate, w_lin, w_gate)


def on_device(
    pair_slab, pair_full, grad_out, w_a_lin, w_a_gate, w_b_lin, w_b_gate, mask_slab, mask_residue
):
    n_row, n_col = lax.axis_size("row"), lax.axis_size("col")
    row_bits, col_bits = bits_of(n_row), bits_of(n_col)
    residues = mask_residue.shape[0]

    steps = [row_bits[-1]] + row_bits[1:-1] + row_bits[:1]
    held, own_slab = stage(grad_out, pair_slab)
    slab_flags, flags = (
        jnp.broadcast_to(m.astype(BF16)[:, None], m.shape + (w_a_lin.shape[1],))
        for m in (mask_slab, mask_residue)
    )
    order = [0]
    blocks = {0: own_slab}
    for bit in reversed(col_bits[1:]):
        for b in list(blocks):
            blocks[b ^ bit] = swap(blocks[b], "col", bit)
    got = swap(grad_out, "row", steps[0])
    tied = lax.optimization_barrier((flags, got))[0]
    value, lin, gate = pair_forward(pair_full, w_b_lin, w_b_gate, tied)
    for bit, last in zip(steps, steps[1:]):
        if last == steps[-1]:
            got, value, blocks = lax.optimization_barrier((got, value, blocks))
        held = jnp.concatenate([held, got], axis=0)
        order = order + [r ^ bit for r in order]
        got = swap(held, "row", last)
    slabs = jnp.concatenate([blocks[b] for b in sorted(blocks)], axis=0)
    slabs = [slabs, swap(slabs, "col", 1)]
    slab, s_value, s_lin, s_gate = slab_forward(
        slabs, n_col, w_a_lin, w_a_gate, slab_flags, flags
    )
    order = order + [r ^ last for r in order]
    first = first_part(order[: len(order) // 2], [held], value, s_value)
    d_lin, d_gate, sum_keep, sum_send, w_keep, w_send = main_part(
        order, n_col, [got], first, pair_full, value, lin, gate, slab, s_value, s_lin, s_gate
    )
    weights = w_keep + swap(w_send, "col", 1)
    sums = sum_keep + swap(sum_send, "col", 1)
    for bit in col_bits[1:]:
        narrow = weights.astype(BF16)
        weights = narrow.astype(F32) + swap(narrow, "col", bit).astype(F32)
    for bit in row_bits:
        narrow = weights.astype(BF16)
        weights = narrow.astype(F32) + swap(narrow, "row", bit).astype(F32)
    for bit in reversed(col_bits[2:]):
        half = sums.shape[0] // 2
        sums = sums[:half] + swap(sums[half:].astype(BF16), "col", bit).astype(F32)
    got = swap(sums[1].astype(BF16), "col", 2)
    grad_slab = slab_out(sums[0], got, s_lin, s_gate, w_a_lin, w_a_gate)
    grad_pair = pair_out(d_lin, d_gate, w_b_lin, w_b_gate)
    weights = weights / residues
    other = swap(weights, "col", 1)
    first = lax.axis_index("col") % 2 == 0
    grad_weights = jnp.where(
        first,
        jnp.concatenate([weights, other], axis=0),
        jnp.concatenate([other, weights], axis=0),
    )
    return (grad_slab, grad_pair, grad_weights)


def solution(mesh):
    return jax.shard_map(
        on_device,
        mesh=mesh,
        in_specs=(
            P("col", "row", None),
            P("col", "row", None),
            P("row", "col", None),
            P(),
            P(),
            P(),
            P(),
            P(),
            P(),
        ),
        out_specs=(P("col", "row", None), P("col", "row", None), P()),
        check_vma=False,
    )
```

```python
import functools

import jax
import jax.numpy as jnp
from jax import lax
from jax.experimental import pallas as pl
from jax.experimental.pallas import tpu as pltpu
from jax.sharding import PartitionSpec as P

F32 = jnp.float32
BF16 = jnp.bfloat16
VMEM = pl.BlockSpec(memory_space=pltpu.VMEM)
WHOLE = pl.BlockSpec()
SMEM = pl.BlockSpec(memory_space=pltpu.SMEM)
J_STEP = 4
FORWARD_STEP = 32
STAGE_COST = 400000


def bits_of(size):
    return [1 << b for b in range(size.bit_length() - 1)]


def swap(value, axis, bit):
    size = lax.axis_size(axis)
    return lax.ppermute(value, axis, [(d, d ^ bit) for d in range(size)])


def swap_chips(value, bit):
    n_row, n_col = lax.axis_size("row"), lax.axis_size("col")
    pairs = [(d, d ^ bit ^ 1) for d in range(n_row * n_col)]
    return lax.ppermute(value, ("row", "col"), pairs)


def parity():
    number = lax.axis_index("row") ^ lax.axis_index("col")
    for shift in (16, 8, 4, 2, 1):
        number = number ^ (number >> shift)
    return number & 1


def params(mib=32):
    return pltpu.CompilerParams(vmem_limit_bytes=mib * 1024 * 1024)


def cost(flops, bytes_accessed, transcendentals=0):
    return pl.CostEstimate(
        flops=flops, bytes_accessed=bytes_accessed, transcendentals=transcendentals
    )


def project(rows, w_lin, w_gate):
    both = jnp.dot(
        rows, jnp.concatenate([w_lin, w_gate], axis=1), preferred_element_type=F32
    )
    ch = w_lin.shape[1]
    linear = both[:, :ch]
    sigmoid = 1.0 / (1.0 + jnp.exp(-both[:, ch:]))
    return linear, sigmoid


def stage_kernel(n, *refs):
    for source_ref, copy_ref in zip(refs[:n], refs[n:]):
        copy_ref[...] = source_ref[...]


def stage(*sources):
    n = len(sources)
    return pl.pallas_call(
        functools.partial(stage_kernel, n),
        out_shape=tuple(jax.ShapeDtypeStruct(s.shape, s.dtype) for s in sources),
        in_specs=[VMEM] * n,
        out_specs=(VMEM,) * n,
        compiler_params=params(),
        cost_estimate=cost(STAGE_COST * sources[0].size, 4 * sources[0].size),
        name="stage",
    )(*sources)


def pair_forward_kernel(pair_ref, w_lin_ref, w_gate_ref, flags_ref, value_ref, lin_ref, gate_ref):
    cols, keys, cz = pair_ref.shape
    row, col = lax.axis_index("row"), lax.axis_index("col")
    km = flags_ref[pl.ds(pl.multiple_of(row * keys, 16), keys)].astype(F32)
    step = min(cols, FORWARD_STEP)

    def body(s, carry):
        j0 = pl.multiple_of(s * step, step)
        rows = pair_ref[pl.ds(j0, step)].reshape(step * keys, cz)
        linear, sigmoid = project(rows, w_lin_ref[...], w_gate_ref[...])
        linear = linear.reshape(step, keys, -1)
        sigmoid = sigmoid.reshape(step, keys, -1)
        flags = flags_ref[pl.ds(pl.multiple_of(col * cols + j0, step), step)].astype(F32)
        for j in range(step):
            m = km * flags[j : j + 1]
            masked = m * sigmoid[j]
            lin = linear[j]
            value_ref[j0 + j] = (masked * lin).astype(BF16)
            lin_ref[j0 + j] = masked
            gate_ref[j0 + j] = masked * lin * (1.0 - sigmoid[j])
        return carry

    lax.fori_loop(0, cols // step, body, 0)


def pair_forward(pair, w_lin, w_gate, flags):
    cols, keys, cz = pair.shape
    ch = w_lin.shape[1]
    out = jax.ShapeDtypeStruct((cols, keys, ch), F32)
    return pl.pallas_call(
        pair_forward_kernel,
        out_shape=(jax.ShapeDtypeStruct((cols, keys, ch), BF16), out, out),
        in_specs=[VMEM] * 4,
        out_specs=(VMEM, VMEM, VMEM),
        compiler_params=params(),
        cost_estimate=cost(4 * cols * keys * cz * ch, 14 * cols * keys * ch, cols * keys * ch),
        name="pair_forward",
    )(pair, w_lin, w_gate, flags)


def slab_forward_kernel(
    n_blocks,
    even_ref,
    odd_ref,
    w_lin_ref,
    w_gate_ref,
    slab_flags_ref,
    flags_ref,
    slab_ref,
    value_ref,
    lin_ref,
    gate_ref,
):
    _, keys, cz = even_ref.shape
    rows = 2 * even_ref.shape[0] // n_blocks
    row, col = lax.axis_index("row"), lax.axis_index("col")
    km = flags_ref[pl.ds(pl.multiple_of(row * keys, 16), keys)].astype(F32)
    flags = slab_flags_ref[...].astype(F32)
    for i in range(n_blocks * rows):
        value_ref[i] = km * flags[i : i + 1]
    for b in range(n_blocks):
        first = (col ^ b) * rows
        block = (odd_ref if b % 2 else even_ref)[(b // 2) * rows : (b // 2 + 1) * rows]
        linear, sigmoid = project(
            block.reshape(rows * keys, cz),
            w_lin_ref[...],
            w_gate_ref[...],
        )
        linear = linear.reshape(rows, keys, -1)
        sigmoid = sigmoid.reshape(rows, keys, -1)
        for r in range(rows):
            i = first + r
            masked = value_ref[i] * sigmoid[r]
            slab_ref[i] = block[r]
            value_ref[i] = (masked * linear[r]).astype(BF16).astype(F32)
            lin_ref[i] = masked
            gate_ref[i] = masked * linear[r] * (1.0 - sigmoid[r])


def slab_forward(blocks, n, w_lin, w_gate, slab_flags, flags):
    half, keys, cz = blocks[0].shape
    rows = 2 * half // n
    ch = w_lin.shape[1]
    out = jax.ShapeDtypeStruct((n * rows, keys, ch), F32)
    raw = jax.ShapeDtypeStruct((n * rows, keys, cz), BF16)
    return pl.pallas_call(
        functools.partial(slab_forward_kernel, n),
        out_shape=(raw, out, out, out),
        in_specs=[VMEM] * 6,
        out_specs=(VMEM,) * 4,
        compiler_params=params(),
        cost_estimate=cost(4 * n * rows * keys * cz * ch, 16 * n * rows * keys * ch),
        name="slab_forward",
    )(*blocks, w_lin, w_gate, slab_flags, flags)


def row_of(order, per, p):
    return (lax.axis_index("row") ^ order[p // per]) * per + p % per


def widen(grads, wide):
    at = 0
    for grad_ref in grads:
        wide[at : at + grad_ref.shape[0]] = grad_ref[...].astype(F32)
        at += grad_ref.shape[0]
    return at


def add_sums(wide, count, j0, keys, values, sums_ref):
    ch = wide.shape[2]
    for p in range(count):
        total = sums_ref[p]
        for j, value in enumerate(values):
            total = total + jnp.broadcast_to(wide[p, pl.ds(j0 + j, 1), :], (keys, ch)) * value
        sums_ref[p] = total


def add_totals(wide, rows, j0, slab_value_ref, totals):
    _, keys, ch = slab_value_ref.shape
    totals = list(totals)
    for p, i in enumerate(rows):
        mine = slab_value_ref[i]
        for j in range(len(totals)):
            g = jnp.broadcast_to(wide[p, pl.ds(j0 + j, 1), :], (keys, ch))
            totals[j] = totals[j] + g * mine
    return totals


def sums_kernel(n_grads, *refs):
    grads, (value_ref, sums_ref, wide) = refs[:n_grads], refs[n_grads:]
    cols, keys, ch = value_ref.shape
    count = widen(grads, wide)
    sums_ref[...] = jnp.zeros_like(sums_ref)

    def step(s, carry):
        j0 = pl.multiple_of(s * J_STEP, J_STEP)
        values = [value_ref[j0 + j].astype(F32) for j in range(J_STEP)]
        add_sums(wide, count, j0, keys, values, sums_ref)
        return carry

    lax.fori_loop(0, cols // J_STEP, step, 0, unroll=2)


def first_sums(grads, value):
    cols, keys, ch = value.shape
    rows = sum(g.shape[0] for g in grads)
    return pl.pallas_call(
        functools.partial(sums_kernel, len(grads)),
        out_shape=jax.ShapeDtypeStruct((rows, keys, ch), F32),
        in_specs=[VMEM] * (len(grads) + 1),
        out_specs=VMEM,
        scratch_shapes=[pltpu.VMEM((rows, cols, ch), F32)],
        compiler_params=params(),
        cost_estimate=cost(2 * rows * cols * keys * ch, 8 * cols * keys * ch),
        name="first_sums_over_j",
    )(*grads, value)


def totals_kernel(order, n_grads, *refs):
    grads, (slab_value_ref, total_ref, wide) = refs[:n_grads], refs[n_grads:]
    cols, keys, ch = total_ref.shape
    count = widen(grads, wide)
    per = slab_value_ref.shape[0] // len(order)
    rows = [row_of(order, per, p) for p in range(count)]

    def step(s, carry):
        j0 = pl.multiple_of(s * J_STEP, J_STEP)
        totals = [jnp.zeros((keys, ch), F32)] * J_STEP
        totals = add_totals(wide, rows, j0, slab_value_ref, totals)
        for j in range(J_STEP):
            total_ref[j0 + j] = totals[j]
        return carry

    lax.fori_loop(0, cols // J_STEP, step, 0, unroll=2)


def first_totals(order, grads, slab_value):
    _, keys, ch = slab_value.shape
    cols = grads[0].shape[1]
    rows = sum(g.shape[0] for g in grads)
    return pl.pallas_call(
        functools.partial(totals_kernel, order, len(grads)),
        out_shape=jax.ShapeDtypeStruct((cols, keys, ch), F32),
        in_specs=[VMEM] * (len(grads) + 1),
        out_specs=VMEM,
        scratch_shapes=[pltpu.VMEM((rows, cols, ch), F32)],
        compiler_params=params(),
        cost_estimate=cost(2 * rows * cols * keys * ch, 8 * cols * keys * ch),
        name="first_totals_over_i",
    )(*grads, slab_value)


def main_kernel(
    order,
    blocks,
    grad_ref,
    total_ref,
    first_sums_ref,
    pair_ref,
    value_ref,
    lin_ref,
    gate_ref,
    slab_ref,
    slab_value_ref,
    slab_lin_ref,
    slab_gate_ref,
    d_lin_ref,
    d_gate_ref,
    sum_keep_ref,
    sum_send_ref,
    w_keep_ref,
    w_send_ref,
    wide,
    sums_ref,
    slab_sum,
):
    cols, keys, cz = pair_ref.shape
    ch = value_ref.shape[2]
    slab_rows = slab_ref.shape[0]
    done = first_sums_ref.shape[0]
    per = slab_rows // len(order)
    col = lax.axis_index("col")
    count = widen([grad_ref], wide)
    sums_ref[...] = jnp.zeros_like(sums_ref)
    rows = [row_of(order, per, done + p) for p in range(count)]

    def step(s, carry):
        j0 = pl.multiple_of(s * J_STEP, J_STEP)
        values = [value_ref[j0 + j].astype(F32) for j in range(J_STEP)]
        add_sums(wide, count, j0, keys, values, sums_ref)
        totals = [total_ref[j0 + j] for j in range(J_STEP)]
        totals = add_totals(wide, rows, j0, slab_value_ref, totals)
        for j in range(J_STEP):
            d_lin_ref[j0 + j] = (totals[j] * lin_ref[j0 + j]).astype(BF16)
            d_gate_ref[j0 + j] = (totals[j] * gate_ref[j0 + j]).astype(BF16)
        return carry

    lax.fori_loop(0, cols // J_STEP, step, 0, unroll=2)
    for p in range(done):
        slab_sum[row_of(order, per, p)] = first_sums_ref[p]
    for p in range(count):
        slab_sum[rows[p]] = sums_ref[p]

    def weights(rows, d_lin, d_gate):
        both = jnp.concatenate([d_lin, d_gate], axis=1)
        return lax.dot_general(
            rows, both, (((0,), (0,)), ((), ())), preferred_element_type=F32
        )

    sums = slab_sum[...]
    s_lin = (sums * slab_lin_ref[...]).astype(BF16).reshape(slab_rows * keys, ch)
    s_gate = (sums * slab_gate_ref[...]).astype(BF16).reshape(slab_rows * keys, ch)
    slab_w = weights(slab_ref[...].reshape(slab_rows * keys, cz), s_lin, s_gate)
    pair_w = weights(
        pair_ref[...].reshape(cols * keys, cz),
        d_lin_ref[...].reshape(cols * keys, ch),
        d_gate_ref[...].reshape(cols * keys, ch),
    )
    first = parity() == 0
    keep = jnp.where(first, slab_w, pair_w)
    send = jnp.where(first, pair_w, slab_w)
    for h in range(2):
        w_keep_ref[h] = keep[:, h * ch : (h + 1) * ch]
        w_send_ref[h] = send[:, h * ch : (h + 1) * ch]
    own = sum_keep_ref.shape[1]
    for n, b in enumerate(blocks):
        sum_keep_ref[n] = slab_sum[pl.ds((col ^ b) * own, own)]
        sum_send_ref[n] = slab_sum[pl.ds((col ^ b ^ 1) * own, own)]


def main_part(order, blocks, grads, first, pair, forward, slab):
    cols, keys, cz = pair.shape
    ch = forward[0].shape[2]
    slab_rows = slab[0].shape[0]
    own = slab_rows // (2 * len(blocks))
    d_type = jax.ShapeDtypeStruct((cols, keys, ch), BF16)
    s_type = jax.ShapeDtypeStruct((len(blocks), own, keys, ch), F32)
    w_type = jax.ShapeDtypeStruct((2, cz, ch), F32)
    return pl.pallas_call(
        functools.partial(main_kernel, order, blocks),
        out_shape=(d_type, d_type, s_type, s_type, w_type, w_type),
        in_specs=[VMEM] * 11,
        out_specs=(VMEM,) * 6,
        scratch_shapes=[
            pltpu.VMEM((grads.shape[0], cols, ch), F32),
            pltpu.VMEM((grads.shape[0], keys, ch), F32),
            pltpu.VMEM((slab_rows, keys, ch), F32),
        ],
        compiler_params=params(),
        cost_estimate=cost(8 * cols * keys * cz * ch, 16 * cols * keys * ch),
        name="last_rows",
    )(grads, *first, pair, *forward, *slab)


def pair_out_kernel(d_lin_ref, d_gate_ref, w_lin_ref, w_gate_ref, out_ref):
    rows, ch = d_lin_ref.shape
    weights = jnp.concatenate([w_lin_ref[...], w_gate_ref[...]], axis=1)
    step = rows

    def body(s, carry):
        at = pl.ds(pl.multiple_of(s * step, step), step)
        both = jnp.concatenate([d_lin_ref[at, :], d_gate_ref[at, :]], axis=1)
        out = lax.dot_general(
            both, weights, (((1,), (1,)), ((), ())), preferred_element_type=F32
        )
        out_ref[at, :] = out.astype(BF16)
        return carry

    lax.fori_loop(0, rows // step, body, 0)


def pair_out(d_lin, d_gate, w_lin, w_gate):
    cols, keys, ch = d_lin.shape
    cz = w_lin.shape[0]
    out = pl.pallas_call(
        pair_out_kernel,
        out_shape=jax.ShapeDtypeStruct((cols * keys, cz), BF16),
        in_specs=[VMEM] * 4,
        out_specs=VMEM,
        compiler_params=params(),
        cost_estimate=cost(4 * cols * keys * cz * ch, 6 * cols * keys * ch),
        name="pair_input_grad",
    )(d_lin.reshape(cols * keys, ch), d_gate.reshape(cols * keys, ch), w_lin, w_gate)
    return out.reshape(cols, keys, cz)


def fold_kernel(kept_ref, got_ref, sum_ref, moved_ref):
    half = sum_ref.shape[0]
    sum_ref[...] = kept_ref[:half] + got_ref[:half].astype(F32)
    moved_ref[...] = (kept_ref[half:] + got_ref[half:].astype(F32)).astype(BF16)


def fold(kept, got):
    half = (kept.shape[0] // 2,) + kept.shape[1:]
    return pl.pallas_call(
        fold_kernel,
        out_shape=(jax.ShapeDtypeStruct(half, F32), jax.ShapeDtypeStruct(half, BF16)),
        in_specs=[VMEM, VMEM],
        out_specs=(VMEM, VMEM),
        compiler_params=params(),
        cost_estimate=cost(STAGE_COST * kept.size, 8 * kept.size),
        name="fold",
    )(kept, got)


def slab_out_kernel(sum_ref, got_ref, lin_ref, gate_ref, w_lin_ref, w_gate_ref, out_ref):
    own, keys, ch = sum_ref.shape
    col = lax.axis_index("col")
    at = pl.ds(col * own, own)
    total = sum_ref[...] + got_ref[...].astype(F32)
    d_lin = (total * lin_ref[at]).astype(BF16).reshape(own * keys, ch)
    d_gate = (total * gate_ref[at]).astype(BF16).reshape(own * keys, ch)
    both = jnp.concatenate([d_lin, d_gate], axis=1)
    weights = jnp.concatenate([w_lin_ref[...], w_gate_ref[...]], axis=1)
    out = lax.dot_general(both, weights, (((1,), (1,)), ((), ())), preferred_element_type=F32)
    out_ref[...] = out.astype(BF16).reshape(own, keys, w_lin_ref.shape[0])


def slab_out(total, got, lin, gate, w_lin, w_gate):
    own, keys, ch = total.shape
    cz = w_lin.shape[0]
    return pl.pallas_call(
        slab_out_kernel,
        out_shape=jax.ShapeDtypeStruct((own, keys, cz), BF16),
        in_specs=[VMEM] * 6,
        out_specs=VMEM,
        compiler_params=params(),
        cost_estimate=cost(4 * own * keys * cz * ch, 16 * own * keys * ch),
        name="slab_input_grad",
    )(total, got, lin, gate, w_lin, w_gate)


def on_device(
    pair_slab, pair_full, grad_out, w_a_lin, w_a_gate, w_b_lin, w_b_gate, mask_slab, mask_residue
):
    n_row, n_col = lax.axis_size("row"), lax.axis_size("col")
    row_bits, col_bits = bits_of(n_row), bits_of(n_col)
    residues = mask_residue.shape[0]

    steps = [row_bits[-1]] + row_bits[1:-1] + row_bits[:1]
    ch = w_a_lin.shape[1]
    held, own_slab = stage(grad_out, pair_slab)
    order = [0]
    blocks = {0: own_slab}
    for bit in reversed(col_bits[1:]):
        for b in list(blocks):
            blocks[b ^ bit] = swap(blocks[b], "col", bit)
    got = swap(grad_out, "row", steps[0])
    for bit, later in zip(steps, steps[1:-1]):
        held = jnp.concatenate([held, got], axis=0)
        order = order + [r ^ bit for r in order]
        got = swap(held, "row", later)
    masks = lax.optimization_barrier(((mask_slab, mask_residue), held, blocks))[0]
    slab_flags, flags = (
        jnp.broadcast_to(m.astype(BF16)[:, None], m.shape + (ch,)) for m in masks
    )
    value, lin, gate = pair_forward(pair_full, w_b_lin, w_b_gate, flags)
    got_last = swap(held, "row", steps[-1])
    got, value = lax.optimization_barrier((got, value))
    got_both = swap(got, "row", steps[-1])
    for bit in steps[-2:]:
        order = order + [r ^ bit for r in order]
    slabs = jnp.concatenate([blocks[b] for b in sorted(blocks)], axis=0)
    slabs = [slabs, swap(slabs, "col", 1)]
    slab = slab_forward(slabs, n_col, w_a_lin, w_a_gate, slab_flags, flags)
    pieces = [held, got, got_last]
    first = (first_totals(order, pieces, slab[1]), first_sums(pieces, value))
    kept = [0]
    for bit in reversed(col_bits[1:]):
        kept = kept + [b ^ bit for b in kept]
    d_lin, d_gate, sum_keep, sum_send, w_keep, w_send = main_part(
        order, kept, got_both, first, pair_full, (value, lin, gate), slab
    )
    pair_bit, col = col_bits[1], lax.axis_index("col")
    got_w = swap(w_send, "col", 1)
    sum_send, _ = lax.optimization_barrier((sum_send, got_w))
    side = w_keep + got_w
    upper = (col & pair_bit) != 0
    moved = jnp.where(upper, side[0], side[1]).astype(BF16)
    part = jnp.where(upper, side[1], side[0])
    part = part + swap_chips(moved, pair_bit).astype(F32)
    bits = col_bits[2:] + [bit * n_col for bit in row_bits]
    sums, got = sum_keep, swap(sum_send, "col", 1)
    for bit in bits:
        narrow = part.astype(BF16)
        if bit == bits[1]:
            narrow, got = lax.optimization_barrier((narrow, got))
            for far in col_bits[1:]:
                sums, moved = fold(sums, got)
                got = swap(moved, "col", far)
        if bit == bits[0]:
            narrow, d_lin, d_gate = lax.optimization_barrier((narrow, d_lin, d_gate))
            grad_pair = pair_out(d_lin, d_gate, w_b_lin, w_b_gate)
        if bit == bits[-1]:
            narrow, grad_pair = lax.optimization_barrier((narrow, grad_pair))
        part = narrow.astype(F32) + swap_chips(narrow, bit).astype(F32)
    narrow = part.astype(BF16)
    mine = jnp.stack([narrow, swap_chips(narrow, pair_bit)])
    both = [mine, swap(mine, "col", 1)]
    both = [jnp.where(upper, m[::-1], m).astype(F32) / residues for m in both]
    first = parity() == 0
    grad_weights = jnp.where(
        first, jnp.concatenate(both, axis=0), jnp.concatenate(both[::-1], axis=0)
    )
    grad_slab = slab_out(sums[0], got[0], slab[2], slab[3], w_a_lin, w_a_gate)
    return (grad_slab, grad_pair, grad_weights)


def solution(mesh):
    return jax.shard_map(
        on_device,
        mesh=mesh,
        in_specs=(
            P("col", "row", None),
            P("col", "row", None),
            P("row", "col", None),
            P(),
            P(),
            P(),
            P(),
            P(),
            P(),
        ),
        out_specs=(P("col", "row", None), P("col", "row", None), P()),
        check_vma=False,
    )
```

```python
import functools

import jax
import jax.numpy as jnp
from jax import lax
from jax.experimental import pallas as pl
from jax.experimental.pallas import tpu as pltpu
from jax.sharding import PartitionSpec as P

F32 = jnp.float32
BF16 = jnp.bfloat16
VMEM = pl.BlockSpec(memory_space=pltpu.VMEM)
WHOLE = pl.BlockSpec()
SMEM = pl.BlockSpec(memory_space=pltpu.SMEM)
J_STEP = 4
FORWARD_STEP = 32
W_STEP = 16
STAGE_COST = 400000


def bits_of(size):
    return [1 << b for b in range(size.bit_length() - 1)]


def swap(value, axis, bit):
    size = lax.axis_size(axis)
    return lax.ppermute(value, axis, [(d, d ^ bit) for d in range(size)])


def swap_chips(value, bit):
    n_row, n_col = lax.axis_size("row"), lax.axis_size("col")
    pairs = [(d, d ^ bit ^ 1) for d in range(n_row * n_col)]
    return lax.ppermute(value, ("row", "col"), pairs)


def parity():
    number = lax.axis_index("row") ^ lax.axis_index("col")
    for shift in (16, 8, 4, 2, 1):
        number = number ^ (number >> shift)
    return number & 1


def params(mib=32):
    return pltpu.CompilerParams(vmem_limit_bytes=mib * 1024 * 1024)


def cost(flops, bytes_accessed, transcendentals=0):
    return pl.CostEstimate(
        flops=flops, bytes_accessed=bytes_accessed, transcendentals=transcendentals
    )


def project(rows, w_lin, w_gate):
    both = jnp.dot(
        rows, jnp.concatenate([w_lin, w_gate], axis=1), preferred_element_type=F32
    )
    ch = w_lin.shape[1]
    linear = both[:, :ch]
    sigmoid = 1.0 / (1.0 + jnp.exp(-both[:, ch:]))
    return linear, sigmoid


def lead_kernel(out_ref):
    out_ref[...] = jnp.zeros_like(out_ref)


def lead():
    return pl.pallas_call(
        lead_kernel,
        out_shape=jax.ShapeDtypeStruct((8, 128), F32),
        out_specs=VMEM,
        compiler_params=params(),
        cost_estimate=cost(STAGE_COST * 8192, 4096),
        name="lead",
    )()


def stage_kernel(n, _, *refs):
    for source_ref, copy_ref in zip(refs[:n], refs[n:]):
        copy_ref[...] = source_ref[...]


def stage(after, *sources):
    n = len(sources)
    return pl.pallas_call(
        functools.partial(stage_kernel, n),
        out_shape=tuple(jax.ShapeDtypeStruct(s.shape, s.dtype) for s in sources),
        in_specs=[VMEM] * (n + 1),
        out_specs=(VMEM,) * n,
        compiler_params=params(),
        cost_estimate=cost(STAGE_COST * sources[0].size, 4 * sources[0].size),
        name="stage",
    )(after, *sources)


def pair_forward_kernel(pair_ref, w_lin_ref, w_gate_ref, flags_ref, value_ref, lin_ref, gate_ref):
    cols, keys, cz = pair_ref.shape
    row, col = lax.axis_index("row"), lax.axis_index("col")
    km = flags_ref[pl.ds(pl.multiple_of(row * keys, 16), keys)].astype(F32)
    step = min(cols, FORWARD_STEP)

    def body(s, carry):
        j0 = pl.multiple_of(s * step, step)
        rows = pair_ref[pl.ds(j0, step)].reshape(step * keys, cz)
        linear, sigmoid = project(rows, w_lin_ref[...], w_gate_ref[...])
        linear = linear.reshape(step, keys, -1)
        sigmoid = sigmoid.reshape(step, keys, -1)
        flags = flags_ref[pl.ds(pl.multiple_of(col * cols + j0, step), step)].astype(F32)
        for j in range(step):
            m = km * flags[j : j + 1]
            masked = m * sigmoid[j]
            lin = linear[j]
            value_ref[j0 + j] = (masked * lin).astype(BF16)
            lin_ref[j0 + j] = masked
            gate_ref[j0 + j] = masked * lin * (1.0 - sigmoid[j])
        return carry

    lax.fori_loop(0, cols // step, body, 0)


def pair_forward(pair, w_lin, w_gate, flags):
    cols, keys, cz = pair.shape
    ch = w_lin.shape[1]
    out = jax.ShapeDtypeStruct((cols, keys, ch), F32)
    return pl.pallas_call(
        pair_forward_kernel,
        out_shape=(jax.ShapeDtypeStruct((cols, keys, ch), BF16), out, out),
        in_specs=[VMEM] * 4,
        out_specs=(VMEM, VMEM, VMEM),
        compiler_params=params(),
        cost_estimate=cost(4 * cols * keys * cz * ch, 14 * cols * keys * ch, cols * keys * ch),
        name="pair_forward",
    )(pair, w_lin, w_gate, flags)


def slab_forward_kernel(
    n_blocks,
    even_ref,
    odd_ref,
    w_lin_ref,
    w_gate_ref,
    slab_flags_ref,
    flags_ref,
    slab_ref,
    value_ref,
    lin_ref,
    gate_ref,
):
    _, keys, cz = even_ref.shape
    rows = 2 * even_ref.shape[0] // n_blocks
    row, col = lax.axis_index("row"), lax.axis_index("col")
    km = flags_ref[pl.ds(pl.multiple_of(row * keys, 16), keys)].astype(F32)
    flags = slab_flags_ref[...].astype(F32)
    for i in range(n_blocks * rows):
        value_ref[i] = km * flags[i : i + 1]
    for b in range(n_blocks):
        first = (col ^ b) * rows
        block = (odd_ref if b % 2 else even_ref)[(b // 2) * rows : (b // 2 + 1) * rows]
        linear, sigmoid = project(
            block.reshape(rows * keys, cz),
            w_lin_ref[...],
            w_gate_ref[...],
        )
        linear = linear.reshape(rows, keys, -1)
        sigmoid = sigmoid.reshape(rows, keys, -1)
        for r in range(rows):
            i = first + r
            masked = value_ref[i] * sigmoid[r]
            slab_ref[i] = block[r]
            value_ref[i] = (masked * linear[r]).astype(BF16).astype(F32)
            lin_ref[i] = masked
            gate_ref[i] = masked * linear[r] * (1.0 - sigmoid[r])


def slab_forward(blocks, n, w_lin, w_gate, slab_flags, flags):
    half, keys, cz = blocks[0].shape
    rows = 2 * half // n
    ch = w_lin.shape[1]
    out = jax.ShapeDtypeStruct((n * rows, keys, ch), F32)
    raw = jax.ShapeDtypeStruct((n * rows, keys, cz), BF16)
    return pl.pallas_call(
        functools.partial(slab_forward_kernel, n),
        out_shape=(raw, out, out, out),
        in_specs=[VMEM] * 6,
        out_specs=(VMEM,) * 4,
        compiler_params=params(),
        cost_estimate=cost(4 * n * rows * keys * cz * ch, 16 * n * rows * keys * ch),
        name="slab_forward",
    )(*blocks, w_lin, w_gate, slab_flags, flags)


def row_of(order, per, p):
    return (lax.axis_index("row") ^ order[p // per]) * per + p % per


def widen(grads, wide):
    at = 0
    for grad_ref in grads:
        wide[at : at + grad_ref.shape[0]] = grad_ref[...].astype(F32)
        at += grad_ref.shape[0]
    return at


def add_sums(wide, count, j0, keys, values, sums_ref):
    ch = wide.shape[2]
    for p in range(count):
        total = sums_ref[p]
        for j, value in enumerate(values):
            total = total + jnp.broadcast_to(wide[p, pl.ds(j0 + j, 1), :], (keys, ch)) * value
        sums_ref[p] = total


def add_totals(wide, rows, j0, slab_value_ref, totals):
    _, keys, ch = slab_value_ref.shape
    totals = list(totals)
    for p, i in enumerate(rows):
        mine = slab_value_ref[i]
        for j in range(len(totals)):
            g = jnp.broadcast_to(wide[p, pl.ds(j0 + j, 1), :], (keys, ch))
            totals[j] = totals[j] + g * mine
    return totals


def sums_kernel(n_grads, *refs):
    grads, (value_ref, sums_ref, wide) = refs[:n_grads], refs[n_grads:]
    cols, keys, ch = value_ref.shape
    count = widen(grads, wide)
    sums_ref[...] = jnp.zeros_like(sums_ref)

    def step(s, carry):
        j0 = pl.multiple_of(s * J_STEP, J_STEP)
        values = [value_ref[j0 + j].astype(F32) for j in range(J_STEP)]
        add_sums(wide, count, j0, keys, values, sums_ref)
        return carry

    lax.fori_loop(0, cols // J_STEP, step, 0, unroll=2)


def first_sums(grads, value):
    cols, keys, ch = value.shape
    rows = sum(g.shape[0] for g in grads)
    return pl.pallas_call(
        functools.partial(sums_kernel, len(grads)),
        out_shape=jax.ShapeDtypeStruct((rows, keys, ch), F32),
        in_specs=[VMEM] * (len(grads) + 1),
        out_specs=VMEM,
        scratch_shapes=[pltpu.VMEM((rows, cols, ch), F32)],
        compiler_params=params(),
        cost_estimate=cost(2 * rows * cols * keys * ch, 8 * cols * keys * ch),
        name="first_sums_over_j",
    )(*grads, value)


def totals_kernel(order, n_grads, *refs):
    grads, (slab_value_ref, total_ref, wide) = refs[:n_grads], refs[n_grads:]
    cols, keys, ch = total_ref.shape
    count = widen(grads, wide)
    per = slab_value_ref.shape[0] // len(order)
    rows = [row_of(order, per, p) for p in range(count)]

    def step(s, carry):
        j0 = pl.multiple_of(s * J_STEP, J_STEP)
        totals = [jnp.zeros((keys, ch), F32)] * J_STEP
        totals = add_totals(wide, rows, j0, slab_value_ref, totals)
        for j in range(J_STEP):
            total_ref[j0 + j] = totals[j]
        return carry

    lax.fori_loop(0, cols // J_STEP, step, 0, unroll=2)


def first_totals(order, grads, slab_value):
    _, keys, ch = slab_value.shape
    cols = grads[0].shape[1]
    rows = sum(g.shape[0] for g in grads)
    return pl.pallas_call(
        functools.partial(totals_kernel, order, len(grads)),
        out_shape=jax.ShapeDtypeStruct((cols, keys, ch), F32),
        in_specs=[VMEM] * (len(grads) + 1),
        out_specs=VMEM,
        scratch_shapes=[pltpu.VMEM((rows, cols, ch), F32)],
        compiler_params=params(),
        cost_estimate=cost(2 * rows * cols * keys * ch, 8 * cols * keys * ch),
        name="first_totals_over_i",
    )(*grads, slab_value)


def main_kernel(
    order,
    blocks,
    grad_ref,
    total_ref,
    first_sums_ref,
    pair_ref,
    value_ref,
    lin_ref,
    gate_ref,
    slab_ref,
    slab_value_ref,
    slab_lin_ref,
    slab_gate_ref,
    d_lin_ref,
    d_gate_ref,
    sum_keep_ref,
    sum_send_ref,
    w_keep_ref,
    w_send_ref,
    wide,
    sums_ref,
    slab_sum,
):
    cols, keys, cz = pair_ref.shape
    ch = value_ref.shape[2]
    slab_rows = slab_ref.shape[0]
    done = first_sums_ref.shape[0]
    per = slab_rows // len(order)
    col = lax.axis_index("col")
    count = widen([grad_ref], wide)
    sums_ref[...] = jnp.zeros_like(sums_ref)
    rows = [row_of(order, per, done + p) for p in range(count)]

    def weights(rows, d_lin, d_gate):
        both = jnp.concatenate([d_lin, d_gate], axis=1)
        return lax.dot_general(
            rows, both, (((0,), (0,)), ((), ())), preferred_element_type=F32
        )

    pair_w = jnp.zeros((cz, 2 * ch), F32)
    for first in range(0, cols, W_STEP):
        for j0 in range(first, first + W_STEP, J_STEP):
            values = [value_ref[j0 + j].astype(F32) for j in range(J_STEP)]
            add_sums(wide, count, j0, keys, values, sums_ref)
            totals = [total_ref[j0 + j] for j in range(J_STEP)]
            totals = add_totals(wide, rows, j0, slab_value_ref, totals)
            for j in range(J_STEP):
                d_lin_ref[j0 + j] = (totals[j] * lin_ref[j0 + j]).astype(BF16)
                d_gate_ref[j0 + j] = (totals[j] * gate_ref[j0 + j]).astype(BF16)
        some = slice(first, first + W_STEP)
        pair_w = pair_w + weights(
            pair_ref[some].reshape(W_STEP * keys, cz),
            d_lin_ref[some].reshape(W_STEP * keys, ch),
            d_gate_ref[some].reshape(W_STEP * keys, ch),
        )
    for p in range(done):
        slab_sum[row_of(order, per, p)] = first_sums_ref[p]
    for p in range(count):
        slab_sum[rows[p]] = sums_ref[p]

    sums = slab_sum[...]
    s_lin = (sums * slab_lin_ref[...]).astype(BF16).reshape(slab_rows * keys, ch)
    s_gate = (sums * slab_gate_ref[...]).astype(BF16).reshape(slab_rows * keys, ch)
    slab_w = weights(slab_ref[...].reshape(slab_rows * keys, cz), s_lin, s_gate)
    first = parity() == 0
    keep = jnp.where(first, slab_w, pair_w)
    send = jnp.where(first, pair_w, slab_w)
    for h in range(2):
        w_keep_ref[h] = keep[:, h * ch : (h + 1) * ch]
        w_send_ref[h] = send[:, h * ch : (h + 1) * ch]
    own = sum_keep_ref.shape[1]
    for n, b in enumerate(blocks):
        sum_keep_ref[n] = slab_sum[pl.ds((col ^ b) * own, own)]
        sum_send_ref[n] = slab_sum[pl.ds((col ^ b ^ 1) * own, own)]


def main_part(order, blocks, grads, first, pair, forward, slab):
    cols, keys, cz = pair.shape
    ch = forward[0].shape[2]
    slab_rows = slab[0].shape[0]
    own = slab_rows // (2 * len(blocks))
    d_type = jax.ShapeDtypeStruct((cols, keys, ch), BF16)
    s_type = jax.ShapeDtypeStruct((len(blocks), own, keys, ch), F32)
    w_type = jax.ShapeDtypeStruct((2, cz, ch), F32)
    return pl.pallas_call(
        functools.partial(main_kernel, order, blocks),
        out_shape=(d_type, d_type, s_type, s_type, w_type, w_type),
        in_specs=[VMEM] * 11,
        out_specs=(VMEM,) * 6,
        scratch_shapes=[
            pltpu.VMEM((grads.shape[0], cols, ch), F32),
            pltpu.VMEM((grads.shape[0], keys, ch), F32),
            pltpu.VMEM((slab_rows, keys, ch), F32),
        ],
        compiler_params=params(),
        cost_estimate=cost(8 * cols * keys * cz * ch, 16 * cols * keys * ch),
        name="last_rows",
    )(grads, *first, pair, *forward, *slab)


def pair_out_kernel(d_lin_ref, d_gate_ref, w_lin_ref, w_gate_ref, out_ref):
    rows, ch = d_lin_ref.shape
    weights = jnp.concatenate([w_lin_ref[...], w_gate_ref[...]], axis=1)
    step = rows

    def body(s, carry):
        at = pl.ds(pl.multiple_of(s * step, step), step)
        both = jnp.concatenate([d_lin_ref[at, :], d_gate_ref[at, :]], axis=1)
        out = lax.dot_general(
            both, weights, (((1,), (1,)), ((), ())), preferred_element_type=F32
        )
        out_ref[at, :] = out.astype(BF16)
        return carry

    lax.fori_loop(0, rows // step, body, 0)


def pair_out(d_lin, d_gate, w_lin, w_gate):
    cols, keys, ch = d_lin.shape
    cz = w_lin.shape[0]
    out = pl.pallas_call(
        pair_out_kernel,
        out_shape=jax.ShapeDtypeStruct((cols * keys, cz), BF16),
        in_specs=[VMEM] * 4,
        out_specs=VMEM,
        compiler_params=params(),
        cost_estimate=cost(4 * cols * keys * cz * ch, 6 * cols * keys * ch),
        name="pair_input_grad",
    )(d_lin.reshape(cols * keys, ch), d_gate.reshape(cols * keys, ch), w_lin, w_gate)
    return out.reshape(cols, keys, cz)


def fold_kernel(kept_ref, got_ref, sum_ref, moved_ref):
    half = sum_ref.shape[0]
    sum_ref[...] = kept_ref[:half] + got_ref[:half].astype(F32)
    moved_ref[...] = (kept_ref[half:] + got_ref[half:].astype(F32)).astype(BF16)


def fold(kept, got):
    half = (kept.shape[0] // 2,) + kept.shape[1:]
    return pl.pallas_call(
        fold_kernel,
        out_shape=(jax.ShapeDtypeStruct(half, F32), jax.ShapeDtypeStruct(half, BF16)),
        in_specs=[VMEM, VMEM],
        out_specs=(VMEM, VMEM),
        compiler_params=params(),
        cost_estimate=cost(STAGE_COST * kept.size, 8 * kept.size),
        name="fold",
    )(kept, got)


def slab_out_kernel(sum_ref, got_ref, lin_ref, gate_ref, w_lin_ref, w_gate_ref, out_ref):
    own, keys, ch = sum_ref.shape
    col = lax.axis_index("col")
    at = pl.ds(col * own, own)
    total = sum_ref[...] + got_ref[...].astype(F32)
    d_lin = (total * lin_ref[at]).astype(BF16).reshape(own * keys, ch)
    d_gate = (total * gate_ref[at]).astype(BF16).reshape(own * keys, ch)
    both = jnp.concatenate([d_lin, d_gate], axis=1)
    weights = jnp.concatenate([w_lin_ref[...], w_gate_ref[...]], axis=1)
    out = lax.dot_general(both, weights, (((1,), (1,)), ((), ())), preferred_element_type=F32)
    out_ref[...] = out.astype(BF16).reshape(own, keys, w_lin_ref.shape[0])


def slab_out(total, got, lin, gate, w_lin, w_gate):
    own, keys, ch = total.shape
    cz = w_lin.shape[0]
    return pl.pallas_call(
        slab_out_kernel,
        out_shape=jax.ShapeDtypeStruct((own, keys, cz), BF16),
        in_specs=[VMEM] * 6,
        out_specs=VMEM,
        compiler_params=params(),
        cost_estimate=cost(4 * own * keys * cz * ch, 16 * own * keys * ch),
        name="slab_input_grad",
    )(total, got, lin, gate, w_lin, w_gate)


def on_device(
    pair_slab, pair_full, grad_out, w_a_lin, w_a_gate, w_b_lin, w_b_gate, mask_slab, mask_residue
):
    n_row, n_col = lax.axis_size("row"), lax.axis_size("col")
    row_bits, col_bits = bits_of(n_row), bits_of(n_col)
    residues = mask_residue.shape[0]

    steps = [row_bits[-1]] + row_bits[1:-1] + row_bits[:1]
    ch = w_a_lin.shape[1]
    held, own_slab = stage(lead(), grad_out, pair_slab)
    order = [0]
    blocks = {0: own_slab}
    for bit in reversed(col_bits[1:]):
        for b in list(blocks):
            blocks[b ^ bit] = swap(blocks[b], "col", bit)
    got = swap(grad_out, "row", steps[0])
    for bit, later in zip(steps, steps[1:-1]):
        held = jnp.concatenate([held, got], axis=0)
        order = order + [r ^ bit for r in order]
        got = swap(held, "row", later)
    masks = lax.optimization_barrier(((mask_slab, mask_residue), held, blocks))[0]
    slab_flags, flags = (
        jnp.broadcast_to(m.astype(BF16)[:, None], m.shape + (ch,)) for m in masks
    )
    value, lin, gate = pair_forward(pair_full, w_b_lin, w_b_gate, flags)
    got_last = swap(held, "row", steps[-1])
    got, value = lax.optimization_barrier((got, value))
    got_both = swap(got, "row", steps[-1])
    for bit in steps[-2:]:
        order = order + [r ^ bit for r in order]
    slabs = jnp.concatenate([blocks[b] for b in sorted(blocks)], axis=0)
    slabs = [slabs, swap(slabs, "col", 1)]
    slab = slab_forward(slabs, n_col, w_a_lin, w_a_gate, slab_flags, flags)
    pieces = [held, got, got_last]
    first = (first_totals(order, pieces, slab[1]), first_sums(pieces, value))
    kept = [0]
    for bit in reversed(col_bits[1:]):
        kept = kept + [b ^ bit for b in kept]
    d_lin, d_gate, sum_keep, sum_send, w_keep, w_send = main_part(
        order, kept, got_both, first, pair_full, (value, lin, gate), slab
    )
    pair_bit, col = col_bits[1], lax.axis_index("col")
    got_w = swap(w_send, "col", 1)
    sum_send, _ = lax.optimization_barrier((sum_send, got_w))
    side = w_keep + got_w
    upper = (col & pair_bit) != 0
    moved = jnp.where(upper, side[0], side[1]).astype(BF16)
    part = jnp.where(upper, side[1], side[0])
    part = part + swap_chips(moved, pair_bit).astype(F32)
    bits = col_bits[2:] + [bit * n_col for bit in row_bits]
    sums, got = sum_keep, swap(sum_send, "col", 1)
    for bit in bits:
        narrow = part.astype(BF16)
        if bit == bits[1]:
            narrow, got = lax.optimization_barrier((narrow, got))
            for far in col_bits[1:]:
                sums, moved = fold(sums, got)
                got = swap(moved, "col", far)
        if bit == bits[0]:
            narrow, d_lin, d_gate = lax.optimization_barrier((narrow, d_lin, d_gate))
            grad_pair = pair_out(d_lin, d_gate, w_b_lin, w_b_gate)
        if bit == bits[-1]:
            narrow, grad_pair = lax.optimization_barrier((narrow, grad_pair))
        part = narrow.astype(F32) + swap_chips(narrow, bit).astype(F32)
    narrow = part.astype(BF16)
    mine = jnp.stack([narrow, swap_chips(narrow, pair_bit)])
    both = [mine, swap(mine, "col", 1)]
    both = [jnp.where(upper, m[::-1], m).astype(F32) / residues for m in both]
    first = parity() == 0
    grad_weights = jnp.where(
        first, jnp.concatenate(both, axis=0), jnp.concatenate(both[::-1], axis=0)
    )
    grad_slab = slab_out(sums[0], got[0], slab[2], slab[3], w_a_lin, w_a_gate)
    return (grad_slab, grad_pair, grad_weights)


def solution(mesh):
    return jax.shard_map(
        on_device,
        mesh=mesh,
        in_specs=(
            P("col", "row", None),
            P("col", "row", None),
            P("row", "col", None),
            P(),
            P(),
            P(),
            P(),
            P(),
            P(),
        ),
        out_specs=(P("col", "row", None), P("col", "row", None), P()),
        check_vma=False,
    )
```

```python
import functools

import jax
import jax.numpy as jnp
from jax import lax
from jax.experimental import pallas as pl
from jax.experimental.pallas import tpu as pltpu
from jax.sharding import PartitionSpec as P

F32 = jnp.float32
BF16 = jnp.bfloat16
VMEM = pl.BlockSpec(memory_space=pltpu.VMEM)
WHOLE = pl.BlockSpec()
SMEM = pl.BlockSpec(memory_space=pltpu.SMEM)
J_STEP = 4
FORWARD_STEP = 32
W_STEP = 16
STAGE_COST = 400000


def bits_of(size):
    return [1 << b for b in range(size.bit_length() - 1)]


def swap(value, axis, bit):
    size = lax.axis_size(axis)
    return lax.ppermute(value, axis, [(d, d ^ bit) for d in range(size)])


def swap_chips(value, bit, flip=1):
    n_row, n_col = lax.axis_size("row"), lax.axis_size("col")
    pairs = [(d, d ^ bit ^ flip) for d in range(n_row * n_col)]
    return lax.ppermute(value, ("row", "col"), pairs)


def parity():
    number = lax.axis_index("row") ^ lax.axis_index("col")
    for shift in (16, 8, 4, 2, 1):
        number = number ^ (number >> shift)
    return number & 1


def params(mib=32):
    return pltpu.CompilerParams(vmem_limit_bytes=mib * 1024 * 1024)


def cost(flops, bytes_accessed, transcendentals=0):
    return pl.CostEstimate(
        flops=flops, bytes_accessed=bytes_accessed, transcendentals=transcendentals
    )


def project(rows, w_lin, w_gate):
    both = jnp.dot(
        rows, jnp.concatenate([w_lin, w_gate], axis=1), preferred_element_type=F32
    )
    ch = w_lin.shape[1]
    linear = both[:, :ch]
    sigmoid = 1.0 / (1.0 + jnp.exp(-both[:, ch:]))
    return linear, sigmoid


def lead_kernel(out_ref):
    out_ref[...] = jnp.zeros_like(out_ref)


def lead():
    return pl.pallas_call(
        lead_kernel,
        out_shape=jax.ShapeDtypeStruct((8, 128), F32),
        out_specs=VMEM,
        compiler_params=params(),
        cost_estimate=cost(STAGE_COST * 8192, 4096),
        name="lead",
    )()


def stage_kernel(n, _, *refs):
    for source_ref, copy_ref in zip(refs[:n], refs[n:]):
        copy_ref[...] = source_ref[...]


def stage(after, *sources):
    n = len(sources)
    return pl.pallas_call(
        functools.partial(stage_kernel, n),
        out_shape=tuple(jax.ShapeDtypeStruct(s.shape, s.dtype) for s in sources),
        in_specs=[VMEM] * (n + 1),
        out_specs=(VMEM,) * n,
        compiler_params=params(),
        cost_estimate=cost(STAGE_COST * sources[0].size, 4 * sources[0].size),
        name="stage",
    )(after, *sources)


def pair_forward_kernel(pair_ref, w_lin_ref, w_gate_ref, flags_ref, value_ref, lin_ref, gate_ref):
    cols, keys, cz = pair_ref.shape
    row, col = lax.axis_index("row"), lax.axis_index("col")
    km = flags_ref[pl.ds(pl.multiple_of(row * keys, 16), keys)].astype(F32)
    step = min(cols, FORWARD_STEP)

    def body(s, carry):
        j0 = pl.multiple_of(s * step, step)
        rows = pair_ref[pl.ds(j0, step)].reshape(step * keys, cz)
        linear, sigmoid = project(rows, w_lin_ref[...], w_gate_ref[...])
        linear = linear.reshape(step, keys, -1)
        sigmoid = sigmoid.reshape(step, keys, -1)
        flags = flags_ref[pl.ds(pl.multiple_of(col * cols + j0, step), step)].astype(F32)
        for j in range(step):
            m = km * flags[j : j + 1]
            masked = m * sigmoid[j]
            lin = linear[j]
            value_ref[j0 + j] = (masked * lin).astype(BF16)
            lin_ref[j0 + j] = masked
            gate_ref[j0 + j] = masked * lin * (1.0 - sigmoid[j])
        return carry

    lax.fori_loop(0, cols // step, body, 0)


def pair_forward(pair, w_lin, w_gate, flags):
    cols, keys, cz = pair.shape
    ch = w_lin.shape[1]
    out = jax.ShapeDtypeStruct((cols, keys, ch), F32)
    return pl.pallas_call(
        pair_forward_kernel,
        out_shape=(jax.ShapeDtypeStruct((cols, keys, ch), BF16), out, out),
        in_specs=[VMEM] * 4,
        out_specs=(VMEM, VMEM, VMEM),
        compiler_params=params(),
        cost_estimate=cost(4 * cols * keys * cz * ch, 14 * cols * keys * ch, cols * keys * ch),
        name="pair_forward",
    )(pair, w_lin, w_gate, flags)


def slab_forward_kernel(
    n_blocks,
    even_ref,
    odd_ref,
    w_lin_ref,
    w_gate_ref,
    slab_flags_ref,
    flags_ref,
    slab_ref,
    value_ref,
    lin_ref,
    gate_ref,
):
    _, keys, cz = even_ref.shape
    rows = 2 * even_ref.shape[0] // n_blocks
    row, col = lax.axis_index("row"), lax.axis_index("col")
    km = flags_ref[pl.ds(pl.multiple_of(row * keys, 16), keys)].astype(F32)
    flags = slab_flags_ref[...].astype(F32)
    for i in range(n_blocks * rows):
        value_ref[i] = km * flags[i : i + 1]
    for b in range(n_blocks):
        first = (col ^ b) * rows
        block = (odd_ref if b % 2 else even_ref)[(b // 2) * rows : (b // 2 + 1) * rows]
        linear, sigmoid = project(
            block.reshape(rows * keys, cz),
            w_lin_ref[...],
            w_gate_ref[...],
        )
        linear = linear.reshape(rows, keys, -1)
        sigmoid = sigmoid.reshape(rows, keys, -1)
        for r in range(rows):
            i = first + r
            masked = value_ref[i] * sigmoid[r]
            slab_ref[i] = block[r]
            value_ref[i] = (masked * linear[r]).astype(BF16).astype(F32)
            lin_ref[i] = masked
            gate_ref[i] = masked * linear[r] * (1.0 - sigmoid[r])


def slab_forward(blocks, n, w_lin, w_gate, slab_flags, flags):
    half, keys, cz = blocks[0].shape
    rows = 2 * half // n
    ch = w_lin.shape[1]
    out = jax.ShapeDtypeStruct((n * rows, keys, ch), F32)
    raw = jax.ShapeDtypeStruct((n * rows, keys, cz), BF16)
    return pl.pallas_call(
        functools.partial(slab_forward_kernel, n),
        out_shape=(raw, out, out, out),
        in_specs=[VMEM] * 6,
        out_specs=(VMEM,) * 4,
        compiler_params=params(),
        cost_estimate=cost(4 * n * rows * keys * cz * ch, 16 * n * rows * keys * ch),
        name="slab_forward",
    )(*blocks, w_lin, w_gate, slab_flags, flags)


def row_of(order, per, p):
    return (lax.axis_index("row") ^ order[p // per]) * per + p % per


def widen(grads, wide):
    at = 0
    for grad_ref in grads:
        wide[at : at + grad_ref.shape[0]] = grad_ref[...].astype(F32)
        at += grad_ref.shape[0]
    return at


def add_sums(wide, count, j0, keys, values, sums_ref):
    ch = wide.shape[2]
    for p in range(count):
        total = sums_ref[p]
        for j, value in enumerate(values):
            total = total + jnp.broadcast_to(wide[p, pl.ds(j0 + j, 1), :], (keys, ch)) * value
        sums_ref[p] = total


def add_totals(wide, rows, j0, slab_value_ref, totals):
    _, keys, ch = slab_value_ref.shape
    totals = list(totals)
    for p, i in enumerate(rows):
        mine = slab_value_ref[i]
        for j in range(len(totals)):
            g = jnp.broadcast_to(wide[p, pl.ds(j0 + j, 1), :], (keys, ch))
            totals[j] = totals[j] + g * mine
    return totals


def sums_kernel(n_grads, *refs):
    grads, (value_ref, sums_ref, wide) = refs[:n_grads], refs[n_grads:]
    cols, keys, ch = value_ref.shape
    count = widen(grads, wide)
    sums_ref[...] = jnp.zeros_like(sums_ref)

    def step(s, carry):
        j0 = pl.multiple_of(s * J_STEP, J_STEP)
        values = [value_ref[j0 + j].astype(F32) for j in range(J_STEP)]
        add_sums(wide, count, j0, keys, values, sums_ref)
        return carry

    lax.fori_loop(0, cols // J_STEP, step, 0, unroll=2)


def first_sums(grads, value):
    cols, keys, ch = value.shape
    rows = sum(g.shape[0] for g in grads)
    return pl.pallas_call(
        functools.partial(sums_kernel, len(grads)),
        out_shape=jax.ShapeDtypeStruct((rows, keys, ch), F32),
        in_specs=[VMEM] * (len(grads) + 1),
        out_specs=VMEM,
        scratch_shapes=[pltpu.VMEM((rows, cols, ch), F32)],
        compiler_params=params(),
        cost_estimate=cost(2 * rows * cols * keys * ch, 8 * cols * keys * ch),
        name="first_sums_over_j",
    )(*grads, value)


def totals_kernel(order, n_grads, *refs):
    grads, (slab_value_ref, total_ref, wide) = refs[:n_grads], refs[n_grads:]
    cols, keys, ch = total_ref.shape
    count = widen(grads, wide)
    per = slab_value_ref.shape[0] // len(order)
    rows = [row_of(order, per, p) for p in range(count)]

    def step(s, carry):
        j0 = pl.multiple_of(s * J_STEP, J_STEP)
        totals = [jnp.zeros((keys, ch), F32)] * J_STEP
        totals = add_totals(wide, rows, j0, slab_value_ref, totals)
        for j in range(J_STEP):
            total_ref[j0 + j] = totals[j]
        return carry

    lax.fori_loop(0, cols // J_STEP, step, 0, unroll=2)


def first_totals(order, grads, slab_value):
    _, keys, ch = slab_value.shape
    cols = grads[0].shape[1]
    rows = sum(g.shape[0] for g in grads)
    return pl.pallas_call(
        functools.partial(totals_kernel, order, len(grads)),
        out_shape=jax.ShapeDtypeStruct((cols, keys, ch), F32),
        in_specs=[VMEM] * (len(grads) + 1),
        out_specs=VMEM,
        scratch_shapes=[pltpu.VMEM((rows, cols, ch), F32)],
        compiler_params=params(),
        cost_estimate=cost(2 * rows * cols * keys * ch, 8 * cols * keys * ch),
        name="first_totals_over_i",
    )(*grads, slab_value)


def main_kernel(
    order,
    blocks,
    grad_ref,
    total_ref,
    first_sums_ref,
    pair_ref,
    value_ref,
    lin_ref,
    gate_ref,
    slab_ref,
    slab_value_ref,
    slab_lin_ref,
    slab_gate_ref,
    d_lin_ref,
    d_gate_ref,
    sum_keep_ref,
    sum_send_ref,
    w_keep_ref,
    w_send_ref,
    wide,
    sums_ref,
    slab_sum,
):
    cols, keys, cz = pair_ref.shape
    ch = value_ref.shape[2]
    slab_rows = slab_ref.shape[0]
    done = first_sums_ref.shape[0]
    per = slab_rows // len(order)
    col = lax.axis_index("col")
    count = widen([grad_ref], wide)
    sums_ref[...] = jnp.zeros_like(sums_ref)
    rows = [row_of(order, per, done + p) for p in range(count)]

    def weights(rows, d_lin, d_gate):
        both = jnp.concatenate([d_lin, d_gate], axis=1)
        return lax.dot_general(
            rows, both, (((0,), (0,)), ((), ())), preferred_element_type=F32
        )

    pair_w = jnp.zeros((cz, 2 * ch), F32)
    for first in range(0, cols, W_STEP):
        for j0 in range(first, first + W_STEP, J_STEP):
            values = [value_ref[j0 + j].astype(F32) for j in range(J_STEP)]
            add_sums(wide, count, j0, keys, values, sums_ref)
            totals = [total_ref[j0 + j] for j in range(J_STEP)]
            totals = add_totals(wide, rows, j0, slab_value_ref, totals)
            for j in range(J_STEP):
                d_lin_ref[j0 + j] = (totals[j] * lin_ref[j0 + j]).astype(BF16)
                d_gate_ref[j0 + j] = (totals[j] * gate_ref[j0 + j]).astype(BF16)
        some = slice(first, first + W_STEP)
        pair_w = pair_w + weights(
            pair_ref[some].reshape(W_STEP * keys, cz),
            d_lin_ref[some].reshape(W_STEP * keys, ch),
            d_gate_ref[some].reshape(W_STEP * keys, ch),
        )
    for p in range(done):
        slab_sum[row_of(order, per, p)] = first_sums_ref[p]
    for p in range(count):
        slab_sum[rows[p]] = sums_ref[p]

    sums = slab_sum[...]
    s_lin = (sums * slab_lin_ref[...]).astype(BF16).reshape(slab_rows * keys, ch)
    s_gate = (sums * slab_gate_ref[...]).astype(BF16).reshape(slab_rows * keys, ch)
    slab_w = weights(slab_ref[...].reshape(slab_rows * keys, cz), s_lin, s_gate)
    first = parity() == 0
    keep = jnp.where(first, slab_w, pair_w)
    send = jnp.where(first, pair_w, slab_w)
    for h in range(2):
        w_keep_ref[h] = keep[:, h * ch : (h + 1) * ch]
        w_send_ref[h] = send[:, h * ch : (h + 1) * ch]
    own = sum_keep_ref.shape[1]
    for n, b in enumerate(blocks):
        sum_keep_ref[n] = slab_sum[pl.ds((col ^ b) * own, own)]
        sum_send_ref[n] = slab_sum[pl.ds((col ^ b ^ 1) * own, own)]


def main_part(order, blocks, grads, first, pair, forward, slab):
    cols, keys, cz = pair.shape
    ch = forward[0].shape[2]
    slab_rows = slab[0].shape[0]
    own = slab_rows // (2 * len(blocks))
    d_type = jax.ShapeDtypeStruct((cols, keys, ch), BF16)
    s_type = jax.ShapeDtypeStruct((len(blocks), own, keys, ch), F32)
    w_type = jax.ShapeDtypeStruct((2, cz, ch), F32)
    return pl.pallas_call(
        functools.partial(main_kernel, order, blocks),
        out_shape=(d_type, d_type, s_type, s_type, w_type, w_type),
        in_specs=[VMEM] * 11,
        out_specs=(VMEM,) * 6,
        scratch_shapes=[
            pltpu.VMEM((grads.shape[0], cols, ch), F32),
            pltpu.VMEM((grads.shape[0], keys, ch), F32),
            pltpu.VMEM((slab_rows, keys, ch), F32),
        ],
        compiler_params=params(),
        cost_estimate=cost(8 * cols * keys * cz * ch, 16 * cols * keys * ch),
        name="last_rows",
    )(grads, *first, pair, *forward, *slab)


def pair_out_kernel(d_lin_ref, d_gate_ref, w_lin_ref, w_gate_ref, out_ref):
    rows, ch = d_lin_ref.shape
    weights = jnp.concatenate([w_lin_ref[...], w_gate_ref[...]], axis=1)
    step = rows

    def body(s, carry):
        at = pl.ds(pl.multiple_of(s * step, step), step)
        both = jnp.concatenate([d_lin_ref[at, :], d_gate_ref[at, :]], axis=1)
        out = lax.dot_general(
            both, weights, (((1,), (1,)), ((), ())), preferred_element_type=F32
        )
        out_ref[at, :] = out.astype(BF16)
        return carry

    lax.fori_loop(0, rows // step, body, 0)


def pair_out(d_lin, d_gate, w_lin, w_gate):
    cols, keys, ch = d_lin.shape
    cz = w_lin.shape[0]
    out = pl.pallas_call(
        pair_out_kernel,
        out_shape=jax.ShapeDtypeStruct((cols * keys, cz), BF16),
        in_specs=[VMEM] * 4,
        out_specs=VMEM,
        compiler_params=params(),
        cost_estimate=cost(4 * cols * keys * cz * ch, 6 * cols * keys * ch),
        name="pair_input_grad",
    )(d_lin.reshape(cols * keys, ch), d_gate.reshape(cols * keys, ch), w_lin, w_gate)
    return out.reshape(cols, keys, cz)


def fold_kernel(kept_ref, got_ref, sum_ref, moved_ref):
    half = sum_ref.shape[0]
    sum_ref[...] = kept_ref[:half] + got_ref[:half].astype(F32)
    moved_ref[...] = (kept_ref[half:] + got_ref[half:].astype(F32)).astype(BF16)


def fold(kept, got):
    half = (kept.shape[0] // 2,) + kept.shape[1:]
    return pl.pallas_call(
        fold_kernel,
        out_shape=(jax.ShapeDtypeStruct(half, F32), jax.ShapeDtypeStruct(half, BF16)),
        in_specs=[VMEM, VMEM],
        out_specs=(VMEM, VMEM),
        compiler_params=params(),
        cost_estimate=cost(STAGE_COST * kept.size, 8 * kept.size),
        name="fold",
    )(kept, got)


def slab_out_kernel(sum_ref, got_ref, lin_ref, gate_ref, w_lin_ref, w_gate_ref, out_ref):
    own, keys, ch = sum_ref.shape
    col = lax.axis_index("col")
    at = pl.ds(col * own, own)
    total = sum_ref[...] + got_ref[...].astype(F32)
    d_lin = (total * lin_ref[at]).astype(BF16).reshape(own * keys, ch)
    d_gate = (total * gate_ref[at]).astype(BF16).reshape(own * keys, ch)
    both = jnp.concatenate([d_lin, d_gate], axis=1)
    weights = jnp.concatenate([w_lin_ref[...], w_gate_ref[...]], axis=1)
    out = lax.dot_general(both, weights, (((1,), (1,)), ((), ())), preferred_element_type=F32)
    out_ref[...] = out.astype(BF16).reshape(own, keys, w_lin_ref.shape[0])


def slab_out(total, got, lin, gate, w_lin, w_gate):
    own, keys, ch = total.shape
    cz = w_lin.shape[0]
    return pl.pallas_call(
        slab_out_kernel,
        out_shape=jax.ShapeDtypeStruct((own, keys, cz), BF16),
        in_specs=[VMEM] * 6,
        out_specs=VMEM,
        compiler_params=params(),
        cost_estimate=cost(4 * own * keys * cz * ch, 16 * own * keys * ch),
        name="slab_input_grad",
    )(total, got, lin, gate, w_lin, w_gate)


def on_device(
    pair_slab, pair_full, grad_out, w_a_lin, w_a_gate, w_b_lin, w_b_gate, mask_slab, mask_residue
):
    n_row, n_col = lax.axis_size("row"), lax.axis_size("col")
    row_bits, col_bits = bits_of(n_row), bits_of(n_col)
    residues = mask_residue.shape[0]

    steps = [row_bits[-1]] + row_bits[1:-1] + row_bits[:1]
    ch = w_a_lin.shape[1]
    held, own_slab = stage(lead(), grad_out, pair_slab)
    order = [0]
    blocks = {0: own_slab}
    for bit in reversed(col_bits[1:]):
        for b in list(blocks):
            blocks[b ^ bit] = swap(blocks[b], "col", bit)
    got = swap(grad_out, "row", steps[0])
    for bit, later in zip(steps, steps[1:-1]):
        held = jnp.concatenate([held, got], axis=0)
        order = order + [r ^ bit for r in order]
        got = swap(held, "row", later)
    masks = lax.optimization_barrier(((mask_slab, mask_residue), held, blocks))[0]
    slab_flags, flags = (
        jnp.broadcast_to(m.astype(BF16)[:, None], m.shape + (ch,)) for m in masks
    )
    value, lin, gate = pair_forward(pair_full, w_b_lin, w_b_gate, flags)
    got_last = swap(held, "row", steps[-1])
    got, value = lax.optimization_barrier((got, value))
    got_both = swap(got, "row", steps[-1])
    for bit in steps[-2:]:
        order = order + [r ^ bit for r in order]
    slabs = jnp.concatenate([blocks[b] for b in sorted(blocks)], axis=0)
    slabs = [slabs, swap(slabs, "col", 1)]
    slab = slab_forward(slabs, n_col, w_a_lin, w_a_gate, slab_flags, flags)
    pieces = [held, got, got_last]
    first = (first_totals(order, pieces, slab[1]), first_sums(pieces, value))
    kept = [0]
    for bit in reversed(col_bits[1:]):
        kept = kept + [b ^ bit for b in kept]
    d_lin, d_gate, sum_keep, sum_send, w_keep, w_send = main_part(
        order, kept, got_both, first, pair_full, (value, lin, gate), slab
    )
    pair_bit, col = col_bits[1], lax.axis_index("col")
    got_w = swap(w_send, "col", 1)
    sum_send, _ = lax.optimization_barrier((sum_send, got_w))
    side = w_keep + got_w
    upper = (col & pair_bit) != 0
    moved = jnp.where(upper, side[0], side[1]).astype(BF16)
    part = jnp.where(upper, side[1], side[0])
    part = part + swap_chips(moved, pair_bit).astype(F32)
    bits = col_bits[2:] + [bit * n_col for bit in row_bits]
    sums, got = sum_keep, swap(sum_send, "col", 1)
    narrow = part.astype(BF16)
    near, next_ = bits[0], bits[1]
    diagonal = swap_chips(narrow, near | next_, 0)
    part = narrow.astype(F32) + swap_chips(narrow, near).astype(F32)
    part = part + (swap_chips(narrow, next_).astype(F32) + diagonal.astype(F32))
    for bit in bits[2:]:
        narrow = part.astype(BF16)
        if bit == bits[2]:
            narrow, got, d_lin, d_gate = lax.optimization_barrier((narrow, got, d_lin, d_gate))
            grad_pair = pair_out(d_lin, d_gate, w_b_lin, w_b_gate)
            for far in col_bits[1:]:
                sums, moved = fold(sums, got)
                got = swap(moved, "col", far)
        part = narrow.astype(F32) + swap_chips(narrow, bit).astype(F32)
    narrow = part.astype(BF16)
    mine = jnp.stack([narrow, swap_chips(narrow, pair_bit)])
    both = [mine, swap(mine, "col", 1)]
    both = [jnp.where(upper, m[::-1], m).astype(F32) / residues for m in both]
    first = parity() == 0
    grad_weights = jnp.where(
        first, jnp.concatenate(both, axis=0), jnp.concatenate(both[::-1], axis=0)
    )
    grad_slab = slab_out(sums[0], got[0], slab[2], slab[3], w_a_lin, w_a_gate)
    return (grad_slab, grad_pair, grad_weights)


def solution(mesh):
    return jax.shard_map(
        on_device,
        mesh=mesh,
        in_specs=(
            P("col", "row", None),
            P("col", "row", None),
            P("row", "col", None),
            P(),
            P(),
            P(),
            P(),
            P(),
            P(),
        ),
        out_specs=(P("col", "row", None), P("col", "row", None), P()),
        check_vma=False,
    )
```

```python
import functools

import jax
import jax.numpy as jnp
from jax import lax
from jax.experimental import pallas as pl
from jax.experimental.pallas import tpu as pltpu
from jax.sharding import PartitionSpec as P

F32 = jnp.float32
BF16 = jnp.bfloat16
VMEM = pl.BlockSpec(memory_space=pltpu.VMEM)
WHOLE = pl.BlockSpec()
SMEM = pl.BlockSpec(memory_space=pltpu.SMEM)
J_STEP = 4
FORWARD_STEP = 32
W_STEP = 16
STAGE_COST = 400000


def bits_of(size):
    return [1 << b for b in range(size.bit_length() - 1)]


def swap(value, axis, bit):
    size = lax.axis_size(axis)
    return lax.ppermute(value, axis, [(d, d ^ bit) for d in range(size)])


def swap_chips(value, bit, flip=1):
    n_row, n_col = lax.axis_size("row"), lax.axis_size("col")
    pairs = [(d, d ^ bit ^ flip) for d in range(n_row * n_col)]
    return lax.ppermute(value, ("row", "col"), pairs)


def parity():
    number = lax.axis_index("row") ^ lax.axis_index("col")
    for shift in (16, 8, 4, 2, 1):
        number = number ^ (number >> shift)
    return number & 1


def params(mib=32):
    return pltpu.CompilerParams(vmem_limit_bytes=mib * 1024 * 1024)


def cost(flops, bytes_accessed, transcendentals=0):
    return pl.CostEstimate(
        flops=flops, bytes_accessed=bytes_accessed, transcendentals=transcendentals
    )


def project(rows, w_lin, w_gate):
    both = jnp.dot(
        rows, jnp.concatenate([w_lin, w_gate], axis=1), preferred_element_type=F32
    )
    ch = w_lin.shape[1]
    linear = both[:, :ch]
    sigmoid = 1.0 / (1.0 + jnp.exp(-both[:, ch:]))
    return linear, sigmoid


def lead_kernel(out_ref):
    out_ref[...] = jnp.zeros_like(out_ref)


def lead():
    return pl.pallas_call(
        lead_kernel,
        out_shape=jax.ShapeDtypeStruct((8, 128), F32),
        out_specs=VMEM,
        compiler_params=params(),
        cost_estimate=cost(STAGE_COST * 8192, 4096),
        name="lead",
    )()


def stage_kernel(n, _, *refs):
    for source_ref, copy_ref in zip(refs[:n], refs[n:]):
        copy_ref[...] = source_ref[...]


def stage(after, *sources):
    n = len(sources)
    return pl.pallas_call(
        functools.partial(stage_kernel, n),
        out_shape=tuple(jax.ShapeDtypeStruct(s.shape, s.dtype) for s in sources),
        in_specs=[VMEM] * (n + 1),
        out_specs=(VMEM,) * n,
        compiler_params=params(),
        cost_estimate=cost(STAGE_COST * sources[0].size, 4 * sources[0].size),
        name="stage",
    )(after, *sources)


def pair_forward_kernel(pair_ref, w_lin_ref, w_gate_ref, flags_ref, value_ref, lin_ref, gate_ref):
    cols, keys, cz = pair_ref.shape
    row, col = lax.axis_index("row"), lax.axis_index("col")
    km = flags_ref[pl.ds(pl.multiple_of(row * keys, 16), keys)].astype(F32)
    step = min(cols, FORWARD_STEP)

    def body(s, carry):
        j0 = pl.multiple_of(s * step, step)
        rows = pair_ref[pl.ds(j0, step)].reshape(step * keys, cz)
        linear, sigmoid = project(rows, w_lin_ref[...], w_gate_ref[...])
        linear = linear.reshape(step, keys, -1)
        sigmoid = sigmoid.reshape(step, keys, -1)
        flags = flags_ref[pl.ds(pl.multiple_of(col * cols + j0, step), step)].astype(F32)
        for j in range(step):
            m = km * flags[j : j + 1]
            masked = m * sigmoid[j]
            lin = linear[j]
            value_ref[j0 + j] = (masked * lin).astype(BF16)
            lin_ref[j0 + j] = masked
            gate_ref[j0 + j] = masked * lin * (1.0 - sigmoid[j])
        return carry

    lax.fori_loop(0, cols // step, body, 0)


def pair_forward(pair, w_lin, w_gate, flags):
    cols, keys, cz = pair.shape
    ch = w_lin.shape[1]
    out = jax.ShapeDtypeStruct((cols, keys, ch), F32)
    return pl.pallas_call(
        pair_forward_kernel,
        out_shape=(jax.ShapeDtypeStruct((cols, keys, ch), BF16), out, out),
        in_specs=[VMEM] * 4,
        out_specs=(VMEM, VMEM, VMEM),
        compiler_params=params(),
        cost_estimate=cost(4 * cols * keys * cz * ch, 14 * cols * keys * ch, cols * keys * ch),
        name="pair_forward",
    )(pair, w_lin, w_gate, flags)


def slab_forward_kernel(
    n_blocks,
    even_ref,
    odd_ref,
    w_lin_ref,
    w_gate_ref,
    slab_flags_ref,
    flags_ref,
    slab_ref,
    value_ref,
    lin_ref,
    gate_ref,
):
    _, keys, cz = even_ref.shape
    rows = 2 * even_ref.shape[0] // n_blocks
    row, col = lax.axis_index("row"), lax.axis_index("col")
    km = flags_ref[pl.ds(pl.multiple_of(row * keys, 16), keys)].astype(F32)
    flags = slab_flags_ref[...].astype(F32)
    for i in range(n_blocks * rows):
        value_ref[i] = km * flags[i : i + 1]
    for b in range(n_blocks):
        first = (col ^ b) * rows
        block = (odd_ref if b % 2 else even_ref)[(b // 2) * rows : (b // 2 + 1) * rows]
        linear, sigmoid = project(
            block.reshape(rows * keys, cz),
            w_lin_ref[...],
            w_gate_ref[...],
        )
        linear = linear.reshape(rows, keys, -1)
        sigmoid = sigmoid.reshape(rows, keys, -1)
        for r in range(rows):
            i = first + r
            masked = value_ref[i] * sigmoid[r]
            slab_ref[i] = block[r]
            value_ref[i] = (masked * linear[r]).astype(BF16).astype(F32)
            lin_ref[i] = masked
            gate_ref[i] = masked * linear[r] * (1.0 - sigmoid[r])


def slab_forward(blocks, n, w_lin, w_gate, slab_flags, flags):
    half, keys, cz = blocks[0].shape
    rows = 2 * half // n
    ch = w_lin.shape[1]
    out = jax.ShapeDtypeStruct((n * rows, keys, ch), F32)
    raw = jax.ShapeDtypeStruct((n * rows, keys, cz), BF16)
    return pl.pallas_call(
        functools.partial(slab_forward_kernel, n),
        out_shape=(raw, out, out, out),
        in_specs=[VMEM] * 6,
        out_specs=(VMEM,) * 4,
        compiler_params=params(),
        cost_estimate=cost(4 * n * rows * keys * cz * ch, 16 * n * rows * keys * ch),
        name="slab_forward",
    )(*blocks, w_lin, w_gate, slab_flags, flags)


def row_of(order, per, p):
    return (lax.axis_index("row") ^ order[p // per]) * per + p % per


def widen(grads, wide):
    at = 0
    for grad_ref in grads:
        wide[at : at + grad_ref.shape[0]] = grad_ref[...].astype(F32)
        at += grad_ref.shape[0]
    return at


def add_sums(wide, count, j0, keys, values, sums_ref):
    ch = wide.shape[2]
    for p in range(count):
        total = sums_ref[p]
        for j, value in enumerate(values):
            total = total + jnp.broadcast_to(wide[p, pl.ds(j0 + j, 1), :], (keys, ch)) * value
        sums_ref[p] = total


def add_totals(wide, rows, j0, slab_value_ref, totals):
    _, keys, ch = slab_value_ref.shape
    totals = list(totals)
    for p, i in enumerate(rows):
        mine = slab_value_ref[i]
        for j in range(len(totals)):
            g = jnp.broadcast_to(wide[p, pl.ds(j0 + j, 1), :], (keys, ch))
            totals[j] = totals[j] + g * mine
    return totals


def sums_kernel(n_grads, *refs):
    grads, (value_ref, sums_ref, wide) = refs[:n_grads], refs[n_grads:]
    cols, keys, ch = value_ref.shape
    count = widen(grads, wide)
    sums_ref[...] = jnp.zeros_like(sums_ref)

    def step(s, carry):
        j0 = pl.multiple_of(s * J_STEP, J_STEP)
        values = [value_ref[j0 + j].astype(F32) for j in range(J_STEP)]
        add_sums(wide, count, j0, keys, values, sums_ref)
        return carry

    lax.fori_loop(0, cols // J_STEP, step, 0, unroll=2)


def first_sums(grads, value):
    cols, keys, ch = value.shape
    rows = sum(g.shape[0] for g in grads)
    return pl.pallas_call(
        functools.partial(sums_kernel, len(grads)),
        out_shape=jax.ShapeDtypeStruct((rows, keys, ch), F32),
        in_specs=[VMEM] * (len(grads) + 1),
        out_specs=VMEM,
        scratch_shapes=[pltpu.VMEM((rows, cols, ch), F32)],
        compiler_params=params(),
        cost_estimate=cost(2 * rows * cols * keys * ch, 8 * cols * keys * ch),
        name="first_sums_over_j",
    )(*grads, value)


def totals_kernel(order, n_grads, *refs):
    grads, (slab_value_ref, total_ref, wide) = refs[:n_grads], refs[n_grads:]
    cols, keys, ch = total_ref.shape
    count = widen(grads, wide)
    per = slab_value_ref.shape[0] // len(order)
    rows = [row_of(order, per, p) for p in range(count)]

    def step(s, carry):
        j0 = pl.multiple_of(s * J_STEP, J_STEP)
        totals = [jnp.zeros((keys, ch), F32)] * J_STEP
        totals = add_totals(wide, rows, j0, slab_value_ref, totals)
        for j in range(J_STEP):
            total_ref[j0 + j] = totals[j]
        return carry

    lax.fori_loop(0, cols // J_STEP, step, 0, unroll=2)


def first_totals(order, grads, slab_value):
    _, keys, ch = slab_value.shape
    cols = grads[0].shape[1]
    rows = sum(g.shape[0] for g in grads)
    return pl.pallas_call(
        functools.partial(totals_kernel, order, len(grads)),
        out_shape=jax.ShapeDtypeStruct((cols, keys, ch), F32),
        in_specs=[VMEM] * (len(grads) + 1),
        out_specs=VMEM,
        scratch_shapes=[pltpu.VMEM((rows, cols, ch), F32)],
        compiler_params=params(),
        cost_estimate=cost(2 * rows * cols * keys * ch, 8 * cols * keys * ch),
        name="first_totals_over_i",
    )(*grads, slab_value)


def main_kernel(
    order,
    blocks,
    grad_ref,
    total_ref,
    first_sums_ref,
    pair_ref,
    value_ref,
    lin_ref,
    gate_ref,
    slab_ref,
    slab_value_ref,
    slab_lin_ref,
    slab_gate_ref,
    d_lin_ref,
    d_gate_ref,
    sum_keep_ref,
    sum_send_ref,
    w_keep_ref,
    w_send_ref,
    wide,
    sums_ref,
    slab_sum,
):
    cols, keys, cz = pair_ref.shape
    ch = value_ref.shape[2]
    slab_rows = slab_ref.shape[0]
    done = first_sums_ref.shape[0]
    per = slab_rows // len(order)
    col = lax.axis_index("col")
    count = widen([grad_ref], wide)
    sums_ref[...] = jnp.zeros_like(sums_ref)
    rows = [row_of(order, per, done + p) for p in range(count)]

    def weights(rows, d_lin, d_gate):
        both = jnp.concatenate([d_lin, d_gate], axis=1)
        return lax.dot_general(
            rows, both, (((0,), (0,)), ((), ())), preferred_element_type=F32
        )

    pair_w = jnp.zeros((cz, 2 * ch), F32)
    for first in range(0, cols, W_STEP):
        for j0 in range(first, first + W_STEP, J_STEP):
            values = [value_ref[j0 + j].astype(F32) for j in range(J_STEP)]
            add_sums(wide, count, j0, keys, values, sums_ref)
            totals = [total_ref[j0 + j] for j in range(J_STEP)]
            totals = add_totals(wide, rows, j0, slab_value_ref, totals)
            for j in range(J_STEP):
                d_lin_ref[j0 + j] = (totals[j] * lin_ref[j0 + j]).astype(BF16)
                d_gate_ref[j0 + j] = (totals[j] * gate_ref[j0 + j]).astype(BF16)
        some = slice(first, first + W_STEP)
        pair_w = pair_w + weights(
            pair_ref[some].reshape(W_STEP * keys, cz),
            d_lin_ref[some].reshape(W_STEP * keys, ch),
            d_gate_ref[some].reshape(W_STEP * keys, ch),
        )
    for p in range(done):
        slab_sum[row_of(order, per, p)] = first_sums_ref[p]
    for p in range(count):
        slab_sum[rows[p]] = sums_ref[p]

    sums = slab_sum[...]
    s_lin = (sums * slab_lin_ref[...]).astype(BF16).reshape(slab_rows * keys, ch)
    s_gate = (sums * slab_gate_ref[...]).astype(BF16).reshape(slab_rows * keys, ch)
    slab_w = weights(slab_ref[...].reshape(slab_rows * keys, cz), s_lin, s_gate)
    first = parity() == 0
    keep = jnp.where(first, slab_w, pair_w)
    send = jnp.where(first, pair_w, slab_w)
    for h in range(2):
        w_keep_ref[h] = keep[:, h * ch : (h + 1) * ch]
        w_send_ref[h] = send[:, h * ch : (h + 1) * ch]
    own = sum_keep_ref.shape[1]
    for n, b in enumerate(blocks):
        sum_keep_ref[n] = slab_sum[pl.ds((col ^ b) * own, own)]
        sum_send_ref[n] = slab_sum[pl.ds((col ^ b ^ 1) * own, own)]


def main_part(order, blocks, grads, first, pair, forward, slab):
    cols, keys, cz = pair.shape
    ch = forward[0].shape[2]
    slab_rows = slab[0].shape[0]
    own = slab_rows // (2 * len(blocks))
    d_type = jax.ShapeDtypeStruct((cols, keys, ch), BF16)
    s_type = jax.ShapeDtypeStruct((len(blocks), own, keys, ch), F32)
    w_type = jax.ShapeDtypeStruct((2, cz, ch), F32)
    return pl.pallas_call(
        functools.partial(main_kernel, order, blocks),
        out_shape=(d_type, d_type, s_type, s_type, w_type, w_type),
        in_specs=[VMEM] * 11,
        out_specs=(VMEM,) * 6,
        scratch_shapes=[
            pltpu.VMEM((grads.shape[0], cols, ch), F32),
            pltpu.VMEM((grads.shape[0], keys, ch), F32),
            pltpu.VMEM((slab_rows, keys, ch), F32),
        ],
        compiler_params=params(),
        cost_estimate=cost(8 * cols * keys * cz * ch, 16 * cols * keys * ch),
        name="last_rows",
    )(grads, *first, pair, *forward, *slab)


def pair_out_kernel(d_lin_ref, d_gate_ref, w_lin_ref, w_gate_ref, out_ref):
    rows, ch = d_lin_ref.shape
    weights = jnp.concatenate([w_lin_ref[...], w_gate_ref[...]], axis=1)
    step = rows

    def body(s, carry):
        at = pl.ds(pl.multiple_of(s * step, step), step)
        both = jnp.concatenate([d_lin_ref[at, :], d_gate_ref[at, :]], axis=1)
        out = lax.dot_general(
            both, weights, (((1,), (1,)), ((), ())), preferred_element_type=F32
        )
        out_ref[at, :] = out.astype(BF16)
        return carry

    lax.fori_loop(0, rows // step, body, 0)


def pair_out(d_lin, d_gate, w_lin, w_gate):
    cols, keys, ch = d_lin.shape
    cz = w_lin.shape[0]
    out = pl.pallas_call(
        pair_out_kernel,
        out_shape=jax.ShapeDtypeStruct((cols * keys, cz), BF16),
        in_specs=[VMEM] * 4,
        out_specs=VMEM,
        compiler_params=params(),
        cost_estimate=cost(4 * cols * keys * cz * ch, 6 * cols * keys * ch),
        name="pair_input_grad",
    )(d_lin.reshape(cols * keys, ch), d_gate.reshape(cols * keys, ch), w_lin, w_gate)
    return out.reshape(cols, keys, cz)


def fold_kernel(kept_ref, got_ref, sum_ref, moved_ref):
    half = sum_ref.shape[0]
    sum_ref[...] = kept_ref[:half] + got_ref[:half].astype(F32)
    moved_ref[...] = (kept_ref[half:] + got_ref[half:].astype(F32)).astype(BF16)


def fold(kept, got):
    half = (kept.shape[0] // 2,) + kept.shape[1:]
    return pl.pallas_call(
        fold_kernel,
        out_shape=(jax.ShapeDtypeStruct(half, F32), jax.ShapeDtypeStruct(half, BF16)),
        in_specs=[VMEM, VMEM],
        out_specs=(VMEM, VMEM),
        compiler_params=params(),
        cost_estimate=cost(STAGE_COST * kept.size, 8 * kept.size),
        name="fold",
    )(kept, got)


def add_pair(own, got):
    return (own.astype(F32) + got.astype(F32)).astype(BF16)


def four_kernel(a_ref, b_ref, c_ref, d_ref, out_ref):
    one = d_ref[...].astype(F32) + c_ref[...].astype(F32)
    two = b_ref[...].astype(F32) + a_ref[...].astype(F32)
    out_ref[...] = (one + two).astype(BF16)


def add_sums_of_four(*parts):
    return pl.pallas_call(
        four_kernel,
        out_shape=jax.ShapeDtypeStruct(parts[0].shape, BF16),
        in_specs=[VMEM] * 4,
        out_specs=VMEM,
        compiler_params=params(),
        cost_estimate=cost(4 * parts[0].size, 10 * parts[0].size),
        name="add_four",
    )(*parts)


def join_kernel(pair_bit, diagonal_ref, late_ref, pair_ref, own_ref, out_ref):
    upper = jnp.minimum(lax.axis_index("col") & pair_bit, 1)
    own = own_ref[...].astype(F32) + late_ref[...].astype(F32)
    other = pair_ref[...].astype(F32) + diagonal_ref[...].astype(F32)
    out_ref[upper] = own.astype(BF16)
    out_ref[1 - upper] = other.astype(BF16)


def join_sums(pair_bit, *parts):
    cz, ch = parts[0].shape
    return pl.pallas_call(
        functools.partial(join_kernel, pair_bit),
        out_shape=jax.ShapeDtypeStruct((2, cz, ch), BF16),
        in_specs=[VMEM] * 4,
        out_specs=VMEM,
        compiler_params=params(),
        cost_estimate=cost(4 * cz * ch, 12 * cz * ch),
        name="join_sums",
    )(*parts)


def slab_out_kernel(sum_ref, got_ref, lin_ref, gate_ref, w_lin_ref, w_gate_ref, out_ref):
    own, keys, ch = sum_ref.shape
    col = lax.axis_index("col")
    at = pl.ds(col * own, own)
    total = sum_ref[...] + got_ref[...].astype(F32)
    d_lin = (total * lin_ref[at]).astype(BF16).reshape(own * keys, ch)
    d_gate = (total * gate_ref[at]).astype(BF16).reshape(own * keys, ch)
    both = jnp.concatenate([d_lin, d_gate], axis=1)
    weights = jnp.concatenate([w_lin_ref[...], w_gate_ref[...]], axis=1)
    out = lax.dot_general(both, weights, (((1,), (1,)), ((), ())), preferred_element_type=F32)
    out_ref[...] = out.astype(BF16).reshape(own, keys, w_lin_ref.shape[0])


def slab_out(total, got, lin, gate, w_lin, w_gate):
    own, keys, ch = total.shape
    cz = w_lin.shape[0]
    return pl.pallas_call(
        slab_out_kernel,
        out_shape=jax.ShapeDtypeStruct((own, keys, cz), BF16),
        in_specs=[VMEM] * 6,
        out_specs=VMEM,
        compiler_params=params(),
        cost_estimate=cost(4 * own * keys * cz * ch, 16 * own * keys * ch),
        name="slab_input_grad",
    )(total, got, lin, gate, w_lin, w_gate)


def on_device(
    pair_slab, pair_full, grad_out, w_a_lin, w_a_gate, w_b_lin, w_b_gate, mask_slab, mask_residue
):
    n_row, n_col = lax.axis_size("row"), lax.axis_size("col")
    row_bits, col_bits = bits_of(n_row), bits_of(n_col)
    residues = mask_residue.shape[0]

    steps = [row_bits[-1]] + row_bits[1:-1] + row_bits[:1]
    ch = w_a_lin.shape[1]
    held, own_slab = stage(lead(), grad_out, pair_slab)
    order = [0]
    blocks = {0: own_slab}
    for bit in reversed(col_bits[1:]):
        for b in list(blocks):
            blocks[b ^ bit] = swap(blocks[b], "col", bit)
    got = swap(grad_out, "row", steps[0])
    for bit, later in zip(steps, steps[1:-1]):
        held = jnp.concatenate([held, got], axis=0)
        order = order + [r ^ bit for r in order]
        got = swap(held, "row", later)
    masks = lax.optimization_barrier(((mask_slab, mask_residue), held, blocks))[0]
    slab_flags, flags = (
        jnp.broadcast_to(m.astype(BF16)[:, None], m.shape + (ch,)) for m in masks
    )
    value, lin, gate = pair_forward(pair_full, w_b_lin, w_b_gate, flags)
    got_last = swap(held, "row", steps[-1])
    got, value = lax.optimization_barrier((got, value))
    got_both = swap(got, "row", steps[-1])
    for bit in steps[-2:]:
        order = order + [r ^ bit for r in order]
    slabs = jnp.concatenate([blocks[b] for b in sorted(blocks)], axis=0)
    slabs = [slabs, swap(slabs, "col", 1)]
    slab = slab_forward(slabs, n_col, w_a_lin, w_a_gate, slab_flags, flags)
    pieces = [held, got, got_last]
    first = (first_totals(order, pieces, slab[1]), first_sums(pieces, value))
    kept = [0]
    for bit in reversed(col_bits[1:]):
        kept = kept + [b ^ bit for b in kept]
    d_lin, d_gate, sum_keep, sum_send, w_keep, w_send = main_part(
        order, kept, got_both, first, pair_full, (value, lin, gate), slab
    )
    pair_bit, col = col_bits[1], lax.axis_index("col")
    got_w = swap(w_send, "col", 1)
    sum_send, _ = lax.optimization_barrier((sum_send, got_w))
    side = w_keep + got_w
    upper = (col & pair_bit) != 0
    moved = jnp.where(upper, side[0], side[1]).astype(BF16)
    narrow = jnp.where(upper, side[1], side[0]).astype(BF16)
    moved, d_lin, d_gate = lax.optimization_barrier((moved, d_lin, d_gate))
    grad_pair = pair_out(d_lin, d_gate, w_b_lin, w_b_gate)
    sums, got = sum_keep, swap(sum_send, "col", 1)
    bits = [bit * n_col for bit in row_bits]
    near, late = bits[0], bits[1]
    diagonal = swap_chips(moved, pair_bit | near, 0)
    pair_part, near_part = swap_chips(moved, pair_bit), swap_chips(narrow, near)
    narrow = add_sums_of_four(diagonal, near_part, pair_part, narrow)
    between = col_bits[2:] + [bit for bit in bits if bit not in (near, late)]
    for bit in between:
        if bit == between[-1]:
            narrow, got, grad_pair = lax.optimization_barrier((narrow, got, grad_pair))
            for far in col_bits[1:]:
                sums, moved = fold(sums, got)
                got = swap(moved, "col", far)
        narrow = add_pair(narrow, swap_chips(narrow, bit))
    diagonal = swap_chips(narrow, pair_bit | late, 0)
    late_part, pair_part = swap_chips(narrow, late), swap_chips(narrow, pair_bit)
    mine = join_sums(pair_bit, diagonal, late_part, pair_part, narrow)
    both = [m.astype(F32) / residues for m in (mine, swap(mine, "col", 1))]
    first = parity() == 0
    grad_weights = jnp.where(
        first, jnp.concatenate(both, axis=0), jnp.concatenate(both[::-1], axis=0)
    )
    grad_slab = slab_out(sums[0], got[0], slab[2], slab[3], w_a_lin, w_a_gate)
    return (grad_slab, grad_pair, grad_weights)


def solution(mesh):
    return jax.shard_map(
        on_device,
        mesh=mesh,
        in_specs=(
            P("col", "row", None),
            P("col", "row", None),
            P("row", "col", None),
            P(),
            P(),
            P(),
            P(),
            P(),
            P(),
        ),
        out_specs=(P("col", "row", None), P("col", "row", None), P()),
        check_vma=False,
    )
```

```python
import functools

import jax
import jax.numpy as jnp
from jax import lax
from jax.experimental import pallas as pl
from jax.experimental.pallas import tpu as pltpu
from jax.sharding import PartitionSpec as P

F32 = jnp.float32
BF16 = jnp.bfloat16
VMEM = pl.BlockSpec(memory_space=pltpu.VMEM)
WHOLE = pl.BlockSpec()
SMEM = pl.BlockSpec(memory_space=pltpu.SMEM)
J_STEP = 4
FORWARD_STEP = 64
W_STEP = 16
STAGE_COST = 400000


def bits_of(size):
    return [1 << b for b in range(size.bit_length() - 1)]


def swap(value, axis, bit):
    size = lax.axis_size(axis)
    return lax.ppermute(value, axis, [(d, d ^ bit) for d in range(size)])


def swap_chips(value, bit, flip=1):
    n_row, n_col = lax.axis_size("row"), lax.axis_size("col")
    pairs = [(d, d ^ bit ^ flip) for d in range(n_row * n_col)]
    return lax.ppermute(value, ("row", "col"), pairs)


def parity():
    number = lax.axis_index("row") ^ lax.axis_index("col")
    for shift in (16, 8, 4, 2, 1):
        number = number ^ (number >> shift)
    return number & 1


def params(mib=32):
    return pltpu.CompilerParams(vmem_limit_bytes=mib * 1024 * 1024)


def cost(flops, bytes_accessed, transcendentals=0):
    return pl.CostEstimate(
        flops=flops, bytes_accessed=bytes_accessed, transcendentals=transcendentals
    )


def project(rows, w_lin, w_gate):
    both = jnp.dot(
        rows, jnp.concatenate([w_lin, w_gate], axis=1), preferred_element_type=F32
    )
    ch = w_lin.shape[1]
    linear = both[:, :ch]
    sigmoid = 1.0 / (1.0 + jnp.exp(-both[:, ch:]))
    return linear, sigmoid


def lead_kernel(out_ref):
    out_ref[...] = jnp.zeros_like(out_ref)


def lead():
    return pl.pallas_call(
        lead_kernel,
        out_shape=jax.ShapeDtypeStruct((8, 128), F32),
        out_specs=VMEM,
        compiler_params=params(),
        cost_estimate=cost(STAGE_COST * 8192, 4096),
        name="lead",
    )()


def stage_kernel(n, _, *refs):
    for source_ref, copy_ref in zip(refs[:n], refs[n:]):
        copy_ref[...] = source_ref[...]


def stage(after, *sources):
    n = len(sources)
    return pl.pallas_call(
        functools.partial(stage_kernel, n),
        out_shape=tuple(jax.ShapeDtypeStruct(s.shape, s.dtype) for s in sources),
        in_specs=[VMEM] * (n + 1),
        out_specs=(VMEM,) * n,
        compiler_params=params(),
        cost_estimate=cost(STAGE_COST * sources[0].size, 4 * sources[0].size),
        name="stage",
    )(after, *sources)


def pair_forward_kernel(pair_ref, w_lin_ref, w_gate_ref, flags_ref, value_ref, lin_ref, gate_ref):
    cols, keys, cz = pair_ref.shape
    row, col = lax.axis_index("row"), lax.axis_index("col")
    km = flags_ref[pl.ds(pl.multiple_of(row * keys, 16), keys)].astype(F32)
    step = min(cols, FORWARD_STEP)

    def body(s, carry):
        j0 = pl.multiple_of(s * step, step)
        rows = pair_ref[pl.ds(j0, step)].reshape(step * keys, cz)
        linear, sigmoid = project(rows, w_lin_ref[...], w_gate_ref[...])
        linear = linear.reshape(step, keys, -1)
        sigmoid = sigmoid.reshape(step, keys, -1)
        flags = flags_ref[pl.ds(pl.multiple_of(col * cols + j0, step), step)].astype(F32)
        for j in range(step):
            m = km * flags[j : j + 1]
            masked = m * sigmoid[j]
            lin = linear[j]
            value_ref[j0 + j] = (masked * lin).astype(BF16)
            lin_ref[j0 + j] = masked
            gate_ref[j0 + j] = masked * lin * (1.0 - sigmoid[j])
        return carry

    lax.fori_loop(0, cols // step, body, 0)


def pair_forward(pair, w_lin, w_gate, flags):
    cols, keys, cz = pair.shape
    ch = w_lin.shape[1]
    out = jax.ShapeDtypeStruct((cols, keys, ch), F32)
    return pl.pallas_call(
        pair_forward_kernel,
        out_shape=(jax.ShapeDtypeStruct((cols, keys, ch), BF16), out, out),
        in_specs=[VMEM] * 4,
        out_specs=(VMEM, VMEM, VMEM),
        compiler_params=params(),
        cost_estimate=cost(4 * cols * keys * cz * ch, 14 * cols * keys * ch, cols * keys * ch),
        name="pair_forward",
    )(pair, w_lin, w_gate, flags)


def slab_forward_kernel(
    n_blocks,
    even_ref,
    odd_ref,
    w_lin_ref,
    w_gate_ref,
    slab_flags_ref,
    flags_ref,
    slab_ref,
    value_ref,
    lin_ref,
    gate_ref,
):
    _, keys, cz = even_ref.shape
    rows = 2 * even_ref.shape[0] // n_blocks
    row, col = lax.axis_index("row"), lax.axis_index("col")
    km = flags_ref[pl.ds(pl.multiple_of(row * keys, 16), keys)].astype(F32)
    flags = slab_flags_ref[...].astype(F32)
    for i in range(n_blocks * rows):
        value_ref[i] = km * flags[i : i + 1]
    for b in range(n_blocks):
        first = (col ^ b) * rows
        block = (odd_ref if b % 2 else even_ref)[(b // 2) * rows : (b // 2 + 1) * rows]
        linear, sigmoid = project(
            block.reshape(rows * keys, cz),
            w_lin_ref[...],
            w_gate_ref[...],
        )
        linear = linear.reshape(rows, keys, -1)
        sigmoid = sigmoid.reshape(rows, keys, -1)
        for r in range(rows):
            i = first + r
            masked = value_ref[i] * sigmoid[r]
            slab_ref[i] = block[r]
            value_ref[i] = (masked * linear[r]).astype(BF16).astype(F32)
            lin_ref[i] = masked
            gate_ref[i] = masked * linear[r] * (1.0 - sigmoid[r])


def slab_forward(blocks, n, w_lin, w_gate, slab_flags, flags):
    half, keys, cz = blocks[0].shape
    rows = 2 * half // n
    ch = w_lin.shape[1]
    out = jax.ShapeDtypeStruct((n * rows, keys, ch), F32)
    raw = jax.ShapeDtypeStruct((n * rows, keys, cz), BF16)
    return pl.pallas_call(
        functools.partial(slab_forward_kernel, n),
        out_shape=(raw, out, out, out),
        in_specs=[VMEM] * 6,
        out_specs=(VMEM,) * 4,
        compiler_params=params(),
        cost_estimate=cost(4 * n * rows * keys * cz * ch, 16 * n * rows * keys * ch),
        name="slab_forward",
    )(*blocks, w_lin, w_gate, slab_flags, flags)


def row_of(order, per, p):
    return (lax.axis_index("row") ^ order[p // per]) * per + p % per


def widen(grads, wide):
    at = 0
    for grad_ref in grads:
        wide[at : at + grad_ref.shape[0]] = grad_ref[...].astype(F32)
        at += grad_ref.shape[0]
    return at


def add_sums(wide, count, j0, keys, values, sums_ref):
    ch = wide.shape[2]
    for p in range(count):
        total = sums_ref[p]
        for j, value in enumerate(values):
            total = total + jnp.broadcast_to(wide[p, pl.ds(j0 + j, 1), :], (keys, ch)) * value
        sums_ref[p] = total


def add_totals(wide, rows, j0, slab_value_ref, totals):
    _, keys, ch = slab_value_ref.shape
    totals = list(totals)
    for p, i in enumerate(rows):
        mine = slab_value_ref[i]
        for j in range(len(totals)):
            g = jnp.broadcast_to(wide[p, pl.ds(j0 + j, 1), :], (keys, ch))
            totals[j] = totals[j] + g * mine
    return totals


def sums_kernel(n_grads, *refs):
    grads, (value_ref, sums_ref, wide) = refs[:n_grads], refs[n_grads:]
    cols, keys, ch = value_ref.shape
    count = widen(grads, wide)
    sums_ref[...] = jnp.zeros_like(sums_ref)

    def step(s, carry):
        j0 = pl.multiple_of(s * J_STEP, J_STEP)
        values = [value_ref[j0 + j].astype(F32) for j in range(J_STEP)]
        add_sums(wide, count, j0, keys, values, sums_ref)
        return carry

    lax.fori_loop(0, cols // J_STEP, step, 0, unroll=2)


def first_sums(grads, value):
    cols, keys, ch = value.shape
    rows = sum(g.shape[0] for g in grads)
    return pl.pallas_call(
        functools.partial(sums_kernel, len(grads)),
        out_shape=jax.ShapeDtypeStruct((rows, keys, ch), F32),
        in_specs=[VMEM] * (len(grads) + 1),
        out_specs=VMEM,
        scratch_shapes=[pltpu.VMEM((rows, cols, ch), F32)],
        compiler_params=params(),
        cost_estimate=cost(2 * rows * cols * keys * ch, 8 * cols * keys * ch),
        name="first_sums_over_j",
    )(*grads, value)


def totals_kernel(order, n_grads, *refs):
    grads, (slab_value_ref, total_ref, wide) = refs[:n_grads], refs[n_grads:]
    cols, keys, ch = total_ref.shape
    count = widen(grads, wide)
    per = slab_value_ref.shape[0] // len(order)
    rows = [row_of(order, per, p) for p in range(count)]

    def step(s, carry):
        j0 = pl.multiple_of(s * J_STEP, J_STEP)
        totals = [jnp.zeros((keys, ch), F32)] * J_STEP
        totals = add_totals(wide, rows, j0, slab_value_ref, totals)
        for j in range(J_STEP):
            total_ref[j0 + j] = totals[j]
        return carry

    lax.fori_loop(0, cols // J_STEP, step, 0, unroll=2)


def first_totals(order, grads, slab_value):
    _, keys, ch = slab_value.shape
    cols = grads[0].shape[1]
    rows = sum(g.shape[0] for g in grads)
    return pl.pallas_call(
        functools.partial(totals_kernel, order, len(grads)),
        out_shape=jax.ShapeDtypeStruct((cols, keys, ch), F32),
        in_specs=[VMEM] * (len(grads) + 1),
        out_specs=VMEM,
        scratch_shapes=[pltpu.VMEM((rows, cols, ch), F32)],
        compiler_params=params(),
        cost_estimate=cost(2 * rows * cols * keys * ch, 8 * cols * keys * ch),
        name="first_totals_over_i",
    )(*grads, slab_value)


def main_kernel(
    order,
    blocks,
    grad_ref,
    total_ref,
    first_sums_ref,
    pair_ref,
    value_ref,
    lin_ref,
    gate_ref,
    slab_ref,
    slab_value_ref,
    slab_lin_ref,
    slab_gate_ref,
    d_lin_ref,
    d_gate_ref,
    sum_keep_ref,
    sum_send_ref,
    w_keep_ref,
    w_send_ref,
    wide,
    sums_ref,
    slab_sum,
):
    cols, keys, cz = pair_ref.shape
    ch = value_ref.shape[2]
    slab_rows = slab_ref.shape[0]
    done = first_sums_ref.shape[0]
    per = slab_rows // len(order)
    col = lax.axis_index("col")
    count = widen([grad_ref], wide)
    sums_ref[...] = jnp.zeros_like(sums_ref)
    rows = [row_of(order, per, done + p) for p in range(count)]

    def weights(rows, d_lin, d_gate):
        both = jnp.concatenate([d_lin, d_gate], axis=1)
        return lax.dot_general(
            rows, both, (((0,), (0,)), ((), ())), preferred_element_type=F32
        )

    pair_w = jnp.zeros((cz, 2 * ch), F32)
    for first in range(0, cols, W_STEP):
        for j0 in range(first, first + W_STEP, J_STEP):
            values = [value_ref[j0 + j].astype(F32) for j in range(J_STEP)]
            add_sums(wide, count, j0, keys, values, sums_ref)
            totals = [total_ref[j0 + j] for j in range(J_STEP)]
            totals = add_totals(wide, rows, j0, slab_value_ref, totals)
            for j in range(J_STEP):
                d_lin_ref[j0 + j] = (totals[j] * lin_ref[j0 + j]).astype(BF16)
                d_gate_ref[j0 + j] = (totals[j] * gate_ref[j0 + j]).astype(BF16)
        some = slice(first, first + W_STEP)
        pair_w = pair_w + weights(
            pair_ref[some].reshape(W_STEP * keys, cz),
            d_lin_ref[some].reshape(W_STEP * keys, ch),
            d_gate_ref[some].reshape(W_STEP * keys, ch),
        )
    for p in range(done):
        slab_sum[row_of(order, per, p)] = first_sums_ref[p]
    for p in range(count):
        slab_sum[rows[p]] = sums_ref[p]

    sums = slab_sum[...]
    s_lin = (sums * slab_lin_ref[...]).astype(BF16).reshape(slab_rows * keys, ch)
    s_gate = (sums * slab_gate_ref[...]).astype(BF16).reshape(slab_rows * keys, ch)
    slab_w = weights(slab_ref[...].reshape(slab_rows * keys, cz), s_lin, s_gate)
    first = parity() == 0
    keep = jnp.where(first, slab_w, pair_w)
    send = jnp.where(first, pair_w, slab_w)
    for h in range(2):
        w_keep_ref[h] = keep[:, h * ch : (h + 1) * ch]
        w_send_ref[h] = send[:, h * ch : (h + 1) * ch]
    own = sum_keep_ref.shape[1]
    for n, b in enumerate(blocks):
        sum_keep_ref[n] = slab_sum[pl.ds((col ^ b) * own, own)]
        sum_send_ref[n] = slab_sum[pl.ds((col ^ b ^ 1) * own, own)]


def main_part(order, blocks, grads, first, pair, forward, slab):
    cols, keys, cz = pair.shape
    ch = forward[0].shape[2]
    slab_rows = slab[0].shape[0]
    own = slab_rows // (2 * len(blocks))
    d_type = jax.ShapeDtypeStruct((cols, keys, ch), BF16)
    s_type = jax.ShapeDtypeStruct((len(blocks), own, keys, ch), F32)
    w_type = jax.ShapeDtypeStruct((2, cz, ch), F32)
    return pl.pallas_call(
        functools.partial(main_kernel, order, blocks),
        out_shape=(d_type, d_type, s_type, s_type, w_type, w_type),
        in_specs=[VMEM] * 11,
        out_specs=(VMEM,) * 6,
        scratch_shapes=[
            pltpu.VMEM((grads.shape[0], cols, ch), F32),
            pltpu.VMEM((grads.shape[0], keys, ch), F32),
            pltpu.VMEM((slab_rows, keys, ch), F32),
        ],
        compiler_params=params(),
        cost_estimate=cost(8 * cols * keys * cz * ch, 16 * cols * keys * ch),
        name="last_rows",
    )(grads, *first, pair, *forward, *slab)


def pair_out_kernel(d_lin_ref, d_gate_ref, w_lin_ref, w_gate_ref, out_ref):
    rows, ch = d_lin_ref.shape
    weights = jnp.concatenate([w_lin_ref[...], w_gate_ref[...]], axis=1)
    step = rows

    def body(s, carry):
        at = pl.ds(pl.multiple_of(s * step, step), step)
        both = jnp.concatenate([d_lin_ref[at, :], d_gate_ref[at, :]], axis=1)
        out = lax.dot_general(
            both, weights, (((1,), (1,)), ((), ())), preferred_element_type=F32
        )
        out_ref[at, :] = out.astype(BF16)
        return carry

    lax.fori_loop(0, rows // step, body, 0)


def pair_out(d_lin, d_gate, w_lin, w_gate):
    cols, keys, ch = d_lin.shape
    cz = w_lin.shape[0]
    out = pl.pallas_call(
        pair_out_kernel,
        out_shape=jax.ShapeDtypeStruct((cols * keys, cz), BF16),
        in_specs=[VMEM] * 4,
        out_specs=VMEM,
        compiler_params=params(),
        cost_estimate=cost(4 * cols * keys * cz * ch, 6 * cols * keys * ch),
        name="pair_input_grad",
    )(d_lin.reshape(cols * keys, ch), d_gate.reshape(cols * keys, ch), w_lin, w_gate)
    return out.reshape(cols, keys, cz)


def fold_kernel(kept_ref, got_ref, sum_ref, moved_ref):
    half = sum_ref.shape[0]
    sum_ref[...] = kept_ref[:half] + got_ref[:half].astype(F32)
    moved_ref[...] = (kept_ref[half:] + got_ref[half:].astype(F32)).astype(BF16)


def fold(kept, got):
    half = (kept.shape[0] // 2,) + kept.shape[1:]
    return pl.pallas_call(
        fold_kernel,
        out_shape=(jax.ShapeDtypeStruct(half, F32), jax.ShapeDtypeStruct(half, BF16)),
        in_specs=[VMEM, VMEM],
        out_specs=(VMEM, VMEM),
        compiler_params=params(),
        cost_estimate=cost(STAGE_COST * kept.size, 8 * kept.size),
        name="fold",
    )(kept, got)


def add_pair(own, got):
    return (own.astype(F32) + got.astype(F32)).astype(BF16)


def four_kernel(a_ref, b_ref, c_ref, d_ref, out_ref):
    one = d_ref[...].astype(F32) + c_ref[...].astype(F32)
    two = b_ref[...].astype(F32) + a_ref[...].astype(F32)
    out_ref[...] = (one + two).astype(BF16)


def add_sums_of_four(*parts):
    return pl.pallas_call(
        four_kernel,
        out_shape=jax.ShapeDtypeStruct(parts[0].shape, BF16),
        in_specs=[VMEM] * 4,
        out_specs=VMEM,
        compiler_params=params(),
        cost_estimate=cost(4 * parts[0].size, 10 * parts[0].size),
        name="add_four",
    )(*parts)


def join_kernel(pair_bit, diagonal_ref, late_ref, pair_ref, own_ref, out_ref):
    upper = jnp.minimum(lax.axis_index("col") & pair_bit, 1)
    own = own_ref[...].astype(F32) + late_ref[...].astype(F32)
    other = pair_ref[...].astype(F32) + diagonal_ref[...].astype(F32)
    out_ref[upper] = own.astype(BF16)
    out_ref[1 - upper] = other.astype(BF16)


def join_sums(pair_bit, *parts):
    cz, ch = parts[0].shape
    return pl.pallas_call(
        functools.partial(join_kernel, pair_bit),
        out_shape=jax.ShapeDtypeStruct((2, cz, ch), BF16),
        in_specs=[VMEM] * 4,
        out_specs=VMEM,
        compiler_params=params(),
        cost_estimate=cost(4 * cz * ch, 12 * cz * ch),
        name="join_sums",
    )(*parts)


def slab_out_kernel(sum_ref, got_ref, lin_ref, gate_ref, w_lin_ref, w_gate_ref, out_ref):
    own, keys, ch = sum_ref.shape
    col = lax.axis_index("col")
    at = pl.ds(col * own, own)
    total = sum_ref[...] + got_ref[...].astype(F32)
    d_lin = (total * lin_ref[at]).astype(BF16).reshape(own * keys, ch)
    d_gate = (total * gate_ref[at]).astype(BF16).reshape(own * keys, ch)
    both = jnp.concatenate([d_lin, d_gate], axis=1)
    weights = jnp.concatenate([w_lin_ref[...], w_gate_ref[...]], axis=1)
    out = lax.dot_general(both, weights, (((1,), (1,)), ((), ())), preferred_element_type=F32)
    out_ref[...] = out.astype(BF16).reshape(own, keys, w_lin_ref.shape[0])


def slab_out(total, got, lin, gate, w_lin, w_gate):
    own, keys, ch = total.shape
    cz = w_lin.shape[0]
    return pl.pallas_call(
        slab_out_kernel,
        out_shape=jax.ShapeDtypeStruct((own, keys, cz), BF16),
        in_specs=[VMEM] * 6,
        out_specs=VMEM,
        compiler_params=params(),
        cost_estimate=cost(4 * own * keys * cz * ch, 16 * own * keys * ch),
        name="slab_input_grad",
    )(total, got, lin, gate, w_lin, w_gate)


def on_device(
    pair_slab, pair_full, grad_out, w_a_lin, w_a_gate, w_b_lin, w_b_gate, mask_slab, mask_residue
):
    n_row, n_col = lax.axis_size("row"), lax.axis_size("col")
    row_bits, col_bits = bits_of(n_row), bits_of(n_col)
    residues = mask_residue.shape[0]

    steps = [row_bits[-1]] + row_bits[1:-1] + row_bits[:1]
    ch = w_a_lin.shape[1]
    held, own_slab, *staged = stage(lead(), grad_out, pair_slab, w_a_lin, w_a_gate, w_b_lin, w_b_gate)
    order = [0]
    blocks = {0: own_slab}
    for bit in reversed(col_bits[1:]):
        for b in list(blocks):
            blocks[b ^ bit] = swap(blocks[b], "col", bit)
    got = swap(grad_out, "row", steps[0])
    for bit, later in zip(steps, steps[1:-1]):
        held = jnp.concatenate([held, got], axis=0)
        order = order + [r ^ bit for r in order]
        got = swap(held, "row", later)
    masks = lax.optimization_barrier(((mask_slab, mask_residue), held, blocks))[0]
    slab_flags, flags = (
        jnp.broadcast_to(m.astype(BF16)[:, None], m.shape + (ch,)) for m in masks
    )
    value, lin, gate = pair_forward(pair_full, *staged[2:], flags)
    got_last = swap(held, "row", steps[-1])
    got, value = lax.optimization_barrier((got, value))
    got_both = swap(got, "row", steps[-1])
    for bit in steps[-2:]:
        order = order + [r ^ bit for r in order]
    slabs = jnp.concatenate([blocks[b] for b in sorted(blocks)], axis=0)
    slabs = [slabs, swap(slabs, "col", 1)]
    slab = slab_forward(slabs, n_col, *staged[:2], slab_flags, flags)
    pieces = [held, got, got_last]
    first = (first_totals(order, pieces, slab[1]), first_sums(pieces, value))
    kept = [0]
    for bit in reversed(col_bits[1:]):
        kept = kept + [b ^ bit for b in kept]
    d_lin, d_gate, sum_keep, sum_send, w_keep, w_send = main_part(
        order, kept, got_both, first, pair_full, (value, lin, gate), slab
    )
    pair_bit, col = col_bits[1], lax.axis_index("col")
    got_w = swap(w_send, "col", 1)
    sum_send, _ = lax.optimization_barrier((sum_send, got_w))
    side = w_keep + got_w
    upper = (col & pair_bit) != 0
    moved = jnp.where(upper, side[0], side[1]).astype(BF16)
    narrow = jnp.where(upper, side[1], side[0]).astype(BF16)
    moved, d_lin, d_gate = lax.optimization_barrier((moved, d_lin, d_gate))
    grad_pair = pair_out(d_lin, d_gate, w_b_lin, w_b_gate)
    sums, got = sum_keep, swap(sum_send, "col", 1)
    bits = [bit * n_col for bit in row_bits]
    near, late = bits[0], bits[1]
    diagonal = swap_chips(moved, pair_bit | near, 0)
    pair_part, near_part = swap_chips(moved, pair_bit), swap_chips(narrow, near)
    narrow = add_sums_of_four(diagonal, near_part, pair_part, narrow)
    between = col_bits[2:] + [bit for bit in bits if bit not in (near, late)]
    for bit in between:
        if bit == between[-1]:
            narrow, got, grad_pair = lax.optimization_barrier((narrow, got, grad_pair))
            for far in col_bits[1:]:
                sums, moved = fold(sums, got)
                got = swap(moved, "col", far)
        narrow = add_pair(narrow, swap_chips(narrow, bit))
    diagonal = swap_chips(narrow, pair_bit | late, 0)
    late_part, pair_part = swap_chips(narrow, late), swap_chips(narrow, pair_bit)
    mine = join_sums(pair_bit, diagonal, late_part, pair_part, narrow)
    both = [m.astype(F32) / residues for m in (mine, swap(mine, "col", 1))]
    first = parity() == 0
    grad_weights = jnp.where(
        first, jnp.concatenate(both, axis=0), jnp.concatenate(both[::-1], axis=0)
    )
    grad_slab = slab_out(sums[0], got[0], slab[2], slab[3], w_a_lin, w_a_gate)
    return (grad_slab, grad_pair, grad_weights)


def solution(mesh):
    return jax.shard_map(
        on_device,
        mesh=mesh,
        in_specs=(
            P("col", "row", None),
            P("col", "row", None),
            P("row", "col", None),
            P(),
            P(),
            P(),
            P(),
            P(),
            P(),
        ),
        out_specs=(P("col", "row", None), P("col", "row", None), P()),
        check_vma=False,
    )
```

```python
import functools

import jax
import jax.numpy as jnp
from jax import lax
from jax.experimental import pallas as pl
from jax.experimental.pallas import tpu as pltpu
from jax.sharding import PartitionSpec as P

F32 = jnp.float32
BF16 = jnp.bfloat16
VMEM = pl.BlockSpec(memory_space=pltpu.VMEM)
WHOLE = pl.BlockSpec()
SMEM = pl.BlockSpec(memory_space=pltpu.SMEM)
J_STEP = 4
FORWARD_STEP = 64
W_STEP = 16
STAGE_COST = 400000


def bits_of(size):
    return [1 << b for b in range(size.bit_length() - 1)]


def swap(value, axis, bit):
    size = lax.axis_size(axis)
    return lax.ppermute(value, axis, [(d, d ^ bit) for d in range(size)])


def swap_chips(value, bit, flip=1):
    n_row, n_col = lax.axis_size("row"), lax.axis_size("col")
    pairs = [(d, d ^ bit ^ flip) for d in range(n_row * n_col)]
    return lax.ppermute(value, ("row", "col"), pairs)


def parity():
    number = lax.axis_index("row") ^ lax.axis_index("col")
    for shift in (16, 8, 4, 2, 1):
        number = number ^ (number >> shift)
    return number & 1


def params(mib=32):
    return pltpu.CompilerParams(vmem_limit_bytes=mib * 1024 * 1024)


def cost(flops, bytes_accessed, transcendentals=0):
    return pl.CostEstimate(
        flops=flops, bytes_accessed=bytes_accessed, transcendentals=transcendentals
    )


def project(rows, w_lin, w_gate):
    both = jnp.dot(
        rows, jnp.concatenate([w_lin, w_gate], axis=1), preferred_element_type=F32
    )
    ch = w_lin.shape[1]
    linear = both[:, :ch]
    sigmoid = 1.0 / (1.0 + jnp.exp(-both[:, ch:]))
    return linear, sigmoid


def lead_kernel(out_ref):
    out_ref[...] = jnp.zeros_like(out_ref)


def lead():
    return pl.pallas_call(
        lead_kernel,
        out_shape=jax.ShapeDtypeStruct((8, 128), F32),
        out_specs=VMEM,
        compiler_params=params(),
        cost_estimate=cost(STAGE_COST * 8192, 4096),
        name="lead",
    )()


def stage_kernel(n, _, *refs):
    for source_ref, copy_ref in zip(refs[:n], refs[n:]):
        copy_ref[...] = source_ref[...]


def stage(after, *sources):
    n = len(sources)
    return pl.pallas_call(
        functools.partial(stage_kernel, n),
        out_shape=tuple(jax.ShapeDtypeStruct(s.shape, s.dtype) for s in sources),
        in_specs=[VMEM] * (n + 1),
        out_specs=(VMEM,) * n,
        compiler_params=params(),
        cost_estimate=cost(STAGE_COST * sources[0].size, 4 * sources[0].size),
        name="stage",
    )(after, *sources)


def pair_forward_kernel(pair_ref, w_lin_ref, w_gate_ref, flags_ref, value_ref, lin_ref, gate_ref):
    cols, keys, cz = pair_ref.shape
    row, col = lax.axis_index("row"), lax.axis_index("col")
    km = flags_ref[pl.ds(pl.multiple_of(row * keys, 16), keys)].astype(F32)
    step = min(cols, FORWARD_STEP)

    def body(s, carry):
        j0 = pl.multiple_of(s * step, step)
        rows = pair_ref[pl.ds(j0, step)].reshape(step * keys, cz)
        linear, sigmoid = project(rows, w_lin_ref[...], w_gate_ref[...])
        linear = linear.reshape(step, keys, -1)
        sigmoid = sigmoid.reshape(step, keys, -1)
        flags = flags_ref[pl.ds(pl.multiple_of(col * cols + j0, step), step)].astype(F32)
        for j in range(step):
            m = km * flags[j : j + 1]
            masked = m * sigmoid[j]
            lin = linear[j]
            value_ref[j0 + j] = (masked * lin).astype(BF16)
            lin_ref[j0 + j] = masked
            gate_ref[j0 + j] = masked * lin * (1.0 - sigmoid[j])
        return carry

    lax.fori_loop(0, cols // step, body, 0)


def pair_forward(pair, w_lin, w_gate, flags):
    cols, keys, cz = pair.shape
    ch = w_lin.shape[1]
    out = jax.ShapeDtypeStruct((cols, keys, ch), F32)
    return pl.pallas_call(
        pair_forward_kernel,
        out_shape=(jax.ShapeDtypeStruct((cols, keys, ch), BF16), out, out),
        in_specs=[VMEM] * 4,
        out_specs=(VMEM, VMEM, VMEM),
        compiler_params=params(),
        cost_estimate=cost(4 * cols * keys * cz * ch, 14 * cols * keys * ch, cols * keys * ch),
        name="pair_forward",
    )(pair, w_lin, w_gate, flags)


def slab_forward_kernel(
    n_blocks,
    even_ref,
    odd_ref,
    w_lin_ref,
    w_gate_ref,
    slab_flags_ref,
    flags_ref,
    slab_ref,
    value_ref,
    lin_ref,
    gate_ref,
):
    _, keys, cz = even_ref.shape
    rows = 2 * even_ref.shape[0] // n_blocks
    row, col = lax.axis_index("row"), lax.axis_index("col")
    km = flags_ref[pl.ds(pl.multiple_of(row * keys, 16), keys)].astype(F32)
    flags = slab_flags_ref[...].astype(F32)
    for i in range(n_blocks * rows):
        value_ref[i] = km * flags[i : i + 1]
    for b in range(n_blocks):
        first = (col ^ b) * rows
        block = (odd_ref if b % 2 else even_ref)[(b // 2) * rows : (b // 2 + 1) * rows]
        linear, sigmoid = project(
            block.reshape(rows * keys, cz),
            w_lin_ref[...],
            w_gate_ref[...],
        )
        linear = linear.reshape(rows, keys, -1)
        sigmoid = sigmoid.reshape(rows, keys, -1)
        for r in range(rows):
            i = first + r
            masked = value_ref[i] * sigmoid[r]
            slab_ref[i] = block[r]
            value_ref[i] = (masked * linear[r]).astype(BF16).astype(F32)
            lin_ref[i] = masked
            gate_ref[i] = masked * linear[r] * (1.0 - sigmoid[r])


def slab_forward(blocks, n, w_lin, w_gate, slab_flags, flags):
    half, keys, cz = blocks[0].shape
    rows = 2 * half // n
    ch = w_lin.shape[1]
    out = jax.ShapeDtypeStruct((n * rows, keys, ch), F32)
    raw = jax.ShapeDtypeStruct((n * rows, keys, cz), BF16)
    return pl.pallas_call(
        functools.partial(slab_forward_kernel, n),
        out_shape=(raw, out, out, out),
        in_specs=[VMEM] * 6,
        out_specs=(VMEM,) * 4,
        compiler_params=params(),
        cost_estimate=cost(4 * n * rows * keys * cz * ch, 16 * n * rows * keys * ch),
        name="slab_forward",
    )(*blocks, w_lin, w_gate, slab_flags, flags)


def row_of(order, per, p):
    return (lax.axis_index("row") ^ order[p // per]) * per + p % per


def widen(grads, wide):
    at = 0
    for grad_ref in grads:
        wide[at : at + grad_ref.shape[0]] = grad_ref[...].astype(F32)
        at += grad_ref.shape[0]
    return at


def add_sums(wide, count, j0, keys, values, sums_ref):
    ch = wide.shape[2]
    for p in range(count):
        total = sums_ref[p]
        for j, value in enumerate(values):
            total = total + jnp.broadcast_to(wide[p, pl.ds(j0 + j, 1), :], (keys, ch)) * value
        sums_ref[p] = total


def add_totals(wide, rows, j0, slab_value_ref, totals):
    _, keys, ch = slab_value_ref.shape
    totals = list(totals)
    for p, i in enumerate(rows):
        mine = slab_value_ref[i]
        for j in range(len(totals)):
            g = jnp.broadcast_to(wide[p, pl.ds(j0 + j, 1), :], (keys, ch))
            totals[j] = totals[j] + g * mine
    return totals


def sums_kernel(n_grads, *refs):
    grads, (value_ref, sums_ref, wide) = refs[:n_grads], refs[n_grads:]
    cols, keys, ch = value_ref.shape
    count = widen(grads, wide)
    sums_ref[...] = jnp.zeros_like(sums_ref)

    def step(s, carry):
        j0 = pl.multiple_of(s * J_STEP, J_STEP)
        values = [value_ref[j0 + j].astype(F32) for j in range(J_STEP)]
        add_sums(wide, count, j0, keys, values, sums_ref)
        return carry

    lax.fori_loop(0, cols // J_STEP, step, 0, unroll=2)


def first_sums(grads, value):
    cols, keys, ch = value.shape
    rows = sum(g.shape[0] for g in grads)
    return pl.pallas_call(
        functools.partial(sums_kernel, len(grads)),
        out_shape=jax.ShapeDtypeStruct((rows, keys, ch), F32),
        in_specs=[VMEM] * (len(grads) + 1),
        out_specs=VMEM,
        scratch_shapes=[pltpu.VMEM((rows, cols, ch), F32)],
        compiler_params=params(),
        cost_estimate=cost(2 * rows * cols * keys * ch, 8 * cols * keys * ch),
        name="first_sums_over_j",
    )(*grads, value)


def totals_kernel(order, n_grads, *refs):
    grads, (slab_value_ref, total_ref, wide) = refs[:n_grads], refs[n_grads:]
    cols, keys, ch = total_ref.shape
    count = widen(grads, wide)
    per = slab_value_ref.shape[0] // len(order)
    rows = [row_of(order, per, p) for p in range(count)]

    def step(s, carry):
        j0 = pl.multiple_of(s * J_STEP, J_STEP)
        totals = [jnp.zeros((keys, ch), F32)] * J_STEP
        totals = add_totals(wide, rows, j0, slab_value_ref, totals)
        for j in range(J_STEP):
            total_ref[j0 + j] = totals[j]
        return carry

    lax.fori_loop(0, cols // J_STEP, step, 0, unroll=2)


def first_totals(order, grads, slab_value):
    _, keys, ch = slab_value.shape
    cols = grads[0].shape[1]
    rows = sum(g.shape[0] for g in grads)
    return pl.pallas_call(
        functools.partial(totals_kernel, order, len(grads)),
        out_shape=jax.ShapeDtypeStruct((cols, keys, ch), F32),
        in_specs=[VMEM] * (len(grads) + 1),
        out_specs=VMEM,
        scratch_shapes=[pltpu.VMEM((rows, cols, ch), F32)],
        compiler_params=params(),
        cost_estimate=cost(2 * rows * cols * keys * ch, 8 * cols * keys * ch),
        name="first_totals_over_i",
    )(*grads, slab_value)


def main_kernel(
    order,
    blocks,
    grad_ref,
    total_ref,
    first_sums_ref,
    pair_ref,
    value_ref,
    lin_ref,
    gate_ref,
    slab_ref,
    slab_value_ref,
    slab_lin_ref,
    slab_gate_ref,
    d_lin_ref,
    d_gate_ref,
    sum_keep_ref,
    sum_send_ref,
    w_keep_ref,
    w_send_ref,
    wide,
    sums_ref,
    slab_sum,
):
    cols, keys, cz = pair_ref.shape
    ch = value_ref.shape[2]
    slab_rows = slab_ref.shape[0]
    done = first_sums_ref.shape[0]
    per = slab_rows // len(order)
    col = lax.axis_index("col")
    count = widen([grad_ref], wide)
    sums_ref[...] = jnp.zeros_like(sums_ref)
    rows = [row_of(order, per, done + p) for p in range(count)]

    def weights(rows, d_lin, d_gate):
        both = jnp.concatenate([d_lin, d_gate], axis=1)
        return lax.dot_general(
            rows, both, (((0,), (0,)), ((), ())), preferred_element_type=F32
        )

    pair_w = jnp.zeros((cz, 2 * ch), F32)
    for first in range(0, cols, W_STEP):
        for j0 in range(first, first + W_STEP, J_STEP):
            values = [value_ref[j0 + j].astype(F32) for j in range(J_STEP)]
            add_sums(wide, count, j0, keys, values, sums_ref)
            totals = [total_ref[j0 + j] for j in range(J_STEP)]
            totals = add_totals(wide, rows, j0, slab_value_ref, totals)
            for j in range(J_STEP):
                d_lin_ref[j0 + j] = (totals[j] * lin_ref[j0 + j]).astype(BF16)
                d_gate_ref[j0 + j] = (totals[j] * gate_ref[j0 + j]).astype(BF16)
        some = slice(first, first + W_STEP)
        pair_w = pair_w + weights(
            pair_ref[some].reshape(W_STEP * keys, cz),
            d_lin_ref[some].reshape(W_STEP * keys, ch),
            d_gate_ref[some].reshape(W_STEP * keys, ch),
        )
    for p in range(done):
        slab_sum[row_of(order, per, p)] = first_sums_ref[p]
    for p in range(count):
        slab_sum[rows[p]] = sums_ref[p]

    sums = slab_sum[...]
    s_lin = (sums * slab_lin_ref[...]).astype(BF16).reshape(slab_rows * keys, ch)
    s_gate = (sums * slab_gate_ref[...]).astype(BF16).reshape(slab_rows * keys, ch)
    slab_w = weights(slab_ref[...].reshape(slab_rows * keys, cz), s_lin, s_gate)
    first = parity() == 0
    keep = jnp.where(first, slab_w, pair_w)
    send = jnp.where(first, pair_w, slab_w)
    for h in range(2):
        w_keep_ref[h] = keep[:, h * ch : (h + 1) * ch]
        w_send_ref[h] = send[:, h * ch : (h + 1) * ch]
    own = sum_keep_ref.shape[1]
    for n, b in enumerate(blocks):
        sum_keep_ref[n] = slab_sum[pl.ds((col ^ b) * own, own)]
        sum_send_ref[n] = slab_sum[pl.ds((col ^ b ^ 1) * own, own)]


def main_part(order, blocks, grads, first, pair, forward, slab):
    cols, keys, cz = pair.shape
    ch = forward[0].shape[2]
    slab_rows = slab[0].shape[0]
    own = slab_rows // (2 * len(blocks))
    d_type = jax.ShapeDtypeStruct((cols, keys, ch), BF16)
    s_type = jax.ShapeDtypeStruct((len(blocks), own, keys, ch), F32)
    w_type = jax.ShapeDtypeStruct((2, cz, ch), F32)
    return pl.pallas_call(
        functools.partial(main_kernel, order, blocks),
        out_shape=(d_type, d_type, s_type, s_type, w_type, w_type),
        in_specs=[VMEM] * 11,
        out_specs=(VMEM,) * 6,
        scratch_shapes=[
            pltpu.VMEM((grads.shape[0], cols, ch), F32),
            pltpu.VMEM((grads.shape[0], keys, ch), F32),
            pltpu.VMEM((slab_rows, keys, ch), F32),
        ],
        compiler_params=params(),
        cost_estimate=cost(8 * cols * keys * cz * ch, 16 * cols * keys * ch),
        name="last_rows",
    )(grads, *first, pair, *forward, *slab)


def pair_out_kernel(d_lin_ref, d_gate_ref, w_lin_ref, w_gate_ref, out_ref):
    rows, ch = d_lin_ref.shape
    weights = jnp.concatenate([w_lin_ref[...], w_gate_ref[...]], axis=1)
    step = rows

    def body(s, carry):
        at = pl.ds(pl.multiple_of(s * step, step), step)
        both = jnp.concatenate([d_lin_ref[at, :], d_gate_ref[at, :]], axis=1)
        out = lax.dot_general(
            both, weights, (((1,), (1,)), ((), ())), preferred_element_type=F32
        )
        out_ref[at, :] = out.astype(BF16)
        return carry

    lax.fori_loop(0, rows // step, body, 0)


def pair_out(d_lin, d_gate, w_lin, w_gate):
    cols, keys, ch = d_lin.shape
    cz = w_lin.shape[0]
    out = pl.pallas_call(
        pair_out_kernel,
        out_shape=jax.ShapeDtypeStruct((cols * keys, cz), BF16),
        in_specs=[VMEM] * 4,
        out_specs=VMEM,
        compiler_params=params(),
        cost_estimate=cost(4 * cols * keys * cz * ch, 6 * cols * keys * ch),
        name="pair_input_grad",
    )(d_lin.reshape(cols * keys, ch), d_gate.reshape(cols * keys, ch), w_lin, w_gate)
    return out.reshape(cols, keys, cz)


def hand_on_kernel(given_ref, out_ref):
    out_ref[...] = given_ref[...]


def hand_on(given):
    return pl.pallas_call(
        hand_on_kernel,
        out_shape=jax.ShapeDtypeStruct(given.shape, given.dtype),
        in_specs=[VMEM],
        out_specs=VMEM,
        compiler_params=params(),
        cost_estimate=cost(STAGE_COST * given.size, 8 * given.size),
        name="hand_on",
    )(given)


def fold_kernel(kept_ref, got_ref, sum_ref, moved_ref):
    half = sum_ref.shape[0]
    sum_ref[...] = kept_ref[:half] + got_ref[:half].astype(F32)
    moved_ref[...] = (kept_ref[half:] + got_ref[half:].astype(F32)).astype(BF16)


def fold(kept, got):
    half = (kept.shape[0] // 2,) + kept.shape[1:]
    return pl.pallas_call(
        fold_kernel,
        out_shape=(jax.ShapeDtypeStruct(half, F32), jax.ShapeDtypeStruct(half, BF16)),
        in_specs=[VMEM, VMEM],
        out_specs=(VMEM, VMEM),
        compiler_params=params(),
        cost_estimate=cost(STAGE_COST * kept.size, 8 * kept.size),
        name="fold",
    )(kept, got)


def add_pair(own, got):
    return (own.astype(F32) + got.astype(F32)).astype(BF16)


def four_kernel(a_ref, b_ref, c_ref, d_ref, out_ref):
    one = d_ref[...].astype(F32) + c_ref[...].astype(F32)
    two = b_ref[...].astype(F32) + a_ref[...].astype(F32)
    out_ref[...] = (one + two).astype(BF16)


def add_sums_of_four(*parts):
    return pl.pallas_call(
        four_kernel,
        out_shape=jax.ShapeDtypeStruct(parts[0].shape, BF16),
        in_specs=[VMEM] * 4,
        out_specs=VMEM,
        compiler_params=params(),
        cost_estimate=cost(4 * parts[0].size, 10 * parts[0].size),
        name="add_four",
    )(*parts)


def join_kernel(pair_bit, diagonal_ref, late_ref, pair_ref, own_ref, out_ref):
    upper = jnp.minimum(lax.axis_index("col") & pair_bit, 1)
    own = own_ref[...].astype(F32) + late_ref[...].astype(F32)
    other = pair_ref[...].astype(F32) + diagonal_ref[...].astype(F32)
    out_ref[upper] = own.astype(BF16)
    out_ref[1 - upper] = other.astype(BF16)


def join_sums(pair_bit, *parts):
    cz, ch = parts[0].shape
    return pl.pallas_call(
        functools.partial(join_kernel, pair_bit),
        out_shape=jax.ShapeDtypeStruct((2, cz, ch), BF16),
        in_specs=[VMEM] * 4,
        out_specs=VMEM,
        compiler_params=params(),
        cost_estimate=cost(4 * cz * ch, 12 * cz * ch),
        name="join_sums",
    )(*parts)


def slab_out_kernel(sum_ref, got_ref, lin_ref, gate_ref, w_lin_ref, w_gate_ref, out_ref):
    own, keys, ch = sum_ref.shape
    col = lax.axis_index("col")
    at = pl.ds(col * own, own)
    total = sum_ref[...] + got_ref[...].astype(F32)
    d_lin = (total * lin_ref[at]).astype(BF16).reshape(own * keys, ch)
    d_gate = (total * gate_ref[at]).astype(BF16).reshape(own * keys, ch)
    both = jnp.concatenate([d_lin, d_gate], axis=1)
    weights = jnp.concatenate([w_lin_ref[...], w_gate_ref[...]], axis=1)
    out = lax.dot_general(both, weights, (((1,), (1,)), ((), ())), preferred_element_type=F32)
    out_ref[...] = out.astype(BF16).reshape(own, keys, w_lin_ref.shape[0])


def slab_out(total, got, lin, gate, w_lin, w_gate):
    own, keys, ch = total.shape
    cz = w_lin.shape[0]
    return pl.pallas_call(
        slab_out_kernel,
        out_shape=jax.ShapeDtypeStruct((own, keys, cz), BF16),
        in_specs=[VMEM] * 6,
        out_specs=VMEM,
        compiler_params=params(),
        cost_estimate=cost(4 * own * keys * cz * ch, 16 * own * keys * ch),
        name="slab_input_grad",
    )(total, got, lin, gate, w_lin, w_gate)


def on_device(
    pair_slab, pair_full, grad_out, w_a_lin, w_a_gate, w_b_lin, w_b_gate, mask_slab, mask_residue
):
    n_row, n_col = lax.axis_size("row"), lax.axis_size("col")
    row_bits, col_bits = bits_of(n_row), bits_of(n_col)
    residues = mask_residue.shape[0]

    steps = [row_bits[-1]] + row_bits[1:-1] + row_bits[:1]
    ch = w_a_lin.shape[1]
    held, own_slab, *staged = stage(lead(), grad_out, pair_slab, w_a_lin, w_a_gate, w_b_lin, w_b_gate)
    order = [0]
    blocks = {0: own_slab}
    for bit in reversed(col_bits[1:]):
        for b in list(blocks):
            blocks[b ^ bit] = swap(blocks[b], "col", bit)
    got = swap(grad_out, "row", steps[0])
    for bit, later in zip(steps, steps[1:-1]):
        held = jnp.concatenate([held, got], axis=0)
        order = order + [r ^ bit for r in order]
        got = swap(held, "row", later)
    masks = lax.optimization_barrier(((mask_slab, mask_residue), held, blocks))[0]
    slab_flags, flags = (
        jnp.broadcast_to(m.astype(BF16)[:, None], m.shape + (ch,)) for m in masks
    )
    value, lin, gate = pair_forward(pair_full, *staged[2:], flags)
    got_last = swap(held, "row", steps[-1])
    got, value = lax.optimization_barrier((got, value))
    got_both = swap(got, "row", steps[-1])
    for bit in steps[-2:]:
        order = order + [r ^ bit for r in order]
    slabs = jnp.concatenate([blocks[b] for b in sorted(blocks)], axis=0)
    slabs = [slabs, swap(slabs, "col", 1)]
    slab = slab_forward(slabs, n_col, *staged[:2], slab_flags, flags)
    pieces = [held, got, got_last]
    first = (first_totals(order, pieces, slab[1]), first_sums(pieces, value))
    kept = [0]
    for bit in reversed(col_bits[1:]):
        kept = kept + [b ^ bit for b in kept]
    d_lin, d_gate, sum_keep, sum_send, w_keep, w_send = main_part(
        order, kept, got_both, first, pair_full, (value, lin, gate), slab
    )
    pair_bit, col = col_bits[1], lax.axis_index("col")
    got_w = swap(w_send, "col", 1)
    side = w_keep + got_w
    upper = (col & pair_bit) != 0
    moved = jnp.where(upper, side[0], side[1]).astype(BF16)
    narrow = jnp.where(upper, side[1], side[0]).astype(BF16)
    moved, narrow, sum_send, d_lin, d_gate = lax.optimization_barrier(
        (moved, narrow, sum_send, d_lin, d_gate)
    )
    grad_pair = pair_out(d_lin, d_gate, w_b_lin, w_b_gate)
    sums, got = sum_keep, swap(sum_send, "col", 1)
    bits = [bit * n_col for bit in row_bits]
    near, late = bits[0], bits[1]
    diagonal = swap_chips(moved, pair_bit | near, 0)
    pair_part, near_part = swap_chips(moved, pair_bit), swap_chips(narrow, near)
    narrow = add_sums_of_four(diagonal, near_part, pair_part, narrow)
    between = col_bits[2:] + [bit for bit in bits if bit not in (near, late)]
    for bit in between:
        if bit == between[-1]:
            narrow, got, grad_pair = lax.optimization_barrier((narrow, got, grad_pair))
            for far in col_bits[1:]:
                sums, moved = fold(sums, got)
                got = swap(moved, "col", far)
        narrow = add_pair(narrow, swap_chips(narrow, bit))
    diagonal = swap_chips(narrow, pair_bit | late, 0)
    late_part, pair_part = swap_chips(narrow, late), swap_chips(narrow, pair_bit)
    mine = join_sums(pair_bit, diagonal, late_part, pair_part, narrow)
    both = [m.astype(F32) / residues for m in (mine, swap(mine, "col", 1))]
    first = parity() == 0
    grad_weights = jnp.where(
        first, jnp.concatenate(both, axis=0), jnp.concatenate(both[::-1], axis=0)
    )
    grad_slab = slab_out(sums[0], got[0], slab[2], slab[3], w_a_lin, w_a_gate)
    return (grad_slab, grad_pair, grad_weights)


def solution(mesh):
    return jax.shard_map(
        on_device,
        mesh=mesh,
        in_specs=(
            P("col", "row", None),
            P("col", "row", None),
            P("row", "col", None),
            P(),
            P(),
            P(),
            P(),
            P(),
            P(),
        ),
        out_specs=(P("col", "row", None), P("col", "row", None), P()),
        check_vma=False,
    )
```

```python
import functools

import jax
import jax.numpy as jnp
from jax import lax
from jax.experimental import pallas as pl
from jax.experimental.pallas import tpu as pltpu
from jax.sharding import PartitionSpec as P

F32 = jnp.float32
BF16 = jnp.bfloat16
VMEM = pl.BlockSpec(memory_space=pltpu.VMEM)
WHOLE = pl.BlockSpec()
SMEM = pl.BlockSpec(memory_space=pltpu.SMEM)
J_STEP = 4
FORWARD_STEP = 64
W_STEP = 16
STAGE_COST = 400000


def bits_of(size):
    return [1 << b for b in range(size.bit_length() - 1)]


def swap(value, axis, bit):
    size = lax.axis_size(axis)
    return lax.ppermute(value, axis, [(d, d ^ bit) for d in range(size)])


def swap_chips(value, bit, flip=1):
    n_row, n_col = lax.axis_size("row"), lax.axis_size("col")
    pairs = [(d, d ^ bit ^ flip) for d in range(n_row * n_col)]
    return lax.ppermute(value, ("row", "col"), pairs)


def parity():
    number = lax.axis_index("row") ^ lax.axis_index("col")
    for shift in (16, 8, 4, 2, 1):
        number = number ^ (number >> shift)
    return number & 1


def params(mib=32):
    return pltpu.CompilerParams(vmem_limit_bytes=mib * 1024 * 1024)


def cost(flops, bytes_accessed, transcendentals=0):
    return pl.CostEstimate(
        flops=flops, bytes_accessed=bytes_accessed, transcendentals=transcendentals
    )


def project(rows, w_lin, w_gate):
    both = jnp.dot(
        rows, jnp.concatenate([w_lin, w_gate], axis=1), preferred_element_type=F32
    )
    ch = w_lin.shape[1]
    linear = both[:, :ch]
    sigmoid = 1.0 / (1.0 + jnp.exp(-both[:, ch:]))
    return linear, sigmoid


def lead_kernel(out_ref):
    out_ref[...] = jnp.zeros_like(out_ref)


def lead():
    return pl.pallas_call(
        lead_kernel,
        out_shape=jax.ShapeDtypeStruct((8, 128), F32),
        out_specs=VMEM,
        compiler_params=params(),
        cost_estimate=cost(STAGE_COST * 8192, 4096),
        name="lead",
    )()


def stage_kernel(n, _, *refs):
    for source_ref, copy_ref in zip(refs[:n], refs[n:]):
        copy_ref[...] = source_ref[...]


def stage(after, *sources):
    n = len(sources)
    return pl.pallas_call(
        functools.partial(stage_kernel, n),
        out_shape=tuple(jax.ShapeDtypeStruct(s.shape, s.dtype) for s in sources),
        in_specs=[VMEM] * (n + 1),
        out_specs=(VMEM,) * n,
        compiler_params=params(),
        cost_estimate=cost(STAGE_COST * sources[0].size, 4 * sources[0].size),
        name="stage",
    )(after, *sources)


def pair_forward_kernel(pair_ref, w_lin_ref, w_gate_ref, flags_ref, value_ref, lin_ref, gate_ref):
    cols, keys, cz = pair_ref.shape
    row, col = lax.axis_index("row"), lax.axis_index("col")
    km = flags_ref[pl.ds(pl.multiple_of(row * keys, 16), keys)].astype(F32)
    step = min(cols, FORWARD_STEP)

    def body(s, carry):
        j0 = pl.multiple_of(s * step, step)
        rows = pair_ref[pl.ds(j0, step)].reshape(step * keys, cz)
        linear, sigmoid = project(rows, w_lin_ref[...], w_gate_ref[...])
        linear = linear.reshape(step, keys, -1)
        sigmoid = sigmoid.reshape(step, keys, -1)
        flags = flags_ref[pl.ds(pl.multiple_of(col * cols + j0, step), step)].astype(F32)
        for j in range(step):
            m = km * flags[j : j + 1]
            masked = m * sigmoid[j]
            lin = linear[j]
            value_ref[j0 + j] = (masked * lin).astype(BF16)
            lin_ref[j0 + j] = masked
            gate_ref[j0 + j] = masked * lin * (1.0 - sigmoid[j])
        return carry

    lax.fori_loop(0, cols // step, body, 0)


def pair_forward(pair, w_lin, w_gate, flags):
    cols, keys, cz = pair.shape
    ch = w_lin.shape[1]
    out = jax.ShapeDtypeStruct((cols, keys, ch), F32)
    return pl.pallas_call(
        pair_forward_kernel,
        out_shape=(jax.ShapeDtypeStruct((cols, keys, ch), BF16), out, out),
        in_specs=[VMEM] * 4,
        out_specs=(VMEM, VMEM, VMEM),
        compiler_params=params(),
        cost_estimate=cost(4 * cols * keys * cz * ch, 14 * cols * keys * ch, cols * keys * ch),
        name="pair_forward",
    )(pair, w_lin, w_gate, flags)


def slab_forward_kernel(
    n_blocks,
    even_ref,
    odd_ref,
    w_lin_ref,
    w_gate_ref,
    slab_flags_ref,
    flags_ref,
    slab_ref,
    value_ref,
    lin_ref,
    gate_ref,
):
    _, keys, cz = even_ref.shape
    rows = 2 * even_ref.shape[0] // n_blocks
    row, col = lax.axis_index("row"), lax.axis_index("col")
    km = flags_ref[pl.ds(pl.multiple_of(row * keys, 16), keys)].astype(F32)
    flags = slab_flags_ref[...].astype(F32)
    for i in range(n_blocks * rows):
        value_ref[i] = km * flags[i : i + 1]
    for b in range(n_blocks):
        first = (col ^ b) * rows
        block = (odd_ref if b % 2 else even_ref)[(b // 2) * rows : (b // 2 + 1) * rows]
        linear, sigmoid = project(
            block.reshape(rows * keys, cz),
            w_lin_ref[...],
            w_gate_ref[...],
        )
        linear = linear.reshape(rows, keys, -1)
        sigmoid = sigmoid.reshape(rows, keys, -1)
        for r in range(rows):
            i = first + r
            masked = value_ref[i] * sigmoid[r]
            slab_ref[i] = block[r]
            value_ref[i] = (masked * linear[r]).astype(BF16).astype(F32)
            lin_ref[i] = masked
            gate_ref[i] = masked * linear[r] * (1.0 - sigmoid[r])


def slab_forward(blocks, n, w_lin, w_gate, slab_flags, flags):
    half, keys, cz = blocks[0].shape
    rows = 2 * half // n
    ch = w_lin.shape[1]
    out = jax.ShapeDtypeStruct((n * rows, keys, ch), F32)
    raw = jax.ShapeDtypeStruct((n * rows, keys, cz), BF16)
    return pl.pallas_call(
        functools.partial(slab_forward_kernel, n),
        out_shape=(raw, out, out, out),
        in_specs=[VMEM] * 6,
        out_specs=(VMEM,) * 4,
        compiler_params=params(),
        cost_estimate=cost(4 * n * rows * keys * cz * ch, 16 * n * rows * keys * ch),
        name="slab_forward",
    )(*blocks, w_lin, w_gate, slab_flags, flags)


def row_of(order, per, p):
    return (lax.axis_index("row") ^ order[p // per]) * per + p % per


def widen(grads, wide):
    at = 0
    for grad_ref in grads:
        wide[at : at + grad_ref.shape[0]] = grad_ref[...].astype(F32)
        at += grad_ref.shape[0]
    return at


def add_sums(wide, count, j0, keys, values, sums_ref):
    ch = wide.shape[2]
    for p in range(count):
        total = sums_ref[p]
        for j, value in enumerate(values):
            total = total + jnp.broadcast_to(wide[p, pl.ds(j0 + j, 1), :], (keys, ch)) * value
        sums_ref[p] = total


def add_totals(wide, rows, j0, slab_value_ref, totals):
    _, keys, ch = slab_value_ref.shape
    totals = list(totals)
    for p, i in enumerate(rows):
        mine = slab_value_ref[i]
        for j in range(len(totals)):
            g = jnp.broadcast_to(wide[p, pl.ds(j0 + j, 1), :], (keys, ch))
            totals[j] = totals[j] + g * mine
    return totals


def sums_kernel(n_grads, *refs):
    grads, (value_ref, sums_ref, wide) = refs[:n_grads], refs[n_grads:]
    cols, keys, ch = value_ref.shape
    count = widen(grads, wide)
    sums_ref[...] = jnp.zeros_like(sums_ref)

    def step(s, carry):
        j0 = pl.multiple_of(s * J_STEP, J_STEP)
        values = [value_ref[j0 + j].astype(F32) for j in range(J_STEP)]
        add_sums(wide, count, j0, keys, values, sums_ref)
        return carry

    lax.fori_loop(0, cols // J_STEP, step, 0, unroll=2)


def first_sums(grads, value):
    cols, keys, ch = value.shape
    rows = sum(g.shape[0] for g in grads)
    return pl.pallas_call(
        functools.partial(sums_kernel, len(grads)),
        out_shape=jax.ShapeDtypeStruct((rows, keys, ch), F32),
        in_specs=[VMEM] * (len(grads) + 1),
        out_specs=VMEM,
        scratch_shapes=[pltpu.VMEM((rows, cols, ch), F32)],
        compiler_params=params(),
        cost_estimate=cost(2 * rows * cols * keys * ch, 8 * cols * keys * ch),
        name="first_sums_over_j",
    )(*grads, value)


def totals_kernel(order, n_grads, *refs):
    grads, (slab_value_ref, total_ref, wide) = refs[:n_grads], refs[n_grads:]
    cols, keys, ch = total_ref.shape
    count = widen(grads, wide)
    per = slab_value_ref.shape[0] // len(order)
    rows = [row_of(order, per, p) for p in range(count)]

    def step(s, carry):
        j0 = pl.multiple_of(s * J_STEP, J_STEP)
        totals = [jnp.zeros((keys, ch), F32)] * J_STEP
        totals = add_totals(wide, rows, j0, slab_value_ref, totals)
        for j in range(J_STEP):
            total_ref[j0 + j] = totals[j]
        return carry

    lax.fori_loop(0, cols // J_STEP, step, 0, unroll=2)


def first_totals(order, grads, slab_value):
    _, keys, ch = slab_value.shape
    cols = grads[0].shape[1]
    rows = sum(g.shape[0] for g in grads)
    return pl.pallas_call(
        functools.partial(totals_kernel, order, len(grads)),
        out_shape=jax.ShapeDtypeStruct((cols, keys, ch), F32),
        in_specs=[VMEM] * (len(grads) + 1),
        out_specs=VMEM,
        scratch_shapes=[pltpu.VMEM((rows, cols, ch), F32)],
        compiler_params=params(),
        cost_estimate=cost(2 * rows * cols * keys * ch, 8 * cols * keys * ch),
        name="first_totals_over_i",
    )(*grads, slab_value)


def main_kernel(
    order,
    blocks,
    grad_ref,
    total_ref,
    first_sums_ref,
    pair_ref,
    value_ref,
    lin_ref,
    gate_ref,
    slab_ref,
    slab_value_ref,
    slab_lin_ref,
    slab_gate_ref,
    d_lin_ref,
    d_gate_ref,
    sum_keep_ref,
    sum_send_ref,
    w_keep_ref,
    w_send_ref,
    wide,
    sums_ref,
    slab_sum,
):
    cols, keys, cz = pair_ref.shape
    ch = value_ref.shape[2]
    slab_rows = slab_ref.shape[0]
    done = first_sums_ref.shape[0]
    per = slab_rows // len(order)
    col = lax.axis_index("col")
    count = widen([grad_ref], wide)
    sums_ref[...] = jnp.zeros_like(sums_ref)
    rows = [row_of(order, per, done + p) for p in range(count)]

    def weights(rows, d_lin, d_gate):
        both = jnp.concatenate([d_lin, d_gate], axis=1)
        return lax.dot_general(
            rows, both, (((0,), (0,)), ((), ())), preferred_element_type=F32
        )

    pair_w = jnp.zeros((cz, 2 * ch), F32)
    for first in range(0, cols, W_STEP):
        for j0 in range(first, first + W_STEP, J_STEP):
            values = [value_ref[j0 + j].astype(F32) for j in range(J_STEP)]
            add_sums(wide, count, j0, keys, values, sums_ref)
            totals = [total_ref[j0 + j] for j in range(J_STEP)]
            totals = add_totals(wide, rows, j0, slab_value_ref, totals)
            for j in range(J_STEP):
                d_lin_ref[j0 + j] = (totals[j] * lin_ref[j0 + j]).astype(BF16)
                d_gate_ref[j0 + j] = (totals[j] * gate_ref[j0 + j]).astype(BF16)
        some = slice(first, first + W_STEP)
        pair_w = pair_w + weights(
            pair_ref[some].reshape(W_STEP * keys, cz),
            d_lin_ref[some].reshape(W_STEP * keys, ch),
            d_gate_ref[some].reshape(W_STEP * keys, ch),
        )
    for p in range(done):
        slab_sum[row_of(order, per, p)] = first_sums_ref[p]
    for p in range(count):
        slab_sum[rows[p]] = sums_ref[p]

    sums = slab_sum[...]
    s_lin = (sums * slab_lin_ref[...]).astype(BF16).reshape(slab_rows * keys, ch)
    s_gate = (sums * slab_gate_ref[...]).astype(BF16).reshape(slab_rows * keys, ch)
    slab_w = weights(slab_ref[...].reshape(slab_rows * keys, cz), s_lin, s_gate)
    first = parity() == 0
    keep = jnp.where(first, slab_w, pair_w)
    send = jnp.where(first, pair_w, slab_w)
    for h in range(2):
        w_keep_ref[h] = keep[:, h * ch : (h + 1) * ch]
        w_send_ref[h] = send[:, h * ch : (h + 1) * ch]
    own = sum_keep_ref.shape[1]
    for n, b in enumerate(blocks):
        sum_keep_ref[n] = slab_sum[pl.ds((col ^ b) * own, own)]
        sum_send_ref[n] = slab_sum[pl.ds((col ^ b ^ 1) * own, own)]


def main_part(order, blocks, grads, first, pair, forward, slab):
    cols, keys, cz = pair.shape
    ch = forward[0].shape[2]
    slab_rows = slab[0].shape[0]
    own = slab_rows // (2 * len(blocks))
    d_type = jax.ShapeDtypeStruct((cols, keys, ch), BF16)
    s_type = jax.ShapeDtypeStruct((len(blocks), own, keys, ch), F32)
    w_type = jax.ShapeDtypeStruct((2, cz, ch), F32)
    return pl.pallas_call(
        functools.partial(main_kernel, order, blocks),
        out_shape=(d_type, d_type, s_type, s_type, w_type, w_type),
        in_specs=[VMEM] * 11,
        out_specs=(VMEM,) * 6,
        scratch_shapes=[
            pltpu.VMEM((grads.shape[0], cols, ch), F32),
            pltpu.VMEM((grads.shape[0], keys, ch), F32),
            pltpu.VMEM((slab_rows, keys, ch), F32),
        ],
        compiler_params=params(),
        cost_estimate=cost(8 * cols * keys * cz * ch, 16 * cols * keys * ch),
        name="last_rows",
    )(grads, *first, pair, *forward, *slab)


def pair_out_kernel(d_lin_ref, d_gate_ref, w_lin_ref, w_gate_ref, out_ref):
    rows, ch = d_lin_ref.shape
    weights = jnp.concatenate([w_lin_ref[...], w_gate_ref[...]], axis=1)
    step = rows

    def body(s, carry):
        at = pl.ds(pl.multiple_of(s * step, step), step)
        both = jnp.concatenate([d_lin_ref[at, :], d_gate_ref[at, :]], axis=1)
        out = lax.dot_general(
            both, weights, (((1,), (1,)), ((), ())), preferred_element_type=F32
        )
        out_ref[at, :] = out.astype(BF16)
        return carry

    lax.fori_loop(0, rows // step, body, 0)


def pair_out(d_lin, d_gate, w_lin, w_gate):
    cols, keys, ch = d_lin.shape
    cz = w_lin.shape[0]
    out = pl.pallas_call(
        pair_out_kernel,
        out_shape=jax.ShapeDtypeStruct((cols * keys, cz), BF16),
        in_specs=[VMEM] * 4,
        out_specs=VMEM,
        compiler_params=params(),
        cost_estimate=cost(4 * cols * keys * cz * ch, 6 * cols * keys * ch),
        name="pair_input_grad",
    )(d_lin.reshape(cols * keys, ch), d_gate.reshape(cols * keys, ch), w_lin, w_gate)
    return out.reshape(cols, keys, cz)


def hand_on_kernel(given_ref, out_ref):
    out_ref[...] = given_ref[...]


def hand_on(given):
    return pl.pallas_call(
        hand_on_kernel,
        out_shape=jax.ShapeDtypeStruct(given.shape, given.dtype),
        in_specs=[VMEM],
        out_specs=VMEM,
        compiler_params=params(),
        cost_estimate=cost(STAGE_COST * given.size, 8 * given.size),
        name="hand_on",
    )(given)


def fold_kernel(kept_ref, got_ref, sum_ref, moved_ref):
    half = sum_ref.shape[0]
    sum_ref[...] = kept_ref[:half] + got_ref[:half].astype(F32)
    moved_ref[...] = (kept_ref[half:] + got_ref[half:].astype(F32)).astype(BF16)


def fold(kept, got):
    half = (kept.shape[0] // 2,) + kept.shape[1:]
    return pl.pallas_call(
        fold_kernel,
        out_shape=(jax.ShapeDtypeStruct(half, F32), jax.ShapeDtypeStruct(half, BF16)),
        in_specs=[VMEM, VMEM],
        out_specs=(VMEM, VMEM),
        compiler_params=params(),
        cost_estimate=cost(STAGE_COST * kept.size, 8 * kept.size),
        name="fold",
    )(kept, got)


def add_pair(own, got):
    return (own.astype(F32) + got.astype(F32)).astype(BF16)


def four_kernel(a_ref, b_ref, c_ref, d_ref, out_ref):
    one = d_ref[...].astype(F32) + c_ref[...].astype(F32)
    two = b_ref[...].astype(F32) + a_ref[...].astype(F32)
    out_ref[...] = (one + two).astype(BF16)


def add_sums_of_four(*parts):
    return pl.pallas_call(
        four_kernel,
        out_shape=jax.ShapeDtypeStruct(parts[0].shape, BF16),
        in_specs=[VMEM] * 4,
        out_specs=VMEM,
        compiler_params=params(),
        cost_estimate=cost(4 * parts[0].size, 10 * parts[0].size),
        name="add_four",
    )(*parts)


def join_kernel(pair_bit, diagonal_ref, late_ref, pair_ref, own_ref, out_ref):
    upper = jnp.minimum(lax.axis_index("col") & pair_bit, 1)
    own = own_ref[...].astype(F32) + late_ref[...].astype(F32)
    other = pair_ref[...].astype(F32) + diagonal_ref[...].astype(F32)
    out_ref[upper] = own.astype(BF16)
    out_ref[1 - upper] = other.astype(BF16)


def join_sums(pair_bit, *parts):
    cz, ch = parts[0].shape
    return pl.pallas_call(
        functools.partial(join_kernel, pair_bit),
        out_shape=jax.ShapeDtypeStruct((2, cz, ch), BF16),
        in_specs=[VMEM] * 4,
        out_specs=VMEM,
        compiler_params=params(),
        cost_estimate=cost(4 * cz * ch, 12 * cz * ch),
        name="join_sums",
    )(*parts)


def slab_out_kernel(sum_ref, got_ref, lin_ref, gate_ref, w_lin_ref, w_gate_ref, out_ref):
    own, keys, ch = sum_ref.shape
    col = lax.axis_index("col")
    at = pl.ds(col * own, own)
    total = sum_ref[...] + got_ref[...].astype(F32)
    d_lin = (total * lin_ref[at]).astype(BF16).reshape(own * keys, ch)
    d_gate = (total * gate_ref[at]).astype(BF16).reshape(own * keys, ch)
    both = jnp.concatenate([d_lin, d_gate], axis=1)
    weights = jnp.concatenate([w_lin_ref[...], w_gate_ref[...]], axis=1)
    out = lax.dot_general(both, weights, (((1,), (1,)), ((), ())), preferred_element_type=F32)
    out_ref[...] = out.astype(BF16).reshape(own, keys, w_lin_ref.shape[0])


def slab_out(total, got, lin, gate, w_lin, w_gate):
    own, keys, ch = total.shape
    cz = w_lin.shape[0]
    return pl.pallas_call(
        slab_out_kernel,
        out_shape=jax.ShapeDtypeStruct((own, keys, cz), BF16),
        in_specs=[VMEM] * 6,
        out_specs=VMEM,
        compiler_params=params(),
        cost_estimate=cost(4 * own * keys * cz * ch, 16 * own * keys * ch),
        name="slab_input_grad",
    )(total, got, lin, gate, w_lin, w_gate)


def on_device(
    pair_slab, pair_full, grad_out, w_a_lin, w_a_gate, w_b_lin, w_b_gate, mask_slab, mask_residue
):
    n_row, n_col = lax.axis_size("row"), lax.axis_size("col")
    row_bits, col_bits = bits_of(n_row), bits_of(n_col)
    residues = mask_residue.shape[0]

    steps = row_bits[1:-1] + [row_bits[-1]] + row_bits[:1]
    ch = w_a_lin.shape[1]
    held, own_slab, *staged = stage(lead(), grad_out, pair_slab, w_a_lin, w_a_gate, w_b_lin, w_b_gate)
    order = [0]
    blocks = {0: own_slab}
    for bit in reversed(col_bits[1:]):
        for b in list(blocks):
            blocks[b ^ bit] = swap(blocks[b], "col", bit)
    got = swap(grad_out, "row", steps[0])
    for bit, later in zip(steps, steps[1:-1]):
        held = jnp.concatenate([held, got], axis=0)
        order = order + [r ^ bit for r in order]
        got = swap(held, "row", later)
    masks = lax.optimization_barrier(((mask_slab, mask_residue), held, blocks))[0]
    slab_flags, flags = (
        jnp.broadcast_to(m.astype(BF16)[:, None], m.shape + (ch,)) for m in masks
    )
    value, lin, gate = pair_forward(pair_full, *staged[2:], flags)
    got_last = swap(held, "row", steps[-1])
    got, value = lax.optimization_barrier((got, value))
    got_both = swap(got, "row", steps[-1])
    for bit in steps[-2:]:
        order = order + [r ^ bit for r in order]
    slabs = jnp.concatenate([blocks[b] for b in sorted(blocks)], axis=0)
    slabs = [slabs, swap(slabs, "col", 1)]
    slab = slab_forward(slabs, n_col, *staged[:2], slab_flags, flags)
    pieces = [held, got, got_last]
    first = (first_totals(order, pieces, slab[1]), first_sums(pieces, value))
    kept = [0]
    for bit in reversed(col_bits[1:]):
        kept = kept + [b ^ bit for b in kept]
    d_lin, d_gate, sum_keep, sum_send, w_keep, w_send = main_part(
        order, kept, got_both, first, pair_full, (value, lin, gate), slab
    )
    pair_bit, col = col_bits[1], lax.axis_index("col")
    got_w = swap(w_send, "col", 1)
    side = w_keep + got_w
    upper = (col & pair_bit) != 0
    moved = jnp.where(upper, side[0], side[1]).astype(BF16)
    narrow = jnp.where(upper, side[1], side[0]).astype(BF16)
    moved, narrow, sum_send, d_lin, d_gate = lax.optimization_barrier(
        (moved, narrow, sum_send, d_lin, d_gate)
    )
    grad_pair = pair_out(d_lin, d_gate, w_b_lin, w_b_gate)
    sums, got = sum_keep, swap(sum_send, "col", 1)
    bits = [bit * n_col for bit in row_bits]
    near, late = bits[0], bits[1]
    diagonal = swap_chips(moved, pair_bit | near, 0)
    pair_part, near_part = swap_chips(moved, pair_bit), swap_chips(narrow, near)
    narrow = add_sums_of_four(diagonal, near_part, pair_part, narrow)
    between = col_bits[2:] + [bit for bit in bits if bit not in (near, late)]
    for bit in between:
        if bit == between[-1]:
            narrow, got, grad_pair = lax.optimization_barrier((narrow, got, grad_pair))
            for far in col_bits[1:]:
                sums, moved = fold(sums, got)
                got = swap(moved, "col", far)
        narrow = add_pair(narrow, swap_chips(narrow, bit))
    diagonal = swap_chips(narrow, pair_bit | late, 0)
    late_part, pair_part = swap_chips(narrow, late), swap_chips(narrow, pair_bit)
    mine = join_sums(pair_bit, diagonal, late_part, pair_part, narrow)
    both = [m.astype(F32) / residues for m in (mine, swap(mine, "col", 1))]
    first = parity() == 0
    grad_weights = jnp.where(
        first, jnp.concatenate(both, axis=0), jnp.concatenate(both[::-1], axis=0)
    )
    grad_slab = slab_out(sums[0], got[0], slab[2], slab[3], w_a_lin, w_a_gate)
    return (grad_slab, grad_pair, grad_weights)


def solution(mesh):
    return jax.shard_map(
        on_device,
        mesh=mesh,
        in_specs=(
            P("col", "row", None),
            P("col", "row", None),
            P("row", "col", None),
            P(),
            P(),
            P(),
            P(),
            P(),
            P(),
        ),
        out_specs=(P("col", "row", None), P("col", "row", None), P()),
        check_vma=False,
    )
```

```python
import functools

import jax
import jax.numpy as jnp
from jax import lax
from jax.experimental import pallas as pl
from jax.experimental.pallas import tpu as pltpu
from jax.sharding import PartitionSpec as P

F32 = jnp.float32
BF16 = jnp.bfloat16
VMEM = pl.BlockSpec(memory_space=pltpu.VMEM)
WHOLE = pl.BlockSpec()
SMEM = pl.BlockSpec(memory_space=pltpu.SMEM)
J_STEP = 4
FORWARD_STEP = 64
W_STEP = 16
STAGE_COST = 400000


def bits_of(size):
    return [1 << b for b in range(size.bit_length() - 1)]


def swap(value, axis, bit):
    size = lax.axis_size(axis)
    return lax.ppermute(value, axis, [(d, d ^ bit) for d in range(size)])


def swap_chips(value, bit, flip=1):
    n_row, n_col = lax.axis_size("row"), lax.axis_size("col")
    pairs = [(d, d ^ bit ^ flip) for d in range(n_row * n_col)]
    return lax.ppermute(value, ("row", "col"), pairs)


def parity():
    number = lax.axis_index("row") ^ lax.axis_index("col")
    for shift in (16, 8, 4, 2, 1):
        number = number ^ (number >> shift)
    return number & 1


def params(mib=32):
    return pltpu.CompilerParams(vmem_limit_bytes=mib * 1024 * 1024)


def cost(flops, bytes_accessed, transcendentals=0):
    return pl.CostEstimate(
        flops=flops, bytes_accessed=bytes_accessed, transcendentals=transcendentals
    )


def project(rows, w_lin, w_gate):
    both = jnp.dot(
        rows, jnp.concatenate([w_lin, w_gate], axis=1), preferred_element_type=F32
    )
    ch = w_lin.shape[1]
    linear = both[:, :ch]
    sigmoid = 1.0 / (1.0 + jnp.exp(-both[:, ch:]))
    return linear, sigmoid


def lead_kernel(out_ref):
    out_ref[...] = jnp.zeros_like(out_ref)


def lead():
    return pl.pallas_call(
        lead_kernel,
        out_shape=jax.ShapeDtypeStruct((8, 128), F32),
        out_specs=VMEM,
        compiler_params=params(),
        cost_estimate=cost(STAGE_COST * 8192, 4096),
        name="lead",
    )()


def stage_kernel(n, _, *refs):
    for source_ref, copy_ref in zip(refs[:n], refs[n:]):
        copy_ref[...] = source_ref[...]


def stage(after, *sources):
    n = len(sources)
    return pl.pallas_call(
        functools.partial(stage_kernel, n),
        out_shape=tuple(jax.ShapeDtypeStruct(s.shape, s.dtype) for s in sources),
        in_specs=[VMEM] * (n + 1),
        out_specs=(VMEM,) * n,
        compiler_params=params(),
        cost_estimate=cost(STAGE_COST * sources[0].size, 4 * sources[0].size),
        name="stage",
    )(after, *sources)


def pair_forward_kernel(pair_ref, w_lin_ref, w_gate_ref, flags_ref, value_ref, lin_ref, gate_ref):
    cols, keys, cz = pair_ref.shape
    row, col = lax.axis_index("row"), lax.axis_index("col")
    km = flags_ref[pl.ds(pl.multiple_of(row * keys, 16), keys)].astype(F32)
    step = min(cols, FORWARD_STEP)

    def body(s, carry):
        j0 = pl.multiple_of(s * step, step)
        rows = pair_ref[pl.ds(j0, step)].reshape(step * keys, cz)
        linear, sigmoid = project(rows, w_lin_ref[...], w_gate_ref[...])
        linear = linear.reshape(step, keys, -1)
        sigmoid = sigmoid.reshape(step, keys, -1)
        flags = flags_ref[pl.ds(pl.multiple_of(col * cols + j0, step), step)].astype(F32)
        for j in range(step):
            m = km * flags[j : j + 1]
            masked = m * sigmoid[j]
            lin = linear[j]
            value_ref[j0 + j] = (masked * lin).astype(BF16)
            lin_ref[j0 + j] = masked
            gate_ref[j0 + j] = masked * lin * (1.0 - sigmoid[j])
        return carry

    lax.fori_loop(0, cols // step, body, 0)


def pair_forward(pair, w_lin, w_gate, flags):
    cols, keys, cz = pair.shape
    ch = w_lin.shape[1]
    out = jax.ShapeDtypeStruct((cols, keys, ch), F32)
    return pl.pallas_call(
        pair_forward_kernel,
        out_shape=(jax.ShapeDtypeStruct((cols, keys, ch), BF16), out, out),
        in_specs=[VMEM] * 4,
        out_specs=(VMEM, VMEM, VMEM),
        compiler_params=params(),
        cost_estimate=cost(4 * cols * keys * cz * ch, 14 * cols * keys * ch, cols * keys * ch),
        name="pair_forward",
    )(pair, w_lin, w_gate, flags)


def slab_forward_kernel(
    n_blocks,
    even_ref,
    odd_ref,
    w_lin_ref,
    w_gate_ref,
    slab_flags_ref,
    flags_ref,
    slab_ref,
    value_ref,
    lin_ref,
    gate_ref,
):
    _, keys, cz = even_ref.shape
    rows = 2 * even_ref.shape[0] // n_blocks
    row, col = lax.axis_index("row"), lax.axis_index("col")
    km = flags_ref[pl.ds(pl.multiple_of(row * keys, 16), keys)].astype(F32)
    flags = slab_flags_ref[...].astype(F32)
    for i in range(n_blocks * rows):
        value_ref[i] = km * flags[i : i + 1]
    for b in range(n_blocks):
        first = (col ^ b) * rows
        block = (odd_ref if b % 2 else even_ref)[(b // 2) * rows : (b // 2 + 1) * rows]
        linear, sigmoid = project(
            block.reshape(rows * keys, cz),
            w_lin_ref[...],
            w_gate_ref[...],
        )
        linear = linear.reshape(rows, keys, -1)
        sigmoid = sigmoid.reshape(rows, keys, -1)
        for r in range(rows):
            i = first + r
            masked = value_ref[i] * sigmoid[r]
            slab_ref[i] = block[r]
            value_ref[i] = (masked * linear[r]).astype(BF16).astype(F32)
            lin_ref[i] = masked
            gate_ref[i] = masked * linear[r] * (1.0 - sigmoid[r])


def slab_forward(blocks, n, w_lin, w_gate, slab_flags, flags):
    half, keys, cz = blocks[0].shape
    rows = 2 * half // n
    ch = w_lin.shape[1]
    out = jax.ShapeDtypeStruct((n * rows, keys, ch), F32)
    raw = jax.ShapeDtypeStruct((n * rows, keys, cz), BF16)
    return pl.pallas_call(
        functools.partial(slab_forward_kernel, n),
        out_shape=(raw, out, out, out),
        in_specs=[VMEM] * 6,
        out_specs=(VMEM,) * 4,
        compiler_params=params(),
        cost_estimate=cost(4 * n * rows * keys * cz * ch, 16 * n * rows * keys * ch),
        name="slab_forward",
    )(*blocks, w_lin, w_gate, slab_flags, flags)


def row_of(order, per, p):
    return (lax.axis_index("row") ^ order[p // per]) * per + p % per


def widen(grads, wide):
    at = 0
    for grad_ref in grads:
        wide[at : at + grad_ref.shape[0]] = grad_ref[...].astype(F32)
        at += grad_ref.shape[0]
    return at


def add_sums(wide, count, j0, keys, values, sums_ref):
    ch = wide.shape[2]
    for p in range(count):
        total = sums_ref[p]
        for j, value in enumerate(values):
            total = total + jnp.broadcast_to(wide[p, pl.ds(j0 + j, 1), :], (keys, ch)) * value
        sums_ref[p] = total


def add_totals(wide, rows, j0, slab_value_ref, totals):
    _, keys, ch = slab_value_ref.shape
    totals = list(totals)
    for p, i in enumerate(rows):
        mine = slab_value_ref[i]
        for j in range(len(totals)):
            g = jnp.broadcast_to(wide[p, pl.ds(j0 + j, 1), :], (keys, ch))
            totals[j] = totals[j] + g * mine
    return totals


def sums_kernel(n_grads, *refs):
    grads, (value_ref, sums_ref, wide) = refs[:n_grads], refs[n_grads:]
    cols, keys, ch = value_ref.shape
    count = widen(grads, wide)
    sums_ref[...] = jnp.zeros_like(sums_ref)

    def step(s, carry):
        j0 = pl.multiple_of(s * J_STEP, J_STEP)
        values = [value_ref[j0 + j].astype(F32) for j in range(J_STEP)]
        add_sums(wide, count, j0, keys, values, sums_ref)
        return carry

    lax.fori_loop(0, cols // J_STEP, step, 0, unroll=2)


def first_sums(grads, value):
    cols, keys, ch = value.shape
    rows = sum(g.shape[0] for g in grads)
    return pl.pallas_call(
        functools.partial(sums_kernel, len(grads)),
        out_shape=jax.ShapeDtypeStruct((rows, keys, ch), F32),
        in_specs=[VMEM] * (len(grads) + 1),
        out_specs=VMEM,
        scratch_shapes=[pltpu.VMEM((rows, cols, ch), F32)],
        compiler_params=params(),
        cost_estimate=cost(2 * rows * cols * keys * ch, 8 * cols * keys * ch),
        name="first_sums_over_j",
    )(*grads, value)


def totals_kernel(order, n_grads, *refs):
    grads, (slab_value_ref, total_ref, wide) = refs[:n_grads], refs[n_grads:]
    cols, keys, ch = total_ref.shape
    count = widen(grads, wide)
    per = slab_value_ref.shape[0] // len(order)
    rows = [row_of(order, per, p) for p in range(count)]

    def step(s, carry):
        j0 = pl.multiple_of(s * J_STEP, J_STEP)
        totals = [jnp.zeros((keys, ch), F32)] * J_STEP
        totals = add_totals(wide, rows, j0, slab_value_ref, totals)
        for j in range(J_STEP):
            total_ref[j0 + j] = totals[j]
        return carry

    lax.fori_loop(0, cols // J_STEP, step, 0, unroll=2)


def first_totals(order, grads, slab_value):
    _, keys, ch = slab_value.shape
    cols = grads[0].shape[1]
    rows = sum(g.shape[0] for g in grads)
    return pl.pallas_call(
        functools.partial(totals_kernel, order, len(grads)),
        out_shape=jax.ShapeDtypeStruct((cols, keys, ch), F32),
        in_specs=[VMEM] * (len(grads) + 1),
        out_specs=VMEM,
        scratch_shapes=[pltpu.VMEM((rows, cols, ch), F32)],
        compiler_params=params(),
        cost_estimate=cost(2 * rows * cols * keys * ch, 8 * cols * keys * ch),
        name="first_totals_over_i",
    )(*grads, slab_value)


def main_kernel(
    order,
    blocks,
    grad_ref,
    total_ref,
    first_sums_ref,
    pair_ref,
    value_ref,
    lin_ref,
    gate_ref,
    slab_ref,
    slab_value_ref,
    slab_lin_ref,
    slab_gate_ref,
    d_lin_ref,
    d_gate_ref,
    sum_keep_ref,
    sum_send_ref,
    w_keep_ref,
    w_send_ref,
    wide,
    sums_ref,
    slab_sum,
):
    cols, keys, cz = pair_ref.shape
    ch = value_ref.shape[2]
    slab_rows = slab_ref.shape[0]
    done = first_sums_ref.shape[0]
    per = slab_rows // len(order)
    col = lax.axis_index("col")
    count = widen([grad_ref], wide)
    sums_ref[...] = jnp.zeros_like(sums_ref)
    rows = [row_of(order, per, done + p) for p in range(count)]

    def weights(rows, d_lin, d_gate):
        both = jnp.concatenate([d_lin, d_gate], axis=1)
        return lax.dot_general(
            rows, both, (((0,), (0,)), ((), ())), preferred_element_type=F32
        )

    pair_w = jnp.zeros((cz, 2 * ch), F32)
    for first in range(0, cols, W_STEP):
        for j0 in range(first, first + W_STEP, J_STEP):
            values = [value_ref[j0 + j].astype(F32) for j in range(J_STEP)]
            add_sums(wide, count, j0, keys, values, sums_ref)
            totals = [total_ref[j0 + j] for j in range(J_STEP)]
            totals = add_totals(wide, rows, j0, slab_value_ref, totals)
            for j in range(J_STEP):
                d_lin_ref[j0 + j] = (totals[j] * lin_ref[j0 + j]).astype(BF16)
                d_gate_ref[j0 + j] = (totals[j] * gate_ref[j0 + j]).astype(BF16)
        some = slice(first, first + W_STEP)
        pair_w = pair_w + weights(
            pair_ref[some].reshape(W_STEP * keys, cz),
            d_lin_ref[some].reshape(W_STEP * keys, ch),
            d_gate_ref[some].reshape(W_STEP * keys, ch),
        )
    for p in range(done):
        slab_sum[row_of(order, per, p)] = first_sums_ref[p]
    for p in range(count):
        slab_sum[rows[p]] = sums_ref[p]

    sums = slab_sum[...]
    s_lin = (sums * slab_lin_ref[...]).astype(BF16).reshape(slab_rows * keys, ch)
    s_gate = (sums * slab_gate_ref[...]).astype(BF16).reshape(slab_rows * keys, ch)
    slab_w = weights(slab_ref[...].reshape(slab_rows * keys, cz), s_lin, s_gate)
    first = parity() == 0
    keep = jnp.where(first, slab_w, pair_w)
    send = jnp.where(first, pair_w, slab_w)
    for h in range(2):
        w_keep_ref[h] = keep[:, h * ch : (h + 1) * ch]
        w_send_ref[h] = send[:, h * ch : (h + 1) * ch]
    own = sum_keep_ref.shape[1]
    for n, b in enumerate(blocks):
        sum_keep_ref[n] = slab_sum[pl.ds((col ^ b) * own, own)]
        sum_send_ref[n] = slab_sum[pl.ds((col ^ b ^ 1) * own, own)]


def main_part(order, blocks, grads, first, pair, forward, slab):
    cols, keys, cz = pair.shape
    ch = forward[0].shape[2]
    slab_rows = slab[0].shape[0]
    own = slab_rows // (2 * len(blocks))
    d_type = jax.ShapeDtypeStruct((cols, keys, ch), BF16)
    s_type = jax.ShapeDtypeStruct((len(blocks), own, keys, ch), F32)
    w_type = jax.ShapeDtypeStruct((2, cz, ch), F32)
    return pl.pallas_call(
        functools.partial(main_kernel, order, blocks),
        out_shape=(d_type, d_type, s_type, s_type, w_type, w_type),
        in_specs=[VMEM] * 11,
        out_specs=(VMEM,) * 6,
        scratch_shapes=[
            pltpu.VMEM((grads.shape[0], cols, ch), F32),
            pltpu.VMEM((grads.shape[0], keys, ch), F32),
            pltpu.VMEM((slab_rows, keys, ch), F32),
        ],
        compiler_params=params(),
        cost_estimate=cost(8 * cols * keys * cz * ch, 16 * cols * keys * ch),
        name="last_rows",
    )(grads, *first, pair, *forward, *slab)


def pair_out_kernel(d_lin_ref, d_gate_ref, w_lin_ref, w_gate_ref, out_ref):
    rows, ch = d_lin_ref.shape
    weights = jnp.concatenate([w_lin_ref[...], w_gate_ref[...]], axis=1)
    step = rows

    def body(s, carry):
        at = pl.ds(pl.multiple_of(s * step, step), step)
        both = jnp.concatenate([d_lin_ref[at, :], d_gate_ref[at, :]], axis=1)
        out = lax.dot_general(
            both, weights, (((1,), (1,)), ((), ())), preferred_element_type=F32
        )
        out_ref[at, :] = out.astype(BF16)
        return carry

    lax.fori_loop(0, rows // step, body, 0)


def pair_out(d_lin, d_gate, w_lin, w_gate):
    cols, keys, ch = d_lin.shape
    cz = w_lin.shape[0]
    out = pl.pallas_call(
        pair_out_kernel,
        out_shape=jax.ShapeDtypeStruct((cols * keys, cz), BF16),
        in_specs=[VMEM] * 4,
        out_specs=VMEM,
        compiler_params=params(),
        cost_estimate=cost(4 * cols * keys * cz * ch, 6 * cols * keys * ch),
        name="pair_input_grad",
    )(d_lin.reshape(cols * keys, ch), d_gate.reshape(cols * keys, ch), w_lin, w_gate)
    return out.reshape(cols, keys, cz)


def hand_on_kernel(given_ref, out_ref):
    out_ref[...] = given_ref[...]


def hand_on(given):
    return pl.pallas_call(
        hand_on_kernel,
        out_shape=jax.ShapeDtypeStruct(given.shape, given.dtype),
        in_specs=[VMEM],
        out_specs=VMEM,
        compiler_params=params(),
        cost_estimate=cost(STAGE_COST * given.size, 8 * given.size),
        name="hand_on",
    )(given)


def fold_kernel(kept_ref, got_ref, sum_ref, moved_ref):
    half = sum_ref.shape[0]
    sum_ref[...] = kept_ref[:half] + got_ref[:half].astype(F32)
    moved_ref[...] = (kept_ref[half:] + got_ref[half:].astype(F32)).astype(BF16)


def fold(kept, got):
    half = (kept.shape[0] // 2,) + kept.shape[1:]
    return pl.pallas_call(
        fold_kernel,
        out_shape=(jax.ShapeDtypeStruct(half, F32), jax.ShapeDtypeStruct(half, BF16)),
        in_specs=[VMEM, VMEM],
        out_specs=(VMEM, VMEM),
        compiler_params=params(),
        cost_estimate=cost(STAGE_COST * kept.size, 8 * kept.size),
        name="fold",
    )(kept, got)


def add_pair(own, got):
    return (own.astype(F32) + got.astype(F32)).astype(BF16)


def four_kernel(a_ref, b_ref, c_ref, d_ref, out_ref):
    one = d_ref[...].astype(F32) + c_ref[...].astype(F32)
    two = b_ref[...].astype(F32) + a_ref[...].astype(F32)
    out_ref[...] = (one + two).astype(BF16)


def add_sums_of_four(*parts):
    return pl.pallas_call(
        four_kernel,
        out_shape=jax.ShapeDtypeStruct(parts[0].shape, BF16),
        in_specs=[VMEM] * 4,
        out_specs=VMEM,
        compiler_params=params(),
        cost_estimate=cost(4 * parts[0].size, 10 * parts[0].size),
        name="add_four",
    )(*parts)


def join_kernel(pair_bit, diagonal_ref, late_ref, pair_ref, own_ref, out_ref):
    upper = jnp.minimum(lax.axis_index("col") & pair_bit, 1)
    own = own_ref[...].astype(F32) + late_ref[...].astype(F32)
    other = pair_ref[...].astype(F32) + diagonal_ref[...].astype(F32)
    out_ref[upper] = own.astype(BF16)
    out_ref[1 - upper] = other.astype(BF16)


def join_sums(pair_bit, *parts):
    cz, ch = parts[0].shape
    return pl.pallas_call(
        functools.partial(join_kernel, pair_bit),
        out_shape=jax.ShapeDtypeStruct((2, cz, ch), BF16),
        in_specs=[VMEM] * 4,
        out_specs=VMEM,
        compiler_params=params(),
        cost_estimate=cost(4 * cz * ch, 12 * cz * ch),
        name="join_sums",
    )(*parts)


def slab_out_kernel(sum_ref, got_ref, lin_ref, gate_ref, w_lin_ref, w_gate_ref, out_ref):
    own, keys, ch = sum_ref.shape
    col = lax.axis_index("col")
    at = pl.ds(col * own, own)
    total = sum_ref[...] + got_ref[...].astype(F32)
    d_lin = (total * lin_ref[at]).astype(BF16).reshape(own * keys, ch)
    d_gate = (total * gate_ref[at]).astype(BF16).reshape(own * keys, ch)
    both = jnp.concatenate([d_lin, d_gate], axis=1)
    weights = jnp.concatenate([w_lin_ref[...], w_gate_ref[...]], axis=1)
    out = lax.dot_general(both, weights, (((1,), (1,)), ((), ())), preferred_element_type=F32)
    out_ref[...] = out.astype(BF16).reshape(own, keys, w_lin_ref.shape[0])


def slab_out(total, got, lin, gate, w_lin, w_gate):
    own, keys, ch = total.shape
    cz = w_lin.shape[0]
    return pl.pallas_call(
        slab_out_kernel,
        out_shape=jax.ShapeDtypeStruct((own, keys, cz), BF16),
        in_specs=[VMEM] * 6,
        out_specs=VMEM,
        compiler_params=params(),
        cost_estimate=cost(4 * own * keys * cz * ch, 16 * own * keys * ch),
        name="slab_input_grad",
    )(total, got, lin, gate, w_lin, w_gate)


def on_device(
    pair_slab, pair_full, grad_out, w_a_lin, w_a_gate, w_b_lin, w_b_gate, mask_slab, mask_residue
):
    n_row, n_col = lax.axis_size("row"), lax.axis_size("col")
    row_bits, col_bits = bits_of(n_row), bits_of(n_col)
    residues = mask_residue.shape[0]

    steps = row_bits[1:-1] + [row_bits[-1]] + row_bits[:1]
    ch = w_a_lin.shape[1]
    held, own_slab, *staged = stage(lead(), grad_out, pair_slab, w_a_lin, w_a_gate, w_b_lin, w_b_gate)
    order = [0]
    blocks = {0: own_slab}
    for bit in reversed(col_bits[1:]):
        for b in list(blocks):
            blocks[b ^ bit] = swap(blocks[b], "col", bit)
    got = swap(grad_out, "row", steps[0])
    for bit, later in zip(steps, steps[1:-1]):
        held = jnp.concatenate([held, got], axis=0)
        order = order + [r ^ bit for r in order]
        got = swap(held, "row", later)
    masks = lax.optimization_barrier(((mask_slab, mask_residue), held, blocks))[0]
    slab_flags, flags = (
        jnp.broadcast_to(m.astype(BF16)[:, None], m.shape + (ch,)) for m in masks
    )
    value, lin, gate = pair_forward(pair_full, *staged[2:], flags)
    got_last = swap(held, "row", steps[-1])
    got, value = lax.optimization_barrier((got, value))
    got_both = swap(got, "row", steps[-1])
    for bit in steps[-2:]:
        order = order + [r ^ bit for r in order]
    slabs = jnp.concatenate([blocks[b] for b in sorted(blocks)], axis=0)
    slabs = [slabs, swap(slabs, "col", 1)]
    slab = slab_forward(slabs, n_col, *staged[:2], slab_flags, flags)
    pieces = [held, got, got_last]
    first = (first_totals(order, pieces, slab[1]), first_sums(pieces, value))
    kept = [0]
    for bit in reversed(col_bits[1:]):
        kept = kept + [b ^ bit ^ 1 for b in kept]
    d_lin, d_gate, sum_keep, sum_send, w_keep, w_send = main_part(
        order, kept, got_both, first, pair_full, (value, lin, gate), slab
    )
    pair_bit, col = col_bits[1], lax.axis_index("col")
    got_w = swap(w_send, "col", 1)
    side = w_keep + got_w
    upper = (col & pair_bit) != 0
    moved = jnp.where(upper, side[0], side[1]).astype(BF16)
    narrow = jnp.where(upper, side[1], side[0]).astype(BF16)
    moved, narrow, sum_send, d_lin, d_gate = lax.optimization_barrier(
        (moved, narrow, sum_send, d_lin, d_gate)
    )
    grad_pair = pair_out(d_lin, d_gate, w_b_lin, w_b_gate)
    sums, got = sum_keep, swap(sum_send, "col", 1)
    bits = [bit * n_col for bit in row_bits]
    near, late = bits[0], bits[1]
    diagonal = swap_chips(moved, pair_bit | near, 0)
    pair_part, near_part = swap_chips(moved, pair_bit), swap_chips(narrow, near)
    narrow = add_sums_of_four(diagonal, near_part, pair_part, narrow)
    between = col_bits[2:] + [bit for bit in bits if bit not in (near, late)]
    for bit in between:
        if bit == between[-1]:
            narrow, got, grad_pair = lax.optimization_barrier((narrow, got, grad_pair))
            for far in col_bits[1:]:
                sums, moved = fold(sums, got)
                got = swap_chips(moved, far)
        narrow = add_pair(narrow, swap_chips(narrow, bit))
    diagonal = swap_chips(narrow, pair_bit | late, 0)
    late_part, pair_part = swap_chips(narrow, late), swap_chips(narrow, pair_bit)
    mine = join_sums(pair_bit, diagonal, late_part, pair_part, narrow)
    both = [m.astype(F32) / residues for m in (mine, swap(mine, "col", 1))]
    first = parity() == 0
    grad_weights = jnp.where(
        first, jnp.concatenate(both, axis=0), jnp.concatenate(both[::-1], axis=0)
    )
    grad_slab = slab_out(sums[0], got[0], slab[2], slab[3], w_a_lin, w_a_gate)
    return (grad_slab, grad_pair, grad_weights)


def solution(mesh):
    return jax.shard_map(
        on_device,
        mesh=mesh,
        in_specs=(
            P("col", "row", None),
            P("col", "row", None),
            P("row", "col", None),
            P(),
            P(),
            P(),
            P(),
            P(),
            P(),
        ),
        out_specs=(P("col", "row", None), P("col", "row", None), P()),
        check_vma=False,
    )
```

```python
import functools

import jax
import jax.numpy as jnp
from jax import lax
from jax.experimental import pallas as pl
from jax.experimental.pallas import tpu as pltpu
from jax.sharding import PartitionSpec as P

F32 = jnp.float32
BF16 = jnp.bfloat16
VMEM = pl.BlockSpec(memory_space=pltpu.VMEM)
WHOLE = pl.BlockSpec()
SMEM = pl.BlockSpec(memory_space=pltpu.SMEM)
J_STEP = 4
FORWARD_STEP = 64
W_STEP = 16
STAGE_COST = 400000


def bits_of(size):
    return [1 << b for b in range(size.bit_length() - 1)]


def swap(value, axis, bit):
    size = lax.axis_size(axis)
    return lax.ppermute(value, axis, [(d, d ^ bit) for d in range(size)])


def swap_chips(value, bit, flip=1):
    n_row, n_col = lax.axis_size("row"), lax.axis_size("col")
    pairs = [(d, d ^ bit ^ flip) for d in range(n_row * n_col)]
    return lax.ppermute(value, ("row", "col"), pairs)


def parity():
    number = lax.axis_index("row") ^ lax.axis_index("col")
    for shift in (16, 8, 4, 2, 1):
        number = number ^ (number >> shift)
    return number & 1


def params(mib=32):
    return pltpu.CompilerParams(vmem_limit_bytes=mib * 1024 * 1024)


def cost(flops, bytes_accessed, transcendentals=0):
    return pl.CostEstimate(
        flops=flops, bytes_accessed=bytes_accessed, transcendentals=transcendentals
    )


def project(rows, w_lin, w_gate):
    both = jnp.dot(
        rows, jnp.concatenate([w_lin, w_gate], axis=1), preferred_element_type=F32
    )
    ch = w_lin.shape[1]
    linear = both[:, :ch]
    sigmoid = 1.0 / (1.0 + jnp.exp(-both[:, ch:]))
    return linear, sigmoid


def lead_kernel(out_ref):
    out_ref[...] = jnp.zeros_like(out_ref)


def lead():
    return pl.pallas_call(
        lead_kernel,
        out_shape=jax.ShapeDtypeStruct((8, 128), F32),
        out_specs=VMEM,
        compiler_params=params(),
        cost_estimate=cost(STAGE_COST * 8192, 4096),
        name="lead",
    )()


def stage_kernel(n, _, *refs):
    for source_ref, copy_ref in zip(refs[:n], refs[n:]):
        copy_ref[...] = source_ref[...]


def stage(after, *sources):
    n = len(sources)
    return pl.pallas_call(
        functools.partial(stage_kernel, n),
        out_shape=tuple(jax.ShapeDtypeStruct(s.shape, s.dtype) for s in sources),
        in_specs=[VMEM] * (n + 1),
        out_specs=(VMEM,) * n,
        compiler_params=params(),
        cost_estimate=cost(STAGE_COST * sources[0].size, 4 * sources[0].size),
        name="stage",
    )(after, *sources)


def pair_forward_kernel(pair_ref, w_lin_ref, w_gate_ref, flags_ref, value_ref, lin_ref, gate_ref):
    cols, keys, cz = pair_ref.shape
    row, col = lax.axis_index("row"), lax.axis_index("col")
    km = flags_ref[pl.ds(pl.multiple_of(row * keys, 16), keys)].astype(F32)
    step = min(cols, FORWARD_STEP)

    def body(s, carry):
        j0 = pl.multiple_of(s * step, step)
        rows = pair_ref[pl.ds(j0, step)].reshape(step * keys, cz)
        linear, sigmoid = project(rows, w_lin_ref[...], w_gate_ref[...])
        linear = linear.reshape(step, keys, -1)
        sigmoid = sigmoid.reshape(step, keys, -1)
        flags = flags_ref[pl.ds(pl.multiple_of(col * cols + j0, step), step)].astype(F32)
        for j in range(step):
            m = km * flags[j : j + 1]
            masked = m * sigmoid[j]
            lin = linear[j]
            value_ref[j0 + j] = (masked * lin).astype(BF16)
            lin_ref[j0 + j] = masked
            gate_ref[j0 + j] = masked * lin * (1.0 - sigmoid[j])
        return carry

    lax.fori_loop(0, cols // step, body, 0)


def pair_forward(pair, w_lin, w_gate, flags):
    cols, keys, cz = pair.shape
    ch = w_lin.shape[1]
    out = jax.ShapeDtypeStruct((cols, keys, ch), F32)
    return pl.pallas_call(
        pair_forward_kernel,
        out_shape=(jax.ShapeDtypeStruct((cols, keys, ch), BF16), out, out),
        in_specs=[VMEM] * 4,
        out_specs=(VMEM, VMEM, VMEM),
        compiler_params=params(),
        cost_estimate=cost(4 * cols * keys * cz * ch, 14 * cols * keys * ch, cols * keys * ch),
        name="pair_forward",
    )(pair, w_lin, w_gate, flags)


def slab_forward_kernel(
    n_blocks,
    even_ref,
    odd_ref,
    w_lin_ref,
    w_gate_ref,
    slab_flags_ref,
    flags_ref,
    slab_ref,
    value_ref,
    lin_ref,
    gate_ref,
):
    _, keys, cz = even_ref.shape
    rows = 2 * even_ref.shape[0] // n_blocks
    row, col = lax.axis_index("row"), lax.axis_index("col")
    km = flags_ref[pl.ds(pl.multiple_of(row * keys, 16), keys)].astype(F32)
    flags = slab_flags_ref[...].astype(F32)
    for i in range(n_blocks * rows):
        value_ref[i] = km * flags[i : i + 1]
    for b in range(n_blocks):
        first = (col ^ b) * rows
        block = (odd_ref if b % 2 else even_ref)[(b // 2) * rows : (b // 2 + 1) * rows]
        linear, sigmoid = project(
            block.reshape(rows * keys, cz),
            w_lin_ref[...],
            w_gate_ref[...],
        )
        linear = linear.reshape(rows, keys, -1)
        sigmoid = sigmoid.reshape(rows, keys, -1)
        for r in range(rows):
            i = first + r
            masked = value_ref[i] * sigmoid[r]
            slab_ref[i] = block[r]
            value_ref[i] = (masked * linear[r]).astype(BF16).astype(F32)
            lin_ref[i] = masked
            gate_ref[i] = masked * linear[r] * (1.0 - sigmoid[r])


def slab_forward(blocks, n, w_lin, w_gate, slab_flags, flags):
    half, keys, cz = blocks[0].shape
    rows = 2 * half // n
    ch = w_lin.shape[1]
    out = jax.ShapeDtypeStruct((n * rows, keys, ch), F32)
    raw = jax.ShapeDtypeStruct((n * rows, keys, cz), BF16)
    return pl.pallas_call(
        functools.partial(slab_forward_kernel, n),
        out_shape=(raw, out, out, out),
        in_specs=[VMEM] * 6,
        out_specs=(VMEM,) * 4,
        compiler_params=params(),
        cost_estimate=cost(4 * n * rows * keys * cz * ch, 16 * n * rows * keys * ch),
        name="slab_forward",
    )(*blocks, w_lin, w_gate, slab_flags, flags)


def row_of(order, per, p):
    return (lax.axis_index("row") ^ order[p // per]) * per + p % per


def widen(grads, wide):
    at = 0
    for grad_ref in grads:
        wide[at : at + grad_ref.shape[0]] = grad_ref[...].astype(F32)
        at += grad_ref.shape[0]
    return at


def add_sums(wide, count, j0, keys, values, sums_ref):
    ch = wide.shape[2]
    for p in range(count):
        total = sums_ref[p]
        for j, value in enumerate(values):
            total = total + jnp.broadcast_to(wide[p, pl.ds(j0 + j, 1), :], (keys, ch)) * value
        sums_ref[p] = total


def add_totals(wide, rows, j0, slab_value_ref, totals):
    _, keys, ch = slab_value_ref.shape
    totals = list(totals)
    for p, i in enumerate(rows):
        mine = slab_value_ref[i]
        for j in range(len(totals)):
            g = jnp.broadcast_to(wide[p, pl.ds(j0 + j, 1), :], (keys, ch))
            totals[j] = totals[j] + g * mine
    return totals


def sums_kernel(n_grads, *refs):
    grads, (value_ref, sums_ref, wide) = refs[:n_grads], refs[n_grads:]
    cols, keys, ch = value_ref.shape
    count = widen(grads, wide)
    sums_ref[...] = jnp.zeros_like(sums_ref)

    def step(s, carry):
        j0 = pl.multiple_of(s * J_STEP, J_STEP)
        values = [value_ref[j0 + j].astype(F32) for j in range(J_STEP)]
        add_sums(wide, count, j0, keys, values, sums_ref)
        return carry

    lax.fori_loop(0, cols // J_STEP, step, 0, unroll=4)


def first_sums(grads, value):
    cols, keys, ch = value.shape
    rows = sum(g.shape[0] for g in grads)
    return pl.pallas_call(
        functools.partial(sums_kernel, len(grads)),
        out_shape=jax.ShapeDtypeStruct((rows, keys, ch), F32),
        in_specs=[VMEM] * (len(grads) + 1),
        out_specs=VMEM,
        scratch_shapes=[pltpu.VMEM((rows, cols, ch), F32)],
        compiler_params=params(),
        cost_estimate=cost(2 * rows * cols * keys * ch, 8 * cols * keys * ch),
        name="first_sums_over_j",
    )(*grads, value)


def totals_kernel(order, n_grads, *refs):
    grads, (slab_value_ref, total_ref, wide) = refs[:n_grads], refs[n_grads:]
    cols, keys, ch = total_ref.shape
    count = widen(grads, wide)
    per = slab_value_ref.shape[0] // len(order)
    rows = [row_of(order, per, p) for p in range(count)]

    def step(s, carry):
        j0 = pl.multiple_of(s * J_STEP, J_STEP)
        totals = [jnp.zeros((keys, ch), F32)] * J_STEP
        totals = add_totals(wide, rows, j0, slab_value_ref, totals)
        for j in range(J_STEP):
            total_ref[j0 + j] = totals[j]
        return carry

    lax.fori_loop(0, cols // J_STEP, step, 0, unroll=4)


def first_totals(order, grads, slab_value):
    _, keys, ch = slab_value.shape
    cols = grads[0].shape[1]
    rows = sum(g.shape[0] for g in grads)
    return pl.pallas_call(
        functools.partial(totals_kernel, order, len(grads)),
        out_shape=jax.ShapeDtypeStruct((cols, keys, ch), F32),
        in_specs=[VMEM] * (len(grads) + 1),
        out_specs=VMEM,
        scratch_shapes=[pltpu.VMEM((rows, cols, ch), F32)],
        compiler_params=params(),
        cost_estimate=cost(2 * rows * cols * keys * ch, 8 * cols * keys * ch),
        name="first_totals_over_i",
    )(*grads, slab_value)


def main_kernel(
    order,
    blocks,
    grad_ref,
    total_ref,
    first_sums_ref,
    pair_ref,
    value_ref,
    lin_ref,
    gate_ref,
    slab_ref,
    slab_value_ref,
    slab_lin_ref,
    slab_gate_ref,
    d_lin_ref,
    d_gate_ref,
    sum_keep_ref,
    sum_send_ref,
    w_keep_ref,
    w_send_ref,
    wide,
    sums_ref,
    slab_sum,
):
    cols, keys, cz = pair_ref.shape
    ch = value_ref.shape[2]
    slab_rows = slab_ref.shape[0]
    done = first_sums_ref.shape[0]
    per = slab_rows // len(order)
    col = lax.axis_index("col")
    count = widen([grad_ref], wide)
    sums_ref[...] = jnp.zeros_like(sums_ref)
    rows = [row_of(order, per, done + p) for p in range(count)]

    def weights(rows, d_lin, d_gate):
        both = jnp.concatenate([d_lin, d_gate], axis=1)
        return lax.dot_general(
            rows, both, (((0,), (0,)), ((), ())), preferred_element_type=F32
        )

    pair_w = jnp.zeros((cz, 2 * ch), F32)
    for first in range(0, cols, W_STEP):
        for j0 in range(first, first + W_STEP, J_STEP):
            values = [value_ref[j0 + j].astype(F32) for j in range(J_STEP)]
            add_sums(wide, count, j0, keys, values, sums_ref)
            totals = [total_ref[j0 + j] for j in range(J_STEP)]
            totals = add_totals(wide, rows, j0, slab_value_ref, totals)
            for j in range(J_STEP):
                d_lin_ref[j0 + j] = (totals[j] * lin_ref[j0 + j]).astype(BF16)
                d_gate_ref[j0 + j] = (totals[j] * gate_ref[j0 + j]).astype(BF16)
        some = slice(first, first + W_STEP)
        pair_w = pair_w + weights(
            pair_ref[some].reshape(W_STEP * keys, cz),
            d_lin_ref[some].reshape(W_STEP * keys, ch),
            d_gate_ref[some].reshape(W_STEP * keys, ch),
        )
    for p in range(done):
        slab_sum[row_of(order, per, p)] = first_sums_ref[p]
    for p in range(count):
        slab_sum[rows[p]] = sums_ref[p]

    sums = slab_sum[...]
    s_lin = (sums * slab_lin_ref[...]).astype(BF16).reshape(slab_rows * keys, ch)
    s_gate = (sums * slab_gate_ref[...]).astype(BF16).reshape(slab_rows * keys, ch)
    slab_w = weights(slab_ref[...].reshape(slab_rows * keys, cz), s_lin, s_gate)
    first = parity() == 0
    keep = jnp.where(first, slab_w, pair_w)
    send = jnp.where(first, pair_w, slab_w)
    for h in range(2):
        w_keep_ref[h] = keep[:, h * ch : (h + 1) * ch]
        w_send_ref[h] = send[:, h * ch : (h + 1) * ch]
    own = sum_keep_ref.shape[1]
    for n, b in enumerate(blocks):
        sum_keep_ref[n] = slab_sum[pl.ds((col ^ b) * own, own)]
        sum_send_ref[n] = slab_sum[pl.ds((col ^ b ^ 1) * own, own)]


def main_part(order, blocks, grads, first, pair, forward, slab):
    cols, keys, cz = pair.shape
    ch = forward[0].shape[2]
    slab_rows = slab[0].shape[0]
    own = slab_rows // (2 * len(blocks))
    d_type = jax.ShapeDtypeStruct((cols, keys, ch), BF16)
    s_type = jax.ShapeDtypeStruct((len(blocks), own, keys, ch), F32)
    w_type = jax.ShapeDtypeStruct((2, cz, ch), F32)
    return pl.pallas_call(
        functools.partial(main_kernel, order, blocks),
        out_shape=(d_type, d_type, s_type, s_type, w_type, w_type),
        in_specs=[VMEM] * 11,
        out_specs=(VMEM,) * 6,
        scratch_shapes=[
            pltpu.VMEM((grads.shape[0], cols, ch), F32),
            pltpu.VMEM((grads.shape[0], keys, ch), F32),
            pltpu.VMEM((slab_rows, keys, ch), F32),
        ],
        compiler_params=params(),
        cost_estimate=cost(8 * cols * keys * cz * ch, 16 * cols * keys * ch),
        name="last_rows",
    )(grads, *first, pair, *forward, *slab)


def pair_out_kernel(d_lin_ref, d_gate_ref, w_lin_ref, w_gate_ref, out_ref):
    rows, ch = d_lin_ref.shape
    weights = jnp.concatenate([w_lin_ref[...], w_gate_ref[...]], axis=1)
    step = rows

    def body(s, carry):
        at = pl.ds(pl.multiple_of(s * step, step), step)
        both = jnp.concatenate([d_lin_ref[at, :], d_gate_ref[at, :]], axis=1)
        out = lax.dot_general(
            both, weights, (((1,), (1,)), ((), ())), preferred_element_type=F32
        )
        out_ref[at, :] = out.astype(BF16)
        return carry

    lax.fori_loop(0, rows // step, body, 0)


def pair_out(d_lin, d_gate, w_lin, w_gate):
    cols, keys, ch = d_lin.shape
    cz = w_lin.shape[0]
    out = pl.pallas_call(
        pair_out_kernel,
        out_shape=jax.ShapeDtypeStruct((cols * keys, cz), BF16),
        in_specs=[VMEM] * 4,
        out_specs=VMEM,
        compiler_params=params(),
        cost_estimate=cost(4 * cols * keys * cz * ch, 6 * cols * keys * ch),
        name="pair_input_grad",
    )(d_lin.reshape(cols * keys, ch), d_gate.reshape(cols * keys, ch), w_lin, w_gate)
    return out.reshape(cols, keys, cz)


def hand_on_kernel(given_ref, out_ref):
    out_ref[...] = given_ref[...]


def hand_on(given):
    return pl.pallas_call(
        hand_on_kernel,
        out_shape=jax.ShapeDtypeStruct(given.shape, given.dtype),
        in_specs=[VMEM],
        out_specs=VMEM,
        compiler_params=params(),
        cost_estimate=cost(STAGE_COST * given.size, 8 * given.size),
        name="hand_on",
    )(given)


def fold_kernel(kept_ref, got_ref, sum_ref, moved_ref):
    half = sum_ref.shape[0]
    sum_ref[...] = kept_ref[:half] + got_ref[:half].astype(F32)
    moved_ref[...] = (kept_ref[half:] + got_ref[half:].astype(F32)).astype(BF16)


def fold(kept, got):
    half = (kept.shape[0] // 2,) + kept.shape[1:]
    return pl.pallas_call(
        fold_kernel,
        out_shape=(jax.ShapeDtypeStruct(half, F32), jax.ShapeDtypeStruct(half, BF16)),
        in_specs=[VMEM, VMEM],
        out_specs=(VMEM, VMEM),
        compiler_params=params(),
        cost_estimate=cost(STAGE_COST * kept.size, 8 * kept.size),
        name="fold",
    )(kept, got)


def add_pair(own, got):
    return (own.astype(F32) + got.astype(F32)).astype(BF16)


def four_kernel(a_ref, b_ref, c_ref, d_ref, out_ref):
    one = d_ref[...].astype(F32) + c_ref[...].astype(F32)
    two = b_ref[...].astype(F32) + a_ref[...].astype(F32)
    out_ref[...] = (one + two).astype(BF16)


def add_sums_of_four(*parts):
    return pl.pallas_call(
        four_kernel,
        out_shape=jax.ShapeDtypeStruct(parts[0].shape, BF16),
        in_specs=[VMEM] * 4,
        out_specs=VMEM,
        compiler_params=params(),
        cost_estimate=cost(4 * parts[0].size, 10 * parts[0].size),
        name="add_four",
    )(*parts)


def join_kernel(pair_bit, diagonal_ref, late_ref, pair_ref, own_ref, out_ref):
    upper = jnp.minimum(lax.axis_index("col") & pair_bit, 1)
    own = own_ref[...].astype(F32) + late_ref[...].astype(F32)
    other = pair_ref[...].astype(F32) + diagonal_ref[...].astype(F32)
    out_ref[upper] = own.astype(BF16)
    out_ref[1 - upper] = other.astype(BF16)


def join_sums(pair_bit, *parts):
    cz, ch = parts[0].shape
    return pl.pallas_call(
        functools.partial(join_kernel, pair_bit),
        out_shape=jax.ShapeDtypeStruct((2, cz, ch), BF16),
        in_specs=[VMEM] * 4,
        out_specs=VMEM,
        compiler_params=params(),
        cost_estimate=cost(4 * cz * ch, 12 * cz * ch),
        name="join_sums",
    )(*parts)


def slab_out_kernel(sum_ref, got_ref, lin_ref, gate_ref, w_lin_ref, w_gate_ref, out_ref):
    own, keys, ch = sum_ref.shape
    col = lax.axis_index("col")
    at = pl.ds(col * own, own)
    total = sum_ref[...] + got_ref[...].astype(F32)
    d_lin = (total * lin_ref[at]).astype(BF16).reshape(own * keys, ch)
    d_gate = (total * gate_ref[at]).astype(BF16).reshape(own * keys, ch)
    both = jnp.concatenate([d_lin, d_gate], axis=1)
    weights = jnp.concatenate([w_lin_ref[...], w_gate_ref[...]], axis=1)
    out = lax.dot_general(both, weights, (((1,), (1,)), ((), ())), preferred_element_type=F32)
    out_ref[...] = out.astype(BF16).reshape(own, keys, w_lin_ref.shape[0])


def slab_out(total, got, lin, gate, w_lin, w_gate):
    own, keys, ch = total.shape
    cz = w_lin.shape[0]
    return pl.pallas_call(
        slab_out_kernel,
        out_shape=jax.ShapeDtypeStruct((own, keys, cz), BF16),
        in_specs=[VMEM] * 6,
        out_specs=VMEM,
        compiler_params=params(),
        cost_estimate=cost(4 * own * keys * cz * ch, 16 * own * keys * ch),
        name="slab_input_grad",
    )(total, got, lin, gate, w_lin, w_gate)


def on_device(
    pair_slab, pair_full, grad_out, w_a_lin, w_a_gate, w_b_lin, w_b_gate, mask_slab, mask_residue
):
    n_row, n_col = lax.axis_size("row"), lax.axis_size("col")
    row_bits, col_bits = bits_of(n_row), bits_of(n_col)
    residues = mask_residue.shape[0]

    steps = row_bits[1:-1] + [row_bits[-1]] + row_bits[:1]
    ch = w_a_lin.shape[1]
    held, own_slab, *staged = stage(lead(), grad_out, pair_slab, w_a_lin, w_a_gate, w_b_lin, w_b_gate)
    order = [0]
    blocks = {0: own_slab}
    for bit in reversed(col_bits[1:]):
        for b in list(blocks):
            blocks[b ^ bit] = swap(blocks[b], "col", bit)
    got = swap(grad_out, "row", steps[0])
    for bit, later in zip(steps, steps[1:-1]):
        held = jnp.concatenate([held, got], axis=0)
        order = order + [r ^ bit for r in order]
        got = swap(held, "row", later)
    masks = lax.optimization_barrier(((mask_slab, mask_residue), held, blocks))[0]
    slab_flags, flags = (
        jnp.broadcast_to(m.astype(BF16)[:, None], m.shape + (ch,)) for m in masks
    )
    value, lin, gate = pair_forward(pair_full, *staged[2:], flags)
    got_last = swap(held, "row", steps[-1])
    got, value = lax.optimization_barrier((got, value))
    got_both = swap(got, "row", steps[-1])
    for bit in steps[-2:]:
        order = order + [r ^ bit for r in order]
    slabs = jnp.concatenate([blocks[b] for b in sorted(blocks)], axis=0)
    slabs = [slabs, swap(slabs, "col", 1)]
    slab = slab_forward(slabs, n_col, *staged[:2], slab_flags, flags)
    pieces = [held, got, got_last]
    first = (first_totals(order, pieces, slab[1]), first_sums(pieces, value))
    kept = [0]
    for bit in reversed(col_bits[1:]):
        kept = kept + [b ^ bit ^ 1 for b in kept]
    d_lin, d_gate, sum_keep, sum_send, w_keep, w_send = main_part(
        order, kept, got_both, first, pair_full, (value, lin, gate), slab
    )
    pair_bit, col = col_bits[1], lax.axis_index("col")
    got_w = swap(w_send, "col", 1)
    side = w_keep + got_w
    upper = (col & pair_bit) != 0
    moved = jnp.where(upper, side[0], side[1]).astype(BF16)
    narrow = jnp.where(upper, side[1], side[0]).astype(BF16)
    moved, narrow, sum_send, d_lin, d_gate = lax.optimization_barrier(
        (moved, narrow, sum_send, d_lin, d_gate)
    )
    grad_pair = pair_out(d_lin, d_gate, w_b_lin, w_b_gate)
    sums, got = sum_keep, swap(sum_send, "col", 1)
    bits = [bit * n_col for bit in row_bits]
    near, late = bits[0], bits[1]
    diagonal = swap_chips(moved, pair_bit | near, 0)
    pair_part, near_part = swap_chips(moved, pair_bit), swap_chips(narrow, near)
    narrow = add_sums_of_four(diagonal, near_part, pair_part, narrow)
    between = col_bits[2:] + [bit for bit in bits if bit not in (near, late)]
    for bit in between:
        if bit == between[-1]:
            narrow, got, grad_pair = lax.optimization_barrier((narrow, got, grad_pair))
            for far in col_bits[1:]:
                sums, moved = fold(sums, got)
                got = swap_chips(moved, far)
        narrow = add_pair(narrow, swap_chips(narrow, bit))
    diagonal = swap_chips(narrow, pair_bit | late, 0)
    late_part, pair_part = swap_chips(narrow, late), swap_chips(narrow, pair_bit)
    mine = join_sums(pair_bit, diagonal, late_part, pair_part, narrow)
    both = [m.astype(F32) / residues for m in (mine, swap(mine, "col", 1))]
    first = parity() == 0
    grad_weights = jnp.where(
        first, jnp.concatenate(both, axis=0), jnp.concatenate(both[::-1], axis=0)
    )
    grad_slab = slab_out(sums[0], got[0], slab[2], slab[3], w_a_lin, w_a_gate)
    return (grad_slab, grad_pair, grad_weights)


def solution(mesh):
    return jax.shard_map(
        on_device,
        mesh=mesh,
        in_specs=(
            P("col", "row", None),
            P("col", "row", None),
            P("row", "col", None),
            P(),
            P(),
            P(),
            P(),
            P(),
            P(),
        ),
        out_specs=(P("col", "row", None), P("col", "row", None), P()),
        check_vma=False,
    )
```
